512 devices in a mesh: users: 16 (over x, z_hi, core), cand: 32 (over y, z_lo).
Axes of the slice: x: 4, y: 4, z: 16 (z_hi: 2, z_lo: 8; z = z_hi * 8 + z_lo), core: 2. Of those that a mesh axis runs over, the one named last changes fastest.
Arguments:
- cand_query: bfloat16 [16, 4096, 1024], P('users', 'cand'), may hold values from -6 to 6
- cand_key: bfloat16 [16, 4096, 1024], P('users', 'cand'), may hold values from -6 to 6
- cand_value: bfloat16 [16, 4096, 1024], P('users', 'cand'), may hold values from -6 to 6
- cand_gate: bfloat16 [16, 4096, 1024], P('users', 'cand'), may hold values from -6 to 6
- residual_in: bfloat16 [16, 4096, 1024], P('users', 'cand'), may hold values from -6 to 6
- hist_key: bfloat16 [16, 1024, 1024], P('users', 'cand'), may hold values from -6 to 6
- hist_value: bfloat16 [16, 1024, 1024], P('users', 'cand'), may hold values from -6 to 6
- micro_ids: int32 [16, 4096], P('users'), may hold values from 0 to 63, never falling along the last dimension, each value on 1 to 128 neighbouring positions
- pattern: int32 [128, 128], replicated, may hold values 0 or 1
- out_weight: bfloat16 [1024, 1024], P('cand', 'users'), may hold values from -0.1875 to 0.1875
Outputs:
- layer_out: bfloat16 [16, 4096, 1024], P('users', 'cand')
The draws below stay inside these ranges and needn't reach their ends.
Inputs may be any that keep to these rules, and one draw needn't show every extreme that they name: `micro_ids`: in each row micro-batch numbers never fall; each micro-batch is a run of 1 to 128 consecutive candidates, and some run has exactly 128.
All inputs are finite; a program needn't handle non-finite values.
Results may differ from the reference program's by a relative error of at most 0.0051.
Values may be sent and summed in bfloat16 or wider, within the bound.
A program may use at most 64 MiB of HBM per device.

```python
import math
import jax
import jax.numpy as jnp
import numpy as np
from jax import lax

D = 1024
H = 8
DH = 128
MB_MAX = 128
CANDS = 4096
HIST = 1024
MICRO = 64
N_USERS = 16


def touch_ends(entries, stream_key, smallest, high):
    shape = entries.shape
    spot = [jax.random.randint(jax.random.fold_in(stream_key, axis), (), 0, shape[axis]) for axis in range(len(shape))]
    entries = entries.at[tuple(spot)].set(smallest)
    longest = shape.index(max(shape))
    spot[longest] = (spot[longest] + 1) % shape[longest]
    return entries.at[tuple(spot)].set(high)


def level_of(rng, extent, cuts, smallest, high):
    gain, own = 1.0, jax.random.fold_in(rng, 6)
    for position, blocks in cuts:
        heights = jnp.exp(jax.random.uniform(jax.random.fold_in(own, position), (blocks,), jnp.float32, smallest / len(cuts), high / len(cuts)))
        gain = gain * jnp.repeat(heights, extent[position] // blocks).reshape([-1 if axis == position else 1 for axis in range(len(extent))])
    return gain


def split_up(number_of, total, most, skew):
    portions = [(1 << 20) // math.isqrt(standing ** skew) + 1 for standing in range(2, number_of + 1)]
    spare, counts = total - most - (number_of - 1), [1] * (number_of - 1)
    while spare > 0:
        candidates = [i for i in range(number_of - 1) if counts[i] < most]
        mass, remaining = sum([portions[i] for i in candidates]), spare
        for i in candidates:
            more = min(most - counts[i], max(1, remaining * portions[i] // mass), spare)
            counts[i] = counts[i] + more
            spare = spare - more
    return np.array([most] + counts)


def ragged(rng, count, total, limit, slope):
    if count == 2:
        one = jax.random.randint(rng, (), max(1, total - limit), min(limit, total - 1) + 1)
        return jnp.stack([one, total - one])
    tallies = jnp.asarray(split_up(count, total, limit, slope), jnp.int32)
    pairs = (count - 1) // 2
    donor, sink = tallies[1:1 + 2 * pairs:2], tallies[2:2 + 2 * pairs:2]
    margin = jnp.minimum(donor - 1, limit - sink)
    passed = jax.random.randint(jax.random.fold_in(rng, 1), (pairs,), 0, 1 << 20) % (margin + 1)
    tallies = tallies.at[1:1 + 2 * pairs:2].set(donor - passed).at[2:2 + 2 * pairs:2].set(sink + passed)
    return tallies[jax.random.permutation(jax.random.fold_in(rng, 2), count)]


def scatter_about(key, dims, deviation, most, split=(), kind=jnp.bfloat16):
    level = level_of(key, dims, split, -0.22, 0.18) if split else 1.0
    entries = jax.random.normal(key, dims, jnp.float32) * deviation * level
    return jnp.minimum(jnp.maximum(entries, -most), most).astype(kind)


def setup_inputs(seed: int = 0) -> dict:
    key_list = jax.random.split(jax.random.key(seed), 11)
    return {
        "cand_query": scatter_about(key_list[0], (N_USERS, CANDS, D), 1.0, 6.0, ((0, 16), (1, 32))),
        "cand_key": scatter_about(key_list[1], (N_USERS, CANDS, D), 1.0, 6.0, ((0, 16), (1, 32))),
        "cand_value": scatter_about(key_list[2], (N_USERS, CANDS, D), 1.0, 6.0, ((0, 16), (1, 32))),
        "cand_gate": scatter_about(key_list[3], (N_USERS, CANDS, D), 1.0, 6.0, ((0, 16), (1, 32))),
        "residual_in": scatter_about(key_list[4], (N_USERS, CANDS, D), 1.0, 6.0, ((0, 16), (1, 32))),
        "hist_key": scatter_about(key_list[5], (N_USERS, HIST, D), 1.0, 6.0, ((0, 16), (1, 32))),
        "hist_value": scatter_about(key_list[6], (N_USERS, HIST, D), 1.0, 6.0, ((0, 16), (1, 32))),
        "micro_ids": jax.vmap(lambda own: jnp.searchsorted(jnp.cumsum(ragged(own, MICRO, CANDS, MB_MAX, 2)), jnp.arange(CANDS), side="right"))(jax.random.split(key_list[7], N_USERS)).reshape((N_USERS, CANDS)).astype(jnp.int32),
        "pattern": touch_ends((jax.random.randint(key_list[8], (MB_MAX, MB_MAX), 0, 2) < 1).astype(jnp.int32), jax.random.fold_in(key_list[8], 1), 0, 1),
        "out_weight": scatter_about(key_list[9], (D, D), D ** -0.5, 0.1875, ((0, 32), (1, 16))),
    }


def micro_offsets(ids_row):
    positions = jnp.arange(ids_row.shape[0], dtype=jnp.int32)
    boundary = jnp.concatenate([jnp.ones((1,), jnp.bool_), ids_row[1:] != ids_row[:-1]])
    starts = lax.cummax(jnp.where(boundary, positions, 0).astype(jnp.int32))
    return (positions - starts).astype(jnp.int32)

def pointwise(scores, visible):
    weights = jnp.where(visible, jax.nn.silu(scores), 0.0)
    rounded = lax.optimization_barrier(weights.astype(jnp.bfloat16))
    return rounded.astype(jnp.float32)

def reference(cand_query, cand_key, cand_value, cand_gate, residual_in, hist_key, hist_value, micro_ids, pattern, out_weight):
    reach = MB_MAX - 1
    factor = DH ** (-0.5)
    block = math.gcd(CANDS, 512)
    window = block + 2 * reach

    def one_user(operands):
        query, keys, values, gate, resid, past_keys, past_values, ids_row = operands
        offsets = micro_offsets(ids_row)
        pad_ids = jnp.concatenate([jnp.full((reach,), -1, jnp.int32), ids_row, jnp.full((reach,), -1, jnp.int32)])
        pad_off = jnp.concatenate([jnp.zeros((reach,), jnp.int32), offsets, jnp.zeros((reach,), jnp.int32)])
        pad_keys = jnp.pad(keys, ((reach, reach), (0, 0)))
        pad_values = jnp.pad(values, ((reach, reach), (0, 0)))
        past_k = past_keys.astype(jnp.float32).reshape(HIST, H, DH)
        past_v = past_values.astype(jnp.float32).reshape(HIST, H, DH)

        def one_block(begin):
            queries = lax.dynamic_slice_in_dim(query, begin, block, 0).astype(jnp.float32).reshape(block, H, DH)
            near_k = lax.dynamic_slice_in_dim(pad_keys, begin, window, 0).astype(jnp.float32).reshape(window, H, DH)
            near_v = lax.dynamic_slice_in_dim(pad_values, begin, window, 0).astype(jnp.float32).reshape(window, H, DH)
            ids_rows = lax.dynamic_slice_in_dim(ids_row, begin, block, 0)
            off_rows = lax.dynamic_slice_in_dim(offsets, begin, block, 0)
            ids_keys = lax.dynamic_slice_in_dim(pad_ids, begin, window, 0)
            off_keys = lax.dynamic_slice_in_dim(pad_off, begin, window, 0)
            same = ids_rows[:, None] == ids_keys[None, :]
            diagonal = jnp.arange(block)[:, None] + reach == jnp.arange(window)[None, :]
            allowed = pattern[off_rows][:, off_keys] == 1
            visible = same & (allowed | diagonal)
            self_scores = jnp.einsum('rhd,khd->hrk', queries, near_k) * factor
            self_weights = pointwise(self_scores, visible[None])
            attended = jnp.einsum('hrk,khd->rhd', self_weights, near_v)
            hist_scores = jnp.einsum('rhd,khd->hrk', queries, past_k) * factor
            hist_weights = pointwise(hist_scores, True)
            attended = attended + jnp.einsum('hrk,khd->rhd', hist_weights, past_v)
            attended = attended.reshape(block, D)
            center = lax.optimization_barrier(jnp.mean(attended, axis=1, keepdims=True))
            spread = lax.optimization_barrier(jnp.mean((attended - center) ** 2, axis=1, keepdims=True))
            normed = (attended - center) * lax.rsqrt(spread + 1e-05)
            gate_rows = lax.dynamic_slice_in_dim(gate, begin, block, 0).astype(jnp.float32)
            gated = (normed * gate_rows).astype(jnp.bfloat16)
            projected = jnp.dot(gated, out_weight, preferred_element_type=jnp.float32)
            resid_rows = lax.dynamic_slice_in_dim(resid, begin, block, 0).astype(jnp.float32)
            return (resid_rows + projected).astype(jnp.bfloat16)
        begins = (jnp.arange(CANDS // block) * block).astype(jnp.int32)
        return lax.map(one_block, begins).reshape(CANDS, D)
    return lax.map(one_user, (cand_query, cand_key, cand_value, cand_gate, residual_in, hist_key, hist_value, micro_ids))
```

```python
import jax
import jax.numpy as jnp
from jax import lax
from jax.experimental import pallas as pl
from jax.experimental.pallas import tpu as pltpu
from jax.sharding import PartitionSpec as P

H = 8
DH = 128
NX, NZH, NCORE = 4, 2, 2
NY, NZL = 4, 8
NCAND = NY * NZL
HEADS = H // NY
SHARE = HEADS * DH
MESH = pl.DeviceIdType.MESH
BF16, F32 = jnp.bfloat16, jnp.float32


def dot(a, b):
    return lax.dot_general(a, b, (((1,), (0,)), ((), ())), preferred_element_type=F32)


def dot_t(a, b):
    return lax.dot_general(a, b, (((1,), (1,)), ((), ())), preferred_element_type=F32)


def silu_of_half(h):
    return (h + h * jnp.tanh(h)).astype(BF16)


def kernel(
    q_hbm, k_hbm, v_hbm, gate_hbm, res_hbm, hk_hbm, hv_hbm, ids_hbm, pat_hbm, w_hbm,
    out_ref,
    rows5, ids_ref, pat_ref, w_ref,
    kvh, qh, oh, part_out, part_in, halo, wtmp, wb, maskh, att,
    in_sem, kv_recv, own_send, z_send, ys_send, ys_recv, o_send, o_recv, halo_send, halo_recv,
    wc_send, wc_recv, wz_send, wz_recv, wy_send, wy_recv, wx_send, wx_recv, wo_send, wo_recv,
):
    u, c = lax.axis_index("users"), lax.axis_index("cand")
    core = lax.rem(u, NCORE)
    zh = lax.rem(u // NCORE, NZH)
    x = u // (NCORE * NZH)
    z = lax.rem(c, NZL)
    y = c // NZL
    rows = q_hbm.shape[0]
    q_ref, k_ref, v_ref, gate_ref, res_ref = [rows5.at[i] for i in range(5)]

    def share(y_):
        return pl.ds(pl.multiple_of(y_ * SHARE, SHARE), SHARE)

    incoming = [
        pltpu.make_async_copy(src, dst, in_sem.at[i])
        for i, (src, dst) in enumerate([
            (w_hbm, w_ref), (ids_hbm, ids_ref), (pat_hbm, pat_ref),
            (hk_hbm.at[:, share(y)], kvh.at[z, 0, y]), (hv_hbm.at[:, share(y)], kvh.at[z, 1, y]),
            (q_hbm.at[:, share(y)], qh.at[y]),
            (q_hbm, q_ref), (k_hbm, k_ref), (v_hbm, v_ref), (gate_hbm, gate_ref), (res_hbm, res_ref),
        ])
    ]
    for copy in incoming:
        copy.start()

    def dev(x_, zh_, core_, y_, z_):
        return {"users": (x_ * NZH + zh_) * NCORE + core_, "cand": y_ * NZL + z_}

    def on_cand(c_):
        return {"users": u, "cand": c_}

    def along_z(d):
        far = lax.rem(zh * NZL + z + d, NZH * NZL)
        return far // NZL, lax.rem(far, NZL)

    other_core = dev(x, zh, 1 - core, y, z)
    nxt, prv = lax.rem(c + 1, NCAND), lax.rem(c + NCAND - 1, NCAND)

    barrier = pltpu.get_barrier_semaphore()

    def greet(device):
        pl.semaphore_signal(barrier, inc=1, device_id=device, device_id_type=MESH)

    for d in range(1, NZH * NZL):
        zh_, z_ = along_z(d)
        greet(dev(x, zh_, core, y, z_))
    for d in range(1, NY):
        greet(dev(x, zh, core, lax.rem(y + d, NY), z))
    for d in range(1, NX):
        greet(dev(lax.rem(x + d, NX), zh, core, y, z))
    greet(other_core)

    @pl.when(z == NZL - 1)
    def _():
        greet(on_cand(nxt))

    @pl.when(z == 0)
    def _():
        greet(on_cand(prv))

    partners = NZH * NZL - 1 + NY - 1 + NX - 1 + 1
    edge = jnp.where(z == 0, 1, 0) + jnp.where(z == NZL - 1, 1, 0)
    pl.semaphore_wait(barrier, partners + edge)

    def remote(src, dst, send, recv, device):
        return pltpu.make_async_remote_copy(
            src_ref=src, dst_ref=dst, send_sem=send, recv_sem=recv,
            device_id=device, device_id_type=MESH,
        )

    def z_of(t):
        both = 2 * jnp.minimum(z, NZL - 1 - z)
        turn = z - (t + 1) // 2 if t % 2 else z + t // 2
        return jnp.where(t <= both, turn, jnp.where(2 * z < NZL, t, NZL - 1 - t))

    def to_head(i, d):
        y_ = lax.rem(y + d, NY)
        src = (hk_hbm, hv_hbm, q_hbm)[i].at[:, share(y_)]
        dst = qh.at[y] if i == 2 else kvh.at[z, i, y]
        return remote(src, dst, ys_send.at[i, d - 1], ys_recv.at[i, d - 1], on_cand(y_ * NZL + z))

    def at_head(i, d):
        y_ = lax.rem(y + NY - d, NY)
        here = qh.at[y_] if i == 2 else kvh.at[z, i, y_]
        remote(here, here, ys_send.at[0, 0], ys_recv.at[i, d - 1], other_core).wait_recv()

    def from_head(d):
        y_ = lax.rem(y + d, NY)
        return remote(part_out.at[y_], part_in.at[y], o_send.at[d - 1], o_recv.at[d - 1], on_cand(y_ * NZL + z))

    def back_home(d):
        here = part_in.at[lax.rem(y + NY - d, NY)]
        remote(here, here, o_send.at[0], o_recv.at[d - 1], other_core).wait_recv()

    def own_z(a, way):
        to = on_cand(y * NZL + (z + 1 if way == 0 else z - 1))
        return remote(kvh.at[z, a], kvh.at[z, a], own_send.at[way, a], kv_recv.at[a, z], to)

    def hop_z(a, z_):
        to = on_cand(y * NZL + z + jnp.where(z_ < z, 1, -1))
        return remote(kvh.at[z_, a], kvh.at[z_, a], z_send.at[a, z_], kv_recv.at[a, z_], to)

    def goes_on(z_):
        return ((z_ < z) & (z < NZL - 1)) | ((z_ > z) & (z > 0))

    def arrived(a, z_):
        here = kvh.at[z_, a]
        remote(here, here, own_send.at[0, 0], kv_recv.at[a, z_], other_core).wait_recv()

    def halo_copy(way, a):
        return remote(
            (k_hbm, v_hbm)[a], halo.at[way, a], halo_send.at[way, a], halo_recv.at[way, a],
            on_cand(nxt if way == 0 else prv),
        )

    tile_core = remote(w_hbm, wtmp, wc_send, wc_recv, other_core)

    def tile_z(d):
        zh_, z_ = along_z(d)
        here = wb.at[core, x, y, z]
        return remote(here, here, wz_send.at[d - 1], wz_recv.at[z], dev(x, zh_, core, y, z_))

    def tile_y(d):
        here = wb.at[core, x, y]
        return remote(here, here, wy_send.at[d - 1], wy_recv.at[d - 1], dev(x, zh, core, lax.rem(y + d, NY), z))

    def tile_x(d):
        here = wb.at[core, x]
        return remote(here, here, wx_send.at[d - 1], wx_recv.at[d - 1], dev(lax.rem(x + d, NX), zh, core, y, z))

    def tile_out(d):
        here = wb.at[core, lax.rem(x + d, NX)]
        return remote(here, here, wo_send.at[d], wo_recv.at[d], other_core)

    for i in range(3):
        for d in range(1, NY):
            to_head(i, d).start()
    tile_core.start()

    for copy in incoming[:3]:
        copy.wait()

    def ids_row(b):
        at = jnp.clip(b, 0, NCAND - 1) * DH
        got = ids_ref[:, pl.ds(pl.multiple_of(at, DH), DH)].astype(F32)
        return jnp.where((b >= 0) & (b < NCAND), got, -1.0)

    square = (rows, rows)
    sub = lax.broadcasted_iota(jnp.int32, square, 0)
    lane = lax.broadcasted_iota(jnp.int32, square, 1)
    half_factor = 0.5 * DH ** (-0.5)

    def make_mask():
        ids = [ids_row(c + d) for d in (-2, -1, 0, 1)]
        wide = [jnp.broadcast_to(r, square) for r in ids]
        tall = [w.T for w in wide]
        offs = []
        for b in (1, 2, 3):
            whole = jnp.where(tall[b - 1] == wide[b], 1.0, 0.0)
            part = jnp.where((tall[b] == wide[b]) & (sub < lane), 1.0, 0.0)
            offs.append(jnp.sum(whole + part, axis=0, keepdims=True))
        own_off = jnp.broadcast_to(offs[1], square).T
        hot_rows = jnp.where(own_off == lane.astype(F32), 1.0, 0.0).astype(BF16)
        allowed = jnp.where(pat_ref[...] == 1, 1.0, 0.0).astype(BF16)
        by_row = dot(hot_rows, allowed).astype(BF16)
        for b in range(3):
            hot_keys = jnp.where(sub.astype(F32) == jnp.broadcast_to(offs[b], square), 1.0, 0.0).astype(BF16)
            seen = dot(by_row, hot_keys) > 0.5
            if b == 1:
                seen = seen | (sub == lane)
            seen = seen & (tall[2] == wide[b + 1])
            maskh[b] = jnp.where(seen, half_factor, 0.0)

    for copy in incoming[3:5]:
        copy.wait()
    for a in range(2):
        for d in range(1, NY):
            at_head(a, d)

        @pl.when(z < NZL - 1)
        def _():
            own_z(a, 0).start()

        @pl.when(z > 0)
        def _():
            own_z(a, 1).start()

    tile_core.wait()
    mine, theirs = w_ref[...].astype(F32), wtmp[...].astype(F32)
    tile = jnp.where(
        core == 0, jnp.concatenate([mine, theirs], axis=1), jnp.concatenate([theirs, mine], axis=1)
    ).astype(BF16)

    @pl.when(core == zh)
    def _():
        wb[core, x, y, z] = tile
        for d in range(1, NZH * NZL):
            tile_z(d).start()

    make_mask()

    def own_chunk():
        for copy in incoming[6:9]:
            copy.wait()
        for h in range(H):
            cols = slice(h * DH, (h + 1) * DH)
            weights = silu_of_half(dot_t(q_ref[:, cols], k_ref[:, cols]) * maskh[1])
            att[:, cols] = dot(weights, v_ref[:, cols])

    def halo_chunk(way):
        for a in range(2):
            halo_copy(way, a).wait_recv()
        for h in range(H):
            cols = slice(h * DH, (h + 1) * DH)
            weights = silu_of_half(dot_t(q_ref[:, cols], halo[way, 0, :, cols]) * maskh[2 * way])
            att[:, cols] = att[:, cols] + dot(weights, halo[way, 1, :, cols])

    def hist_chunk(t):
        z_ = z_of(t)
        if t == 0:
            incoming[5].wait()
            for d in range(1, NY):
                at_head(2, d)
        for h in range(HEADS):
            cols = slice(h * DH, (h + 1) * DH)
            keys = kvh[z_, 0, :, :, cols].reshape(-1, DH)
            values = kvh[z_, 1, :, :, cols].reshape(-1, DH)
            weights = silu_of_half(dot_t(qh[:, :, cols].reshape(-1, DH), keys) * half_factor)
            more = dot(weights, values)
            oh[h] = more if t == 0 else oh[h] + more

    halo_at = {1: [(0, 0)], 3: [(0, 1)], 5: [(1, 0)], 7: [(1, 1)]}
    for t in range(1, NZL):
        z_ = z_of(t)
        for a in range(2):
            arrived(a, z_)

            @pl.when(goes_on(z_))
            def _():
                hop_z(a, z_).start()

        for way, a in halo_at.get(t, []):
            halo_copy(way, a).start()
        if t == 1:
            own_chunk()
        if t == 2:
            for z_ in range(NZL):
                @pl.when((core != zh) | (z != z_))
                def _():
                    there = wb.at[core, x, y, z_]
                    remote(there, there, wz_send.at[0], wz_recv.at[z_], other_core).wait_recv()
            for d in range(1, NY):
                tile_y(d).start()
        if t == 4:
            for d in range(1, NY):
                there = wb.at[core, x, lax.rem(y + NY - d, NY)]
                remote(there, there, wy_send.at[0], wy_recv.at[d - 1], other_core).wait_recv()
            for d in range(1, NX):
                tile_x(d).start()
            tile_out(0).start()
        hist_chunk(t - 1)
    hist_chunk(NZL - 1)
    for y_ in range(NY):
        for h in range(HEADS):
            part_out[y_, :, h * DH:(h + 1) * DH] = oh[h, y_ * rows:(y_ + 1) * rows].astype(BF16)
    for d in range(1, NY):
        from_head(d).start()
    part_in[y] = part_out[y]
    for d in range(1, NX):
        there = wb.at[core, lax.rem(x + NX - d, NX)]
        remote(there, there, wx_send.at[0], wx_recv.at[d - 1], other_core).wait_recv()
        tile_out(NX - d).start()
    halo_chunk(0)
    halo_chunk(1)

    for copy in incoming[9:]:
        copy.wait()
    for d in range(1, NY):
        back_home(d)
    for y_ in range(NY):
        cols = slice(y_ * SHARE, (y_ + 1) * SHARE)
        att[:, cols] = att[:, cols] + part_in[y_].astype(F32)
    attended = att[...]
    center = jnp.mean(attended, axis=1, keepdims=True)
    moved = attended - center
    spread = jnp.mean(moved * moved, axis=1, keepdims=True)
    gated = (moved * lax.rsqrt(spread + 1e-05) * gate_ref[...].astype(F32)).astype(BF16)

    for d in range(NX):
        there = wb.at[1 - core, lax.rem(x + d, NX)]
        remote(there, there, wo_send.at[0], wo_recv.at[d], other_core).wait_recv()
    for x_ in range(NX):
        cols = slice(x_ * 2 * DH, (x_ + 1) * 2 * DH)
        weight = jnp.concatenate(
            [wb[0, x_].reshape(-1, DH), wb[1, x_].reshape(-1, DH)], axis=1
        )
        out_ref[:, cols] = (res_ref[:, cols].astype(F32) + dot(gated, weight)).astype(BF16)

    @pl.when(z < NZL - 1)
    def _():
        for a in range(2):
            own_z(a, 0).wait_send()

    @pl.when(z > 0)
    def _():
        for a in range(2):
            own_z(a, 1).wait_send()

    for t in range(1, NZL):
        z_ = z_of(t)

        @pl.when(goes_on(z_))
        def _():
            for a in range(2):
                hop_z(a, z_).wait_send()

    for d in range(1, NY):
        for i in range(3):
            to_head(i, d).wait_send()
        from_head(d).wait_send()
    for way in range(2):
        for a in range(2):
            halo_copy(way, a).wait_send()

    @pl.when(core == zh)
    def _():
        for d in range(1, NZH * NZL):
            tile_z(d).wait_send()

    for d in range(1, NY):
        tile_y(d).wait_send()
    for d in range(1, NX):
        tile_x(d).wait_send()
    for d in range(NX):
        tile_out(d).wait_send()


def shards(q, k, v, gate, resid, hk, hv, ids, pattern, weight):
    rows, width = q.shape[1:]
    hist = hk.shape[1]
    hbm = pl.BlockSpec(memory_space=pl.ANY)
    vmem = pl.BlockSpec(memory_space=pltpu.VMEM)
    dma = pltpu.SemaphoreType.DMA
    out = pl.pallas_call(
        kernel,
        out_shape=jax.ShapeDtypeStruct((rows, width), BF16),
        in_specs=[hbm] * 10,
        out_specs=vmem,
        scratch_shapes=[
            pltpu.VMEM((5, rows, width), BF16),
            pltpu.VMEM(ids.shape, ids.dtype),
            pltpu.VMEM(pattern.shape, pattern.dtype),
            pltpu.VMEM(weight.shape, BF16),
            pltpu.VMEM((NZL, 2, NY, hist, SHARE), BF16),
            pltpu.VMEM((NY, rows, SHARE), BF16),
            pltpu.VMEM((HEADS, NY * rows, DH), F32),
            pltpu.VMEM((NY, rows, SHARE), BF16),
            pltpu.VMEM((NY, rows, SHARE), BF16),
            pltpu.VMEM((2, 2, rows, width), BF16),
            pltpu.VMEM(weight.shape, BF16),
            pltpu.VMEM((NZH, NX, NY, NZL, weight.shape[0], 2 * weight.shape[1]), BF16),
            pltpu.VMEM((3, rows, rows), F32),
            pltpu.VMEM((rows, width), F32),
            dma((11,)), dma((2, NZL)), dma((2, 2)), dma((2, NZL)), dma((3, NY - 1)), dma((3, NY - 1)),
            dma((NY - 1,)), dma((NY - 1,)), dma((2, 2)), dma((2, 2)),
            dma, dma, dma((NZH * NZL - 1,)), dma((NZL,)), dma((NY - 1,)), dma((NY - 1,)),
            dma((NX - 1,)), dma((NX - 1,)), dma((NX,)), dma((NX,)),
        ],
        compiler_params=pltpu.CompilerParams(
            collective_id=0, has_side_effects=True, vmem_limit_bytes=60 * 1024 * 1024
        ),
    )(q[0], k[0], v[0], gate[0], resid[0], hk[0], hv[0], ids, pattern, weight)
    return out[None]


def solution(mesh):
    part = P("users", "cand", None)
    return jax.shard_map(
        shards,
        mesh=mesh,
        in_specs=(part,) * 7 + (P("users", None), P(), P("cand", "users")),
        out_specs=part,
        check_vma=False,
    )
```

```python
import jax
import jax.numpy as jnp
from jax import lax
from jax.experimental import pallas as pl
from jax.experimental.pallas import tpu as pltpu
from jax.sharding import PartitionSpec as P

H = 8
DH = 128
NX, NZH, NCORE = 4, 2, 2
NY, NZL = 4, 8
NCAND = NY * NZL
HEADS = H // NY
SHARE = HEADS * DH
MESH = pl.DeviceIdType.MESH
BF16, F32 = jnp.bfloat16, jnp.float32


def dot(a, b):
    return lax.dot_general(a, b, (((1,), (0,)), ((), ())), preferred_element_type=F32)


def dot_t(a, b):
    return lax.dot_general(a, b, (((1,), (1,)), ((), ())), preferred_element_type=F32)


def silu_of_half(h):
    return (h + h * jnp.tanh(h)).astype(BF16)


def kernel(
    q_hbm, k_hbm, v_hbm, gate_hbm, res_hbm, hk_hbm, hv_hbm, ids_hbm, pat_hbm, w_hbm,
    out_ref,
    rows5, ids_ref, pat_ref, w_ref,
    kvh, qh, oh, part_out, part_in, halo, wtmp, wb, maskh, att,
    in_sem, kv_recv, own_send, z_send, ys_send, ys_recv, o_send, o_recv, halo_send, halo_recv,
    wc_send, wc_recv, wz_send, wz_recv, wy_send, wy_recv, wx_send, wx_recv, wo_send, wo_recv,
):
    u, c = lax.axis_index("users"), lax.axis_index("cand")
    core = lax.rem(u, NCORE)
    zh = lax.rem(u // NCORE, NZH)
    x = u // (NCORE * NZH)
    z = lax.rem(c, NZL)
    y = c // NZL
    rows = q_hbm.shape[0]
    q_ref, k_ref, v_ref, gate_ref, res_ref = [rows5.at[i] for i in range(5)]

    def share(y_):
        return pl.ds(pl.multiple_of(y_ * SHARE, SHARE), SHARE)

    incoming = [
        pltpu.make_async_copy(src, dst, in_sem.at[i])
        for i, (src, dst) in enumerate([
            (w_hbm, w_ref), (ids_hbm, ids_ref), (pat_hbm, pat_ref),
            (hk_hbm.at[:, share(y)], kvh.at[z, 0, y]), (hv_hbm.at[:, share(y)], kvh.at[z, 1, y]),
            (q_hbm.at[:, share(y)], qh.at[y]),
            (q_hbm, q_ref), (k_hbm, k_ref), (v_hbm, v_ref), (gate_hbm, gate_ref), (res_hbm, res_ref),
        ])
    ]
    for copy in incoming:
        copy.start()

    def dev(x_, zh_, core_, y_, z_):
        return {"users": (x_ * NZH + zh_) * NCORE + core_, "cand": y_ * NZL + z_}

    def on_cand(c_):
        return {"users": u, "cand": c_}

    def along_z(d):
        far = lax.rem(zh * NZL + z + d, NZH * NZL)
        return far // NZL, lax.rem(far, NZL)

    other_core = dev(x, zh, 1 - core, y, z)
    nxt, prv = lax.rem(c + 1, NCAND), lax.rem(c + NCAND - 1, NCAND)

    barrier = pltpu.get_barrier_semaphore()

    def greet(device):
        pl.semaphore_signal(barrier, inc=1, device_id=device, device_id_type=MESH)

    for d in range(1, NZH * NZL):
        zh_, z_ = along_z(d)
        greet(dev(x, zh_, core, y, z_))
    for d in range(1, NY):
        greet(dev(x, zh, core, lax.rem(y + d, NY), z))
    for d in range(1, NX):
        greet(dev(lax.rem(x + d, NX), zh, core, y, z))
    greet(other_core)

    @pl.when(z == NZL - 1)
    def _():
        greet(on_cand(nxt))

    @pl.when(z == 0)
    def _():
        greet(on_cand(prv))

    partners = NZH * NZL - 1 + NY - 1 + NX - 1 + 1
    edge = jnp.where(z == 0, 1, 0) + jnp.where(z == NZL - 1, 1, 0)
    pl.semaphore_wait(barrier, partners + edge)

    def remote(src, dst, send, recv, device):
        return pltpu.make_async_remote_copy(
            src_ref=src, dst_ref=dst, send_sem=send, recv_sem=recv,
            device_id=device, device_id_type=MESH,
        )

    def z_of(t):
        both = 2 * jnp.minimum(z, NZL - 1 - z)
        turn = z - (t + 1) // 2 if t % 2 else z + t // 2
        return jnp.where(t <= both, turn, jnp.where(2 * z < NZL, t, NZL - 1 - t))

    def to_head(i, d):
        y_ = lax.rem(y + d, NY)
        src = (hk_hbm, hv_hbm, q_hbm)[i].at[:, share(y_)]
        dst = qh.at[y] if i == 2 else kvh.at[z, i, y]
        return remote(src, dst, ys_send.at[i, d - 1], ys_recv.at[i, d - 1], on_cand(y_ * NZL + z))

    def at_head(i, d):
        y_ = lax.rem(y + NY - d, NY)
        here = qh.at[y_] if i == 2 else kvh.at[z, i, y_]
        remote(here, here, ys_send.at[0, 0], ys_recv.at[i, d - 1], other_core).wait_recv()

    def from_head(d):
        y_ = lax.rem(y + d, NY)
        return remote(part_out.at[y_], part_in.at[y], o_send.at[d - 1], o_recv.at[d - 1], on_cand(y_ * NZL + z))

    def back_home(d):
        here = part_in.at[lax.rem(y + NY - d, NY)]
        remote(here, here, o_send.at[0], o_recv.at[d - 1], other_core).wait_recv()

    def own_z(a, way):
        to = on_cand(y * NZL + (z + 1 if way == 0 else z - 1))
        return remote(kvh.at[z, a], kvh.at[z, a], own_send.at[way, a], kv_recv.at[a, z], to)

    def hop_z(a, z_):
        to = on_cand(y * NZL + z + jnp.where(z_ < z, 1, -1))
        return remote(kvh.at[z_, a], kvh.at[z_, a], z_send.at[a, z_], kv_recv.at[a, z_], to)

    def goes_on(z_):
        return ((z_ < z) & (z < NZL - 1)) | ((z_ > z) & (z > 0))

    def arrived(a, z_):
        here = kvh.at[z_, a]
        remote(here, here, own_send.at[0, 0], kv_recv.at[a, z_], other_core).wait_recv()

    def halo_copy(way, a):
        return remote(
            (k_hbm, v_hbm)[a], halo.at[way, a], halo_send.at[way, a], halo_recv.at[way, a],
            on_cand(nxt if way == 0 else prv),
        )

    tile_core = remote(w_hbm, wtmp, wc_send, wc_recv, other_core)

    def tile_z(d):
        zh_, z_ = along_z(d)
        here = wb.at[core, x, y, z]
        return remote(here, here, wz_send.at[d - 1], wz_recv.at[z], dev(x, zh_, core, y, z_))

    def tile_y(d):
        here = wb.at[core, x, y]
        return remote(here, here, wy_send.at[d - 1], wy_recv.at[d - 1], dev(x, zh, core, lax.rem(y + d, NY), z))

    def tile_x(d):
        here = wb.at[core, x]
        return remote(here, here, wx_send.at[d - 1], wx_recv.at[d - 1], dev(lax.rem(x + d, NX), zh, core, y, z))

    def tile_out(d):
        here = wb.at[core, lax.rem(x + d, NX)]
        return remote(here, here, wo_send.at[d], wo_recv.at[d], other_core)

    for i in range(3):
        for d in range(1, NY):
            to_head(i, d).start()
    halo_copy(0, 0).start()
    tile_core.start()

    for copy in incoming[:3]:
        copy.wait()

    def ids_row(b):
        at = jnp.clip(b, 0, NCAND - 1) * DH
        got = ids_ref[:, pl.ds(pl.multiple_of(at, DH), DH)].astype(F32)
        return jnp.where((b >= 0) & (b < NCAND), got, -1.0)

    square = (rows, rows)
    sub = lax.broadcasted_iota(jnp.int32, square, 0)
    lane = lax.broadcasted_iota(jnp.int32, square, 1)
    half_factor = 0.5 * DH ** (-0.5)

    def make_mask():
        ids = [ids_row(c + d) for d in (-2, -1, 0, 1)]
        wide = [jnp.broadcast_to(r, square) for r in ids]
        tall = [w.T for w in wide]
        offs = []
        for b in (1, 2, 3):
            whole = jnp.where(tall[b - 1] == wide[b], 1.0, 0.0)
            part = jnp.where((tall[b] == wide[b]) & (sub < lane), 1.0, 0.0)
            offs.append(jnp.sum(whole + part, axis=0, keepdims=True))
        own_off = jnp.broadcast_to(offs[1], square).T
        hot_rows = jnp.where(own_off == lane.astype(F32), 1.0, 0.0).astype(BF16)
        allowed = jnp.where(pat_ref[...] == 1, 1.0, 0.0).astype(BF16)
        by_row = dot(hot_rows, allowed).astype(BF16)
        for b in range(3):
            hot_keys = jnp.where(sub.astype(F32) == jnp.broadcast_to(offs[b], square), 1.0, 0.0).astype(BF16)
            seen = dot(by_row, hot_keys) > 0.5
            if b == 1:
                seen = seen | (sub == lane)
            seen = seen & (tall[2] == wide[b + 1])
            maskh[b] = jnp.where(seen, half_factor, 0.0)

    for copy in incoming[3:5]:
        copy.wait()
    for a in range(2):
        for d in range(1, NY):
            at_head(a, d)

        @pl.when(z < NZL - 1)
        def _():
            own_z(a, 0).start()

        @pl.when(z > 0)
        def _():
            own_z(a, 1).start()

    tile_core.wait()
    mine, theirs = w_ref[...].astype(F32), wtmp[...].astype(F32)
    tile = jnp.where(
        core == 0, jnp.concatenate([mine, theirs], axis=1), jnp.concatenate([theirs, mine], axis=1)
    ).astype(BF16)

    @pl.when(core == zh)
    def _():
        wb[core, x, y, z] = tile
        for d in range(1, NZH * NZL):
            tile_z(d).start()

    make_mask()

    def own_chunk():
        for copy in incoming[6:9]:
            copy.wait()
        for h in range(H):
            cols = slice(h * DH, (h + 1) * DH)
            weights = silu_of_half(dot_t(q_ref[:, cols], k_ref[:, cols]) * maskh[1])
            att[:, cols] = dot(weights, v_ref[:, cols])

    def halo_chunk(way):
        for a in range(2):
            halo_copy(way, a).wait_recv()
        for h in range(H):
            cols = slice(h * DH, (h + 1) * DH)
            weights = silu_of_half(dot_t(q_ref[:, cols], halo[way, 0, :, cols]) * maskh[2 * way])
            att[:, cols] = att[:, cols] + dot(weights, halo[way, 1, :, cols])

    def hist_chunk(t):
        z_ = z_of(t)
        if t == 0:
            incoming[5].wait()
            for d in range(1, NY):
                at_head(2, d)
        for h in range(HEADS):
            cols = slice(h * DH, (h + 1) * DH)
            keys = kvh[z_, 0, :, :, cols].reshape(-1, DH)
            values = kvh[z_, 1, :, :, cols].reshape(-1, DH)
            weights = silu_of_half(dot_t(qh[:, :, cols].reshape(-1, DH), keys) * half_factor)
            more = dot(weights, values)
            oh[h] = more if t == 0 else oh[h] + more

    halo_at = {1: [(1, 0)], 3: [(0, 1)], 5: [(1, 1)]}
    for t in range(1, NZL):
        z_ = z_of(t)
        for a in range(2):
            arrived(a, z_)

            @pl.when(goes_on(z_))
            def _():
                hop_z(a, z_).start()

        for way, a in halo_at.get(t, []):
            halo_copy(way, a).start()
        if t == 1:
            own_chunk()
        if t == 2:
            for z_ in range(NZL):
                @pl.when((core != zh) | (z != z_))
                def _():
                    there = wb.at[core, x, y, z_]
                    remote(there, there, wz_send.at[0], wz_recv.at[z_], other_core).wait_recv()
            for d in range(1, NY):
                tile_y(d).start()
        if t == 4:
            for d in range(1, NY):
                there = wb.at[core, x, lax.rem(y + NY - d, NY)]
                remote(there, there, wy_send.at[0], wy_recv.at[d - 1], other_core).wait_recv()
            for d in range(1, NX):
                tile_x(d).start()
            tile_out(0).start()
        hist_chunk(t - 1)
    hist_chunk(NZL - 1)
    for y_ in range(NY):
        for h in range(HEADS):
            part_out[y_, :, h * DH:(h + 1) * DH] = oh[h, y_ * rows:(y_ + 1) * rows].astype(BF16)
    for d in range(1, NY):
        from_head(d).start()
    part_in[y] = part_out[y]
    for d in range(1, NX):
        there = wb.at[core, lax.rem(x + NX - d, NX)]
        remote(there, there, wx_send.at[0], wx_recv.at[d - 1], other_core).wait_recv()
        tile_out(NX - d).start()
    halo_chunk(0)
    halo_chunk(1)

    for copy in incoming[9:]:
        copy.wait()
    for d in range(1, NY):
        back_home(d)
    for y_ in range(NY):
        cols = slice(y_ * SHARE, (y_ + 1) * SHARE)
        att[:, cols] = att[:, cols] + part_in[y_].astype(F32)
    attended = att[...]
    center = jnp.mean(attended, axis=1, keepdims=True)
    moved = attended - center
    spread = jnp.mean(moved * moved, axis=1, keepdims=True)
    gated = (moved * lax.rsqrt(spread + 1e-05) * gate_ref[...].astype(F32)).astype(BF16)

    for d in range(NX):
        there = wb.at[1 - core, lax.rem(x + d, NX)]
        remote(there, there, wo_send.at[0], wo_recv.at[d], other_core).wait_recv()
    for x_ in range(NX):
        cols = slice(x_ * 2 * DH, (x_ + 1) * 2 * DH)
        weight = jnp.concatenate(
            [wb[0, x_].reshape(-1, DH), wb[1, x_].reshape(-1, DH)], axis=1
        )
        out_ref[:, cols] = (res_ref[:, cols].astype(F32) + dot(gated, weight)).astype(BF16)

    @pl.when(z < NZL - 1)
    def _():
        for a in range(2):
            own_z(a, 0).wait_send()

    @pl.when(z > 0)
    def _():
        for a in range(2):
            own_z(a, 1).wait_send()

    for t in range(1, NZL):
        z_ = z_of(t)

        @pl.when(goes_on(z_))
        def _():
            for a in range(2):
                hop_z(a, z_).wait_send()

    for d in range(1, NY):
        for i in range(3):
            to_head(i, d).wait_send()
        from_head(d).wait_send()
    for way in range(2):
        for a in range(2):
            halo_copy(way, a).wait_send()

    @pl.when(core == zh)
    def _():
        for d in range(1, NZH * NZL):
            tile_z(d).wait_send()

    for d in range(1, NY):
        tile_y(d).wait_send()
    for d in range(1, NX):
        tile_x(d).wait_send()
    for d in range(NX):
        tile_out(d).wait_send()


def shards(q, k, v, gate, resid, hk, hv, ids, pattern, weight):
    rows, width = q.shape[1:]
    hist = hk.shape[1]
    hbm = pl.BlockSpec(memory_space=pl.ANY)
    vmem = pl.BlockSpec(memory_space=pltpu.VMEM)
    dma = pltpu.SemaphoreType.DMA
    out = pl.pallas_call(
        kernel,
        out_shape=jax.ShapeDtypeStruct((rows, width), BF16),
        in_specs=[hbm] * 10,
        out_specs=vmem,
        scratch_shapes=[
            pltpu.VMEM((5, rows, width), BF16),
            pltpu.VMEM(ids.shape, ids.dtype),
            pltpu.VMEM(pattern.shape, pattern.dtype),
            pltpu.VMEM(weight.shape, BF16),
            pltpu.VMEM((NZL, 2, NY, hist, SHARE), BF16),
            pltpu.VMEM((NY, rows, SHARE), BF16),
            pltpu.VMEM((HEADS, NY * rows, DH), F32),
            pltpu.VMEM((NY, rows, SHARE), BF16),
            pltpu.VMEM((NY, rows, SHARE), BF16),
            pltpu.VMEM((2, 2, rows, width), BF16),
            pltpu.VMEM(weight.shape, BF16),
            pltpu.VMEM((NZH, NX, NY, NZL, weight.shape[0], 2 * weight.shape[1]), BF16),
            pltpu.VMEM((3, rows, rows), F32),
            pltpu.VMEM((rows, width), F32),
            dma((11,)), dma((2, NZL)), dma((2, 2)), dma((2, NZL)), dma((3, NY - 1)), dma((3, NY - 1)),
            dma((NY - 1,)), dma((NY - 1,)), dma((2, 2)), dma((2, 2)),
            dma, dma, dma((NZH * NZL - 1,)), dma((NZL,)), dma((NY - 1,)), dma((NY - 1,)),
            dma((NX - 1,)), dma((NX - 1,)), dma((NX,)), dma((NX,)),
        ],
        compiler_params=pltpu.CompilerParams(
            collective_id=0, has_side_effects=True, vmem_limit_bytes=60 * 1024 * 1024
        ),
    )(q[0], k[0], v[0], gate[0], resid[0], hk[0], hv[0], ids, pattern, weight)
    return out[None]


def solution(mesh):
    part = P("users", "cand", None)
    return jax.shard_map(
        shards,
        mesh=mesh,
        in_specs=(part,) * 7 + (P("users", None), P(), P("cand", "users")),
        out_specs=part,
        check_vma=False,
    )
```

```python
import jax
import jax.numpy as jnp
from jax import lax
from jax.experimental import pallas as pl
from jax.experimental.pallas import tpu as pltpu
from jax.sharding import PartitionSpec as P

H = 8
DH = 128
NX, NZH, NCORE = 4, 2, 2
NY, NZL = 4, 8
NCAND = NY * NZL
HEADS = H // NY
SHARE = HEADS * DH
MESH = pl.DeviceIdType.MESH
BF16, F32 = jnp.bfloat16, jnp.float32


def dot(a, b):
    return lax.dot_general(a, b, (((1,), (0,)), ((), ())), preferred_element_type=F32)


def dot_t(a, b):
    return lax.dot_general(a, b, (((1,), (1,)), ((), ())), preferred_element_type=F32)


def silu_of_half(h):
    return (h + h * jnp.tanh(h)).astype(BF16)


def kernel(
    q_hbm, k_hbm, v_hbm, gate_hbm, res_hbm, hk_hbm, hv_hbm, ids_hbm, pat_hbm, w_hbm,
    out_ref,
    rows5, ids_ref, pat_ref, w_ref,
    kvh, qh, oh, part_out, part_in, halo, far_out, far_in, wtmp, wb, maskh, att,
    in_sem, kv_recv, own_send, z_send, ys_send, ys_recv, o_send, o_recv, halo_send, halo_recv,
    wc_send, wc_recv, wz_send, wz_recv, wy_send, wy_recv, wx_send, wx_recv, wo_send, wo_recv,
):
    u, c = lax.axis_index("users"), lax.axis_index("cand")
    core = lax.rem(u, NCORE)
    zh = lax.rem(u // NCORE, NZH)
    x = u // (NCORE * NZH)
    z = lax.rem(c, NZL)
    y = c // NZL
    rows = q_hbm.shape[0]
    q_ref, k_ref, v_ref, gate_ref, res_ref = [rows5.at[i] for i in range(5)]

    def share(y_):
        return pl.ds(pl.multiple_of(y_ * SHARE, SHARE), SHARE)

    incoming = [
        pltpu.make_async_copy(src, dst, in_sem.at[i])
        for i, (src, dst) in enumerate([
            (w_hbm, w_ref), (ids_hbm, ids_ref), (pat_hbm, pat_ref),
            (hk_hbm.at[:, share(y)], kvh.at[z, 0, y]), (hv_hbm.at[:, share(y)], kvh.at[z, 1, y]),
            (q_hbm.at[:, share(y)], qh.at[y]),
            (q_hbm, q_ref), (k_hbm, k_ref), (v_hbm, v_ref), (gate_hbm, gate_ref), (res_hbm, res_ref),
        ])
    ]
    for copy in incoming:
        copy.start()

    def dev(x_, zh_, core_, y_, z_):
        return {"users": (x_ * NZH + zh_) * NCORE + core_, "cand": y_ * NZL + z_}

    def on_cand(c_):
        return {"users": u, "cand": c_}

    def along_z(d):
        far = lax.rem(zh * NZL + z + d, NZH * NZL)
        return far // NZL, lax.rem(far, NZL)

    other_core = dev(x, zh, 1 - core, y, z)
    nxt, prv = lax.rem(c + 1, NCAND), lax.rem(c + NCAND - 1, NCAND)

    barrier = pltpu.get_barrier_semaphore()

    def greet(device):
        pl.semaphore_signal(barrier, inc=1, device_id=device, device_id_type=MESH)

    for d in range(1, NZH * NZL):
        zh_, z_ = along_z(d)
        greet(dev(x, zh_, core, y, z_))
    for d in range(1, NY):
        greet(dev(x, zh, core, lax.rem(y + d, NY), z))
    for d in range(1, NX):
        greet(dev(lax.rem(x + d, NX), zh, core, y, z))
    greet(other_core)

    @pl.when(z == NZL - 1)
    def _():
        greet(on_cand(nxt))

    @pl.when(z == 0)
    def _():
        greet(on_cand(prv))

    partners = NZH * NZL - 1 + NY - 1 + NX - 1 + 1
    edge = jnp.where(z == 0, 1, 0) + jnp.where(z == NZL - 1, 1, 0)
    pl.semaphore_wait(barrier, partners + edge)

    def remote(src, dst, send, recv, device):
        return pltpu.make_async_remote_copy(
            src_ref=src, dst_ref=dst, send_sem=send, recv_sem=recv,
            device_id=device, device_id_type=MESH,
        )

    def z_of(t):
        both = 2 * jnp.minimum(z, NZL - 1 - z)
        turn = z - (t + 1) // 2 if t % 2 else z + t // 2
        return jnp.where(t <= both, turn, jnp.where(2 * z < NZL, t, NZL - 1 - t))

    def to_head(i, d):
        y_ = lax.rem(y + d, NY)
        src = (hk_hbm, hv_hbm, q_hbm)[i].at[:, share(y_)]
        dst = qh.at[y] if i == 2 else kvh.at[z, i, y]
        return remote(src, dst, ys_send.at[i, d - 1], ys_recv.at[i, d - 1], on_cand(y_ * NZL + z))

    def at_head(i, d):
        y_ = lax.rem(y + NY - d, NY)
        here = qh.at[y_] if i == 2 else kvh.at[z, i, y_]
        remote(here, here, ys_send.at[0, 0], ys_recv.at[i, d - 1], other_core).wait_recv()

    def from_head(d):
        y_ = lax.rem(y + d, NY)
        return remote(part_out.at[y_], part_in.at[y], o_send.at[d - 1], o_recv.at[d - 1], on_cand(y_ * NZL + z))

    def back_home(d):
        here = part_in.at[lax.rem(y + NY - d, NY)]
        remote(here, here, o_send.at[0], o_recv.at[d - 1], other_core).wait_recv()

    def own_z(a, way):
        to = on_cand(y * NZL + (z + 1 if way == 0 else z - 1))
        return remote(kvh.at[z, a], kvh.at[z, a], own_send.at[way, a], kv_recv.at[a, z], to)

    def hop_z(a, z_):
        to = on_cand(y * NZL + z + jnp.where(z_ < z, 1, -1))
        return remote(kvh.at[z_, a], kvh.at[z_, a], z_send.at[a, z_], kv_recv.at[a, z_], to)

    def goes_on(z_):
        return ((z_ < z) & (z < NZL - 1)) | ((z_ > z) & (z > 0))

    def arrived(a, z_):
        here = kvh.at[z_, a]
        remote(here, here, own_send.at[0, 0], kv_recv.at[a, z_], other_core).wait_recv()

    outer = (z <= 1, z >= NZL - 2)
    inner = ((z == NZL - 3) | (z == NZL - 2), (z == 1) | (z == 2))
    wraps = (z == NZL - 1, z == 0)

    def halo_copy(way, a):
        src = (k_hbm, v_hbm, q_hbm, far_out.at[way])[a]
        dst = far_in.at[way] if a == 3 else halo.at[way, a]
        return remote(src, dst, halo_send.at[way, a], halo_recv.at[way, a], on_cand(nxt if way == 0 else prv))

    def near_copies(kinds, when):
        for way in range(2):
            @pl.when(when[way])
            def _():
                for a in kinds:
                    halo_copy(way, a).start()

    plain = [~inner[way] & ~wraps[way] for way in range(2)]

    tile_core = remote(w_hbm, wtmp, wc_send, wc_recv, other_core)

    def tile_z(d):
        zh_, z_ = along_z(d)
        here = wb.at[core, x, y, z]
        return remote(here, here, wz_send.at[d - 1], wz_recv.at[z], dev(x, zh_, core, y, z_))

    def tile_y(d):
        here = wb.at[core, x, y]
        return remote(here, here, wy_send.at[d - 1], wy_recv.at[d - 1], dev(x, zh, core, lax.rem(y + d, NY), z))

    def tile_x(d):
        here = wb.at[core, x]
        return remote(here, here, wx_send.at[d - 1], wx_recv.at[d - 1], dev(lax.rem(x + d, NX), zh, core, y, z))

    def tile_out(d):
        here = wb.at[core, lax.rem(x + d, NX)]
        return remote(here, here, wo_send.at[d], wo_recv.at[d], other_core)

    for i in range(3):
        for d in range(1, NY):
            to_head(i, d).start()
    near_copies([0], wraps)
    near_copies([2], outer)
    tile_core.start()

    for copy in incoming[:3]:
        copy.wait()

    def ids_row(b):
        at = jnp.clip(b, 0, NCAND - 1) * DH
        got = ids_ref[:, pl.ds(pl.multiple_of(at, DH), DH)].astype(F32)
        return jnp.where((b >= 0) & (b < NCAND), got, -1.0)

    square = (rows, rows)
    sub = lax.broadcasted_iota(jnp.int32, square, 0)
    lane = lax.broadcasted_iota(jnp.int32, square, 1)
    half_factor = 0.5 * DH ** (-0.5)

    def make_mask():
        ids = [ids_row(c + d) for d in (-2, -1, 0, 1)]
        wide = [jnp.broadcast_to(r, square) for r in ids]
        tall = [w.T for w in wide]
        offs = []
        for b in (1, 2, 3):
            whole = jnp.where(tall[b - 1] == wide[b], 1.0, 0.0)
            part = jnp.where((tall[b] == wide[b]) & (sub < lane), 1.0, 0.0)
            offs.append(jnp.sum(whole + part, axis=0, keepdims=True))
        allowed = jnp.where(pat_ref[...] == 1, 1.0, 0.0).astype(BF16)

        def of_rows(b):
            off = jnp.broadcast_to(offs[b], square).T
            return dot(jnp.where(off == lane.astype(F32), 1.0, 0.0).astype(BF16), allowed).astype(BF16)

        by_row = [of_rows(b) for b in range(3)]
        hot_keys = [
            jnp.where(sub.astype(F32) == jnp.broadcast_to(offs[b], square), 1.0, 0.0).astype(BF16)
            for b in range(3)
        ]
        for i, (r, b) in enumerate([(1, 0), (1, 1), (1, 2), (0, 1), (2, 1)]):
            seen = dot(by_row[r], hot_keys[b]) > 0.5
            if r == b:
                seen = seen | (sub == lane)
            seen = seen & (tall[r + 1] == wide[b + 1])
            maskh[i] = jnp.where(seen, half_factor, 0.0)

    for copy in incoming[3:5]:
        copy.wait()
    for a in range(2):
        for d in range(1, NY):
            at_head(a, d)

        @pl.when(z < NZL - 1)
        def _():
            own_z(a, 0).start()

        @pl.when(z > 0)
        def _():
            own_z(a, 1).start()

    tile_core.wait()
    mine, theirs = w_ref[...].astype(F32), wtmp[...].astype(F32)
    tile = jnp.where(
        core == 0, jnp.concatenate([mine, theirs], axis=1), jnp.concatenate([theirs, mine], axis=1)
    ).astype(BF16)

    @pl.when(core == zh)
    def _():
        wb[core, x, y, z] = tile
        for d in range(1, NZH * NZL):
            tile_z(d).start()

    make_mask()

    def own_chunk():
        for copy in incoming[6:9]:
            copy.wait()
        for h in range(H):
            cols = slice(h * DH, (h + 1) * DH)
            weights = silu_of_half(dot_t(q_ref[:, cols], k_ref[:, cols]) * maskh[1])
            att[:, cols] = dot(weights, v_ref[:, cols])

    def halo_chunk(side):
        back = 1 - side

        @pl.when(outer[back])
        def _():
            halo_copy(side, 3).wait_recv()
            att[...] = att[...] + far_in[side].astype(F32)

        @pl.when(~outer[back])
        def _():
            for a in range(2):
                halo_copy(side, a).wait_recv()
            for h in range(H):
                cols = slice(h * DH, (h + 1) * DH)
                weights = silu_of_half(dot_t(q_ref[:, cols], halo[side, 0, :, cols]) * maskh[2 * side])
                att[:, cols] = att[:, cols] + dot(weights, halo[side, 1, :, cols])

    def far_chunk(side):
        back = 1 - side

        @pl.when(inner[back])
        def _():
            halo_copy(side, 2).wait_recv()
            for h in range(H):
                cols = slice(h * DH, (h + 1) * DH)
                weights = silu_of_half(dot_t(halo[side, 2, :, cols], k_ref[:, cols]) * maskh[3 + side])
                far_out[back, :, cols] = dot(weights, v_ref[:, cols]).astype(BF16)
            halo_copy(back, 3).start()

    def hist_chunk(t):
        z_ = z_of(t)
        if t == 0:
            incoming[5].wait()
            for d in range(1, NY):
                at_head(2, d)
        for h in range(HEADS):
            cols = slice(h * DH, (h + 1) * DH)
            keys = kvh[z_, 0, :, :, cols].reshape(-1, DH)
            values = kvh[z_, 1, :, :, cols].reshape(-1, DH)
            weights = silu_of_half(dot_t(qh[:, :, cols].reshape(-1, DH), keys) * half_factor)
            more = dot(weights, values)
            oh[h] = more if t == 0 else oh[h] + more

    for t in range(1, NZL):
        z_ = z_of(t)
        for a in range(2):
            arrived(a, z_)

            @pl.when(goes_on(z_))
            def _():
                hop_z(a, z_).start()

        if t == 1:
            near_copies([0], plain)
            own_chunk()
        if t == 2:
            near_copies([1], wraps)
            for side in range(2):
                far_chunk(side)
        if t == 3:
            near_copies([1], plain)
        if t == 2:
            for z_ in range(NZL):
                @pl.when((core != zh) | (z != z_))
                def _():
                    there = wb.at[core, x, y, z_]
                    remote(there, there, wz_send.at[0], wz_recv.at[z_], other_core).wait_recv()
            for d in range(1, NY):
                tile_y(d).start()
        if t == 4:
            for d in range(1, NY):
                there = wb.at[core, x, lax.rem(y + NY - d, NY)]
                remote(there, there, wy_send.at[0], wy_recv.at[d - 1], other_core).wait_recv()
            for d in range(1, NX):
                tile_x(d).start()
            tile_out(0).start()
        hist_chunk(t - 1)
    hist_chunk(NZL - 1)
    for y_ in range(NY):
        for h in range(HEADS):
            part_out[y_, :, h * DH:(h + 1) * DH] = oh[h, y_ * rows:(y_ + 1) * rows].astype(BF16)
    for d in range(1, NY):
        from_head(d).start()
    part_in[y] = part_out[y]
    for d in range(1, NX):
        there = wb.at[core, lax.rem(x + NX - d, NX)]
        remote(there, there, wx_send.at[0], wx_recv.at[d - 1], other_core).wait_recv()
        tile_out(NX - d).start()
    halo_chunk(0)
    halo_chunk(1)

    for copy in incoming[9:]:
        copy.wait()
    for d in range(1, NY):
        back_home(d)
    for y_ in range(NY):
        cols = slice(y_ * SHARE, (y_ + 1) * SHARE)
        att[:, cols] = att[:, cols] + part_in[y_].astype(F32)
    attended = att[...]
    center = jnp.mean(attended, axis=1, keepdims=True)
    moved = attended - center
    spread = jnp.mean(moved * moved, axis=1, keepdims=True)
    gated = (moved * lax.rsqrt(spread + 1e-05) * gate_ref[...].astype(F32)).astype(BF16)

    for d in range(NX):
        there = wb.at[1 - core, lax.rem(x + d, NX)]
        remote(there, there, wo_send.at[0], wo_recv.at[d], other_core).wait_recv()
    for x_ in range(NX):
        cols = slice(x_ * 2 * DH, (x_ + 1) * 2 * DH)
        weight = jnp.concatenate(
            [wb[0, x_].reshape(-1, DH), wb[1, x_].reshape(-1, DH)], axis=1
        )
        out_ref[:, cols] = (res_ref[:, cols].astype(F32) + dot(gated, weight)).astype(BF16)

    @pl.when(z < NZL - 1)
    def _():
        for a in range(2):
            own_z(a, 0).wait_send()

    @pl.when(z > 0)
    def _():
        for a in range(2):
            own_z(a, 1).wait_send()

    for t in range(1, NZL):
        z_ = z_of(t)

        @pl.when(goes_on(z_))
        def _():
            for a in range(2):
                hop_z(a, z_).wait_send()

    for d in range(1, NY):
        for i in range(3):
            to_head(i, d).wait_send()
        from_head(d).wait_send()
    for way in range(2):
        for a, sent in enumerate([~inner[way], ~inner[way], outer[way], inner[way]]):
            @pl.when(sent)
            def _():
                halo_copy(way, a).wait_send()

    @pl.when(core == zh)
    def _():
        for d in range(1, NZH * NZL):
            tile_z(d).wait_send()

    for d in range(1, NY):
        tile_y(d).wait_send()
    for d in range(1, NX):
        tile_x(d).wait_send()
    for d in range(NX):
        tile_out(d).wait_send()


def shards(q, k, v, gate, resid, hk, hv, ids, pattern, weight):
    rows, width = q.shape[1:]
    hist = hk.shape[1]
    hbm = pl.BlockSpec(memory_space=pl.ANY)
    vmem = pl.BlockSpec(memory_space=pltpu.VMEM)
    dma = pltpu.SemaphoreType.DMA
    out = pl.pallas_call(
        kernel,
        out_shape=jax.ShapeDtypeStruct((rows, width), BF16),
        in_specs=[hbm] * 10,
        out_specs=vmem,
        scratch_shapes=[
            pltpu.VMEM((5, rows, width), BF16),
            pltpu.VMEM(ids.shape, ids.dtype),
            pltpu.VMEM(pattern.shape, pattern.dtype),
            pltpu.VMEM(weight.shape, BF16),
            pltpu.VMEM((NZL, 2, NY, hist, SHARE), BF16),
            pltpu.VMEM((NY, rows, SHARE), BF16),
            pltpu.VMEM((HEADS, NY * rows, DH), F32),
            pltpu.VMEM((NY, rows, SHARE), BF16),
            pltpu.VMEM((NY, rows, SHARE), BF16),
            pltpu.VMEM((2, 3, rows, width), BF16),
            pltpu.VMEM((2, rows, width), BF16),
            pltpu.VMEM((2, rows, width), BF16),
            pltpu.VMEM(weight.shape, BF16),
            pltpu.VMEM((NZH, NX, NY, NZL, weight.shape[0], 2 * weight.shape[1]), BF16),
            pltpu.VMEM((5, rows, rows), F32),
            pltpu.VMEM((rows, width), F32),
            dma((11,)), dma((2, NZL)), dma((2, 2)), dma((2, NZL)), dma((3, NY - 1)), dma((3, NY - 1)),
            dma((NY - 1,)), dma((NY - 1,)), dma((2, 4)), dma((2, 4)),
            dma, dma, dma((NZH * NZL - 1,)), dma((NZL,)), dma((NY - 1,)), dma((NY - 1,)),
            dma((NX - 1,)), dma((NX - 1,)), dma((NX,)), dma((NX,)),
        ],
        compiler_params=pltpu.CompilerParams(
            collective_id=0, has_side_effects=True, vmem_limit_bytes=60 * 1024 * 1024
        ),
    )(q[0], k[0], v[0], gate[0], resid[0], hk[0], hv[0], ids, pattern, weight)
    return out[None]


def solution(mesh):
    part = P("users", "cand", None)
    return jax.shard_map(
        shards,
        mesh=mesh,
        in_specs=(part,) * 7 + (P("users", None), P(), P("cand", "users")),
        out_specs=part,
        check_vma=False,
    )
```

```python
import jax
import jax.numpy as jnp
from jax import lax
from jax.experimental import pallas as pl
from jax.experimental.pallas import tpu as pltpu
from jax.sharding import PartitionSpec as P

H = 8
DH = 128
NX, NZH, NCORE = 4, 2, 2
NY, NZL = 4, 8
NCAND = NY * NZL
HEADS = H // NY
SHARE = HEADS * DH
MESH = pl.DeviceIdType.MESH
BF16, F32 = jnp.bfloat16, jnp.float32


def dot(a, b):
    return lax.dot_general(a, b, (((1,), (0,)), ((), ())), preferred_element_type=F32)


def dot_t(a, b):
    return lax.dot_general(a, b, (((1,), (1,)), ((), ())), preferred_element_type=F32)


def silu_of_half(h):
    return (h + h * jnp.tanh(h)).astype(BF16)


def kernel(
    q_hbm, k_hbm, v_hbm, gate_hbm, res_hbm, hk_hbm, hv_hbm, ids_hbm, pat_hbm, w_hbm,
    out_ref,
    rows5, ids_ref, pat_ref, w_ref,
    kvh, qh, oh, part_out, part_in, halo, far_out, far_in, wtmp, wb, maskh, att,
    in_sem, kv_recv, own_send, z_send, ys_send, ys_recv, o_send, o_recv, halo_send, halo_recv,
    wc_send, wc_recv, wz_send, wz_recv, wy_send, wy_recv, wx_send, wx_recv, wo_send, wo_recv,
):
    u, c = lax.axis_index("users"), lax.axis_index("cand")
    core = lax.rem(u, NCORE)
    zh = lax.rem(u // NCORE, NZH)
    x = u // (NCORE * NZH)
    z = lax.rem(c, NZL)
    y = c // NZL
    rows = q_hbm.shape[0]
    q_ref, k_ref, v_ref, gate_ref, res_ref = [rows5.at[i] for i in range(5)]

    def share(y_):
        return pl.ds(pl.multiple_of(y_ * SHARE, SHARE), SHARE)

    incoming = [
        pltpu.make_async_copy(src, dst, in_sem.at[i])
        for i, (src, dst) in enumerate([
            (w_hbm, w_ref), (ids_hbm, ids_ref), (pat_hbm, pat_ref),
            (hk_hbm.at[:, share(y)], kvh.at[z, 0, y]), (hv_hbm.at[:, share(y)], kvh.at[z, 1, y]),
            (q_hbm.at[:, share(y)], qh.at[y]),
            (q_hbm, q_ref), (k_hbm, k_ref), (v_hbm, v_ref), (gate_hbm, gate_ref), (res_hbm, res_ref),
        ])
    ]
    for copy in incoming:
        copy.start()

    def dev(x_, zh_, core_, y_, z_):
        return {"users": (x_ * NZH + zh_) * NCORE + core_, "cand": y_ * NZL + z_}

    def on_cand(c_):
        return {"users": u, "cand": c_}

    def along_z(d):
        far = lax.rem(zh * NZL + z + d, NZH * NZL)
        return far // NZL, lax.rem(far, NZL)

    other_core = dev(x, zh, 1 - core, y, z)
    nxt, prv = lax.rem(c + 1, NCAND), lax.rem(c + NCAND - 1, NCAND)

    barrier = pltpu.get_barrier_semaphore()

    def greet(device):
        pl.semaphore_signal(barrier, inc=1, device_id=device, device_id_type=MESH)

    for d in range(1, NZH * NZL):
        zh_, z_ = along_z(d)
        greet(dev(x, zh_, core, y, z_))
    for d in range(1, NY):
        greet(dev(x, zh, core, lax.rem(y + d, NY), z))
    for d in range(1, NX):
        greet(dev(lax.rem(x + d, NX), zh, core, y, z))
    greet(other_core)

    @pl.when(z == NZL - 1)
    def _():
        greet(on_cand(nxt))

    @pl.when(z == 0)
    def _():
        greet(on_cand(prv))

    partners = NZH * NZL - 1 + NY - 1 + NX - 1 + 1
    edge = jnp.where(z == 0, 1, 0) + jnp.where(z == NZL - 1, 1, 0)
    pl.semaphore_wait(barrier, partners + edge)

    def remote(src, dst, send, recv, device):
        return pltpu.make_async_remote_copy(
            src_ref=src, dst_ref=dst, send_sem=send, recv_sem=recv,
            device_id=device, device_id_type=MESH,
        )

    def z_of(t):
        both = 2 * jnp.minimum(z, NZL - 1 - z)
        turn = z - (t + 1) // 2 if t % 2 else z + t // 2
        return jnp.where(t <= both, turn, jnp.where(2 * z < NZL, t, NZL - 1 - t))

    def to_head(i, d):
        y_ = lax.rem(y + d, NY)
        src = (hk_hbm, hv_hbm, q_hbm)[i].at[:, share(y_)]
        dst = qh.at[y] if i == 2 else kvh.at[z, i, y]
        return remote(src, dst, ys_send.at[i, d - 1], ys_recv.at[i, d - 1], on_cand(y_ * NZL + z))

    def at_head(i, d):
        y_ = lax.rem(y + NY - d, NY)
        here = qh.at[y_] if i == 2 else kvh.at[z, i, y_]
        remote(here, here, ys_send.at[0, 0], ys_recv.at[i, d - 1], other_core).wait_recv()

    def from_head(d):
        y_ = lax.rem(y + d, NY)
        return remote(part_out.at[y_], part_in.at[y], o_send.at[d - 1], o_recv.at[d - 1], on_cand(y_ * NZL + z))

    def back_home(d):
        here = part_in.at[lax.rem(y + NY - d, NY)]
        remote(here, here, o_send.at[0], o_recv.at[d - 1], other_core).wait_recv()

    def own_z(a, way):
        to = on_cand(y * NZL + (z + 1 if way == 0 else z - 1))
        return remote(kvh.at[z, a], kvh.at[z, a], own_send.at[way, a], kv_recv.at[a, z], to)

    def hop_z(a, z_):
        to = on_cand(y * NZL + z + jnp.where(z_ < z, 1, -1))
        return remote(kvh.at[z_, a], kvh.at[z_, a], z_send.at[a, z_], kv_recv.at[a, z_], to)

    def goes_on(z_):
        return ((z_ < z) & (z < NZL - 1)) | ((z_ > z) & (z > 0))

    def arrived(a, z_):
        here = kvh.at[z_, a]
        remote(here, here, own_send.at[0, 0], kv_recv.at[a, z_], other_core).wait_recv()

    outer = (z <= 1, z >= NZL - 2)
    inner = ((z == NZL - 3) | (z == NZL - 2), (z == 1) | (z == 2))
    wraps = (z == NZL - 1, z == 0)

    def halo_copy(way, a):
        src = (k_hbm, v_hbm, q_hbm, far_out.at[way])[a]
        dst = far_in.at[way] if a == 3 else halo.at[way, a]
        return remote(src, dst, halo_send.at[way, a], halo_recv.at[way, a], on_cand(nxt if way == 0 else prv))

    def near_copies(kinds, when):
        for way in range(2):
            @pl.when(when[way])
            def _():
                for a in kinds:
                    halo_copy(way, a).start()

    plain = [~inner[way] & ~wraps[way] for way in range(2)]

    tile_core = remote(w_hbm, wtmp, wc_send, wc_recv, other_core)

    def tile_z(d):
        zh_, z_ = along_z(d)
        here = wb.at[core, x, y, z]
        return remote(here, here, wz_send.at[d - 1], wz_recv.at[z], dev(x, zh_, core, y, z_))

    def tile_y(d):
        here = wb.at[core, x, y]
        return remote(here, here, wy_send.at[d - 1], wy_recv.at[d - 1], dev(x, zh, core, lax.rem(y + d, NY), z))

    def tile_x(d):
        here = wb.at[core, x]
        return remote(here, here, wx_send.at[d - 1], wx_recv.at[d - 1], dev(lax.rem(x + d, NX), zh, core, y, z))

    def tile_out(d):
        here = wb.at[core, lax.rem(x + d, NX)]
        return remote(here, here, wo_send.at[d], wo_recv.at[d], other_core)

    for i in range(3):
        for d in range(1, NY):
            to_head(i, d).start()
    near_copies([0], wraps)
    near_copies([2], outer)
    tile_core.start()

    for copy in incoming[:3]:
        copy.wait()

    def ids_row(b):
        at = jnp.clip(b, 0, NCAND - 1) * DH
        got = ids_ref[:, pl.ds(pl.multiple_of(at, DH), DH)].astype(F32)
        return jnp.where((b >= 0) & (b < NCAND), got, -1.0)

    square = (rows, rows)
    sub = lax.broadcasted_iota(jnp.int32, square, 0)
    lane = lax.broadcasted_iota(jnp.int32, square, 1)
    half_factor = 0.5 * DH ** (-0.5)

    def make_mask():
        ids = [ids_row(c + d) for d in (-2, -1, 0, 1)]
        wide = [jnp.broadcast_to(r, square) for r in ids]
        tall = [w.T for w in wide]
        offs = []
        for b in (1, 2, 3):
            whole = jnp.where(tall[b - 1] == wide[b], 1.0, 0.0)
            part = jnp.where((tall[b] == wide[b]) & (sub < lane), 1.0, 0.0)
            offs.append(jnp.sum(whole + part, axis=0, keepdims=True))
        allowed = jnp.where(pat_ref[...] == 1, 1.0, 0.0).astype(BF16)

        def of_rows(b):
            off = jnp.broadcast_to(offs[b], square).T
            return dot(jnp.where(off == lane.astype(F32), 1.0, 0.0).astype(BF16), allowed).astype(BF16)

        by_row = [of_rows(b) for b in range(3)]
        hot_keys = [
            jnp.where(sub.astype(F32) == jnp.broadcast_to(offs[b], square), 1.0, 0.0).astype(BF16)
            for b in range(3)
        ]
        for i, (r, b) in enumerate([(1, 0), (1, 1), (1, 2), (0, 1), (2, 1)]):
            seen = dot(by_row[r], hot_keys[b]) > 0.5
            if r == b:
                seen = seen | (sub == lane)
            seen = seen & (tall[r + 1] == wide[b + 1])
            maskh[i] = jnp.where(seen, half_factor, 0.0)

    for copy in incoming[3:5]:
        copy.wait()
    for a in range(2):
        for d in range(1, NY):
            at_head(a, d)

        @pl.when(z < NZL - 1)
        def _():
            own_z(a, 0).start()

        @pl.when(z > 0)
        def _():
            own_z(a, 1).start()

    tile_core.wait()
    mine, theirs = w_ref[...].astype(F32), wtmp[...].astype(F32)
    tile = jnp.where(
        core == 0, jnp.concatenate([mine, theirs], axis=1), jnp.concatenate([theirs, mine], axis=1)
    ).astype(BF16)

    @pl.when(core == zh)
    def _():
        wb[core, x, y, z] = tile
        for d in range(1, NZH * NZL):
            tile_z(d).start()

    make_mask()

    def own_chunk():
        for copy in incoming[6:9]:
            copy.wait()
        for h in range(H):
            cols = slice(h * DH, (h + 1) * DH)
            weights = silu_of_half(dot_t(q_ref[:, cols], k_ref[:, cols]) * maskh[1])
            att[:, cols] = dot(weights, v_ref[:, cols])

    def halo_chunk(side):
        back = 1 - side

        @pl.when(outer[back])
        def _():
            halo_copy(side, 3).wait_recv()
            att[...] = att[...] + far_in[side].astype(F32)

        @pl.when(~outer[back])
        def _():
            for a in range(2):
                halo_copy(side, a).wait_recv()
            for h in range(H):
                cols = slice(h * DH, (h + 1) * DH)
                weights = silu_of_half(dot_t(q_ref[:, cols], halo[side, 0, :, cols]) * maskh[2 * side])
                att[:, cols] = att[:, cols] + dot(weights, halo[side, 1, :, cols])

    def far_chunk(side):
        back = 1 - side

        @pl.when(inner[back])
        def _():
            halo_copy(side, 2).wait_recv()
            for h in range(H):
                cols = slice(h * DH, (h + 1) * DH)
                weights = silu_of_half(dot_t(halo[side, 2, :, cols], k_ref[:, cols]) * maskh[3 + side])
                far_out[back, :, cols] = dot(weights, v_ref[:, cols]).astype(BF16)
            halo_copy(back, 3).start()

    def hist_chunk(t):
        z_ = z_of(t)
        if t == 0:
            incoming[5].wait()
            for d in range(1, NY):
                at_head(2, d)
        for h in range(HEADS):
            cols = slice(h * DH, (h + 1) * DH)
            keys = kvh[z_, 0, :, :, cols].reshape(-1, DH)
            values = kvh[z_, 1, :, :, cols].reshape(-1, DH)
            weights = silu_of_half(dot_t(qh[:, :, cols].reshape(-1, DH), keys) * half_factor)
            more = dot(weights, values)
            oh[h] = more if t == 0 else oh[h] + more

    for t in range(1, NZL):
        z_ = z_of(t)
        for a in range(2):
            arrived(a, z_)

            @pl.when(goes_on(z_))
            def _():
                hop_z(a, z_).start()

        if t == 1:
            for z_ in range(NZL):
                @pl.when((core != zh) | (z != z_))
                def _():
                    there = wb.at[core, x, y, z_]
                    remote(there, there, wz_send.at[0], wz_recv.at[z_], other_core).wait_recv()
            for d in range(1, NY):
                tile_y(d).start()
        if t == 2:
            for d in range(1, NY):
                there = wb.at[core, x, lax.rem(y + NY - d, NY)]
                remote(there, there, wy_send.at[0], wy_recv.at[d - 1], other_core).wait_recv()
            for d in range(1, NX):
                tile_x(d).start()
            tile_out(0).start()
        if t == 1:
            near_copies([0], plain)
            own_chunk()
        if t == 2:
            near_copies([1], wraps)
            for side in range(2):
                far_chunk(side)
        if t == 3:
            near_copies([1], plain)
        hist_chunk(t - 1)
        if t == 6:
            for d in range(1, NX):
                there = wb.at[core, lax.rem(x + NX - d, NX)]
                remote(there, there, wx_send.at[0], wx_recv.at[d - 1], other_core).wait_recv()
                tile_out(NX - d).start()
    hist_chunk(NZL - 1)
    for y_ in range(NY):
        for h in range(HEADS):
            part_out[y_, :, h * DH:(h + 1) * DH] = oh[h, y_ * rows:(y_ + 1) * rows].astype(BF16)
    for d in range(1, NY):
        from_head(d).start()
    part_in[y] = part_out[y]
    halo_chunk(0)
    halo_chunk(1)

    for copy in incoming[9:]:
        copy.wait()
    for d in range(1, NY):
        back_home(d)
    for y_ in range(NY):
        cols = slice(y_ * SHARE, (y_ + 1) * SHARE)
        att[:, cols] = att[:, cols] + part_in[y_].astype(F32)
    attended = att[...]
    center = jnp.mean(attended, axis=1, keepdims=True)
    moved = attended - center
    spread = jnp.mean(moved * moved, axis=1, keepdims=True)
    gated = (moved * lax.rsqrt(spread + 1e-05) * gate_ref[...].astype(F32)).astype(BF16)

    for d in range(NX):
        there = wb.at[1 - core, lax.rem(x + d, NX)]
        remote(there, there, wo_send.at[0], wo_recv.at[d], other_core).wait_recv()
    for x_ in range(NX):
        cols = slice(x_ * 2 * DH, (x_ + 1) * 2 * DH)
        weight = jnp.concatenate(
            [wb[0, x_].reshape(-1, DH), wb[1, x_].reshape(-1, DH)], axis=1
        )
        out_ref[:, cols] = (res_ref[:, cols].astype(F32) + dot(gated, weight)).astype(BF16)

    @pl.when(z < NZL - 1)
    def _():
        for a in range(2):
            own_z(a, 0).wait_send()

    @pl.when(z > 0)
    def _():
        for a in range(2):
            own_z(a, 1).wait_send()

    for t in range(1, NZL):
        z_ = z_of(t)

        @pl.when(goes_on(z_))
        def _():
            for a in range(2):
                hop_z(a, z_).wait_send()

    for d in range(1, NY):
        for i in range(3):
            to_head(i, d).wait_send()
        from_head(d).wait_send()
    for way in range(2):
        for a, sent in enumerate([~inner[way], ~inner[way], outer[way], inner[way]]):
            @pl.when(sent)
            def _():
                halo_copy(way, a).wait_send()

    @pl.when(core == zh)
    def _():
        for d in range(1, NZH * NZL):
            tile_z(d).wait_send()

    for d in range(1, NY):
        tile_y(d).wait_send()
    for d in range(1, NX):
        tile_x(d).wait_send()
    for d in range(NX):
        tile_out(d).wait_send()


def shards(q, k, v, gate, resid, hk, hv, ids, pattern, weight):
    rows, width = q.shape[1:]
    hist = hk.shape[1]
    hbm = pl.BlockSpec(memory_space=pl.ANY)
    vmem = pl.BlockSpec(memory_space=pltpu.VMEM)
    dma = pltpu.SemaphoreType.DMA
    out = pl.pallas_call(
        kernel,
        out_shape=jax.ShapeDtypeStruct((rows, width), BF16),
        in_specs=[hbm] * 10,
        out_specs=vmem,
        scratch_shapes=[
            pltpu.VMEM((5, rows, width), BF16),
            pltpu.VMEM(ids.shape, ids.dtype),
            pltpu.VMEM(pattern.shape, pattern.dtype),
            pltpu.VMEM(weight.shape, BF16),
            pltpu.VMEM((NZL, 2, NY, hist, SHARE), BF16),
            pltpu.VMEM((NY, rows, SHARE), BF16),
            pltpu.VMEM((HEADS, NY * rows, DH), F32),
            pltpu.VMEM((NY, rows, SHARE), BF16),
            pltpu.VMEM((NY, rows, SHARE), BF16),
            pltpu.VMEM((2, 3, rows, width), BF16),
            pltpu.VMEM((2, rows, width), BF16),
            pltpu.VMEM((2, rows, width), BF16),
            pltpu.VMEM(weight.shape, BF16),
            pltpu.VMEM((NZH, NX, NY, NZL, weight.shape[0], 2 * weight.shape[1]), BF16),
            pltpu.VMEM((5, rows, rows), F32),
            pltpu.VMEM((rows, width), F32),
            dma((11,)), dma((2, NZL)), dma((2, 2)), dma((2, NZL)), dma((3, NY - 1)), dma((3, NY - 1)),
            dma((NY - 1,)), dma((NY - 1,)), dma((2, 4)), dma((2, 4)),
            dma, dma, dma((NZH * NZL - 1,)), dma((NZL,)), dma((NY - 1,)), dma((NY - 1,)),
            dma((NX - 1,)), dma((NX - 1,)), dma((NX,)), dma((NX,)),
        ],
        compiler_params=pltpu.CompilerParams(
            collective_id=0, has_side_effects=True, vmem_limit_bytes=60 * 1024 * 1024
        ),
    )(q[0], k[0], v[0], gate[0], resid[0], hk[0], hv[0], ids, pattern, weight)
    return out[None]


def solution(mesh):
    part = P("users", "cand", None)
    return jax.shard_map(
        shards,
        mesh=mesh,
        in_specs=(part,) * 7 + (P("users", None), P(), P("cand", "users")),
        out_specs=part,
        check_vma=False,
    )
```

```python
import jax
import jax.numpy as jnp
from jax import lax
from jax.experimental import pallas as pl
from jax.experimental.pallas import tpu as pltpu
from jax.sharding import PartitionSpec as P

H = 8
DH = 128
NX, NZH, NCORE = 4, 2, 2
NY, NZL = 4, 8
NCAND = NY * NZL
HEADS = H // NY
SHARE = HEADS * DH
MESH = pl.DeviceIdType.MESH
BF16, F32 = jnp.bfloat16, jnp.float32


def dot(a, b):
    return lax.dot_general(a, b, (((1,), (0,)), ((), ())), preferred_element_type=F32)


def dot_t(a, b):
    return lax.dot_general(a, b, (((1,), (1,)), ((), ())), preferred_element_type=F32)


def silu_of_half(h):
    return (h + h * jnp.tanh(h)).astype(BF16)


def kernel(
    q_hbm, k_hbm, v_hbm, gate_hbm, res_hbm, hk_hbm, hv_hbm, ids_hbm, pat_hbm, w_hbm,
    out_ref,
    rows5, ids_ref, pat_ref, w_ref,
    kvh, qh, oh, part_out, part_in, halo, far_out, far_in, wtmp, wb, maskh, att,
    in_sem, kv_recv, own_send, z_send, ys_send, ys_recv, o_send, o_recv, halo_send, halo_recv,
    wc_send, wc_recv, wz_send, wz_recv, wy_send, wy_recv, wx_send, wx_recv, wo_send, wo_recv,
):
    u, c = lax.axis_index("users"), lax.axis_index("cand")
    core = lax.rem(u, NCORE)
    zh = lax.rem(u // NCORE, NZH)
    x = u // (NCORE * NZH)
    z = lax.rem(c, NZL)
    y = c // NZL
    rows = q_hbm.shape[0]
    q_ref, k_ref, v_ref, gate_ref, res_ref = [rows5.at[i] for i in range(5)]

    def share(y_):
        return pl.ds(pl.multiple_of(y_ * SHARE, SHARE), SHARE)

    incoming = [
        pltpu.make_async_copy(src, dst, in_sem.at[i])
        for i, (src, dst) in enumerate([
            (w_hbm, w_ref), (ids_hbm, ids_ref), (pat_hbm, pat_ref),
            (hk_hbm.at[:, share(y)], kvh.at[z, 0, y]), (hv_hbm.at[:, share(y)], kvh.at[z, 1, y]),
            (q_hbm.at[:, share(y)], qh.at[y]),
            (q_hbm, q_ref), (k_hbm, k_ref), (v_hbm, v_ref), (gate_hbm, gate_ref), (res_hbm, res_ref),
        ])
    ]
    for copy in incoming:
        copy.start()

    def dev(x_, zh_, core_, y_, z_):
        return {"users": (x_ * NZH + zh_) * NCORE + core_, "cand": y_ * NZL + z_}

    def on_cand(c_):
        return {"users": u, "cand": c_}

    def along_z(d):
        far = lax.rem(zh * NZL + z + d, NZH * NZL)
        return far // NZL, lax.rem(far, NZL)

    other_core = dev(x, zh, 1 - core, y, z)
    nxt, prv = lax.rem(c + 1, NCAND), lax.rem(c + NCAND - 1, NCAND)

    barrier = pltpu.get_barrier_semaphore()

    def greet(device):
        pl.semaphore_signal(barrier, inc=1, device_id=device, device_id_type=MESH)

    for d in range(1, NZH * NZL):
        zh_, z_ = along_z(d)
        greet(dev(x, zh_, core, y, z_))
    for d in range(1, NY):
        greet(dev(x, zh, core, lax.rem(y + d, NY), z))
    for d in range(1, NX):
        greet(dev(lax.rem(x + d, NX), zh, core, y, z))
    greet(other_core)

    @pl.when(z == NZL - 1)
    def _():
        greet(on_cand(nxt))

    @pl.when(z == 0)
    def _():
        greet(on_cand(prv))

    partners = NZH * NZL - 1 + NY - 1 + NX - 1 + 1
    edge = jnp.where(z == 0, 1, 0) + jnp.where(z == NZL - 1, 1, 0)
    pl.semaphore_wait(barrier, partners + edge)

    def remote(src, dst, send, recv, device):
        return pltpu.make_async_remote_copy(
            src_ref=src, dst_ref=dst, send_sem=send, recv_sem=recv,
            device_id=device, device_id_type=MESH,
        )

    def z_of(t):
        both = 2 * jnp.minimum(z, NZL - 1 - z)
        turn = z - (t + 1) // 2 if t % 2 else z + t // 2
        return jnp.where(t <= both, turn, jnp.where(2 * z < NZL, t, NZL - 1 - t))

    def to_head(i, d):
        y_ = lax.rem(y + d, NY)
        src = (hk_hbm, hv_hbm, q_hbm)[i].at[:, share(y_)]
        dst = qh.at[y] if i == 2 else kvh.at[z, i, y]
        return remote(src, dst, ys_send.at[i, d - 1], ys_recv.at[i, d - 1], on_cand(y_ * NZL + z))

    def at_head(i, d):
        y_ = lax.rem(y + NY - d, NY)
        here = qh.at[y_] if i == 2 else kvh.at[z, i, y_]
        remote(here, here, ys_send.at[0, 0], ys_recv.at[i, d - 1], other_core).wait_recv()

    def from_head(d):
        y_ = lax.rem(y + d, NY)
        return remote(part_out.at[y_], part_in.at[y], o_send.at[d - 1], o_recv.at[d - 1], on_cand(y_ * NZL + z))

    def back_home(d):
        here = part_in.at[lax.rem(y + NY - d, NY)]
        remote(here, here, o_send.at[0], o_recv.at[d - 1], other_core).wait_recv()

    def own_z(a, way):
        to = on_cand(y * NZL + (z + 1 if way == 0 else z - 1))
        return remote(kvh.at[z, a], kvh.at[z, a], own_send.at[way, a], kv_recv.at[a, z], to)

    def hop_z(a, z_):
        to = on_cand(y * NZL + z + jnp.where(z_ < z, 1, -1))
        return remote(kvh.at[z_, a], kvh.at[z_, a], z_send.at[a, z_], kv_recv.at[a, z_], to)

    def goes_on(z_):
        return ((z_ < z) & (z < NZL - 1)) | ((z_ > z) & (z > 0))

    def arrived(a, z_):
        here = kvh.at[z_, a]
        remote(here, here, own_send.at[0, 0], kv_recv.at[a, z_], other_core).wait_recv()

    outer = (z <= 1, z >= NZL - 2)
    inner = ((z == NZL - 3) | (z == NZL - 2), (z == 1) | (z == 2))
    wraps = (z == NZL - 1, z == 0)

    def halo_copy(way, a):
        src = (k_hbm, v_hbm, q_hbm, far_out.at[way])[a]
        dst = far_in.at[way] if a == 3 else halo.at[way, a]
        return remote(src, dst, halo_send.at[way, a], halo_recv.at[way, a], on_cand(nxt if way == 0 else prv))

    def near_copies(kinds, when):
        for way in range(2):
            @pl.when(when[way])
            def _():
                for a in kinds:
                    halo_copy(way, a).start()

    plain = [~inner[way] & ~wraps[way] for way in range(2)]

    tile_core = remote(w_hbm, wtmp, wc_send, wc_recv, other_core)

    def tile_z(d):
        zh_, z_ = along_z(d)
        here = wb.at[core, x, y, z]
        return remote(here, here, wz_send.at[d - 1], wz_recv.at[z], dev(x, zh_, core, y, z_))

    def tile_y(d):
        here = wb.at[core, x, y]
        return remote(here, here, wy_send.at[d - 1], wy_recv.at[d - 1], dev(x, zh, core, lax.rem(y + d, NY), z))

    def tile_x(d):
        here = wb.at[core, x]
        return remote(here, here, wx_send.at[d - 1], wx_recv.at[d - 1], dev(lax.rem(x + d, NX), zh, core, y, z))

    def tile_out(d):
        here = wb.at[core, lax.rem(x + d, NX)]
        return remote(here, here, wo_send.at[d], wo_recv.at[d], other_core)

    tile_core.start()
    for i in range(3):
        for d in range(1, NY):
            to_head(i, d).start()

    for copy in incoming[:3]:
        copy.wait()

    def ids_row(b):
        at = jnp.clip(b, 0, NCAND - 1) * DH
        got = ids_ref[:, pl.ds(pl.multiple_of(at, DH), DH)].astype(F32)
        return jnp.where((b >= 0) & (b < NCAND), got, -1.0)

    square = (rows, rows)
    sub = lax.broadcasted_iota(jnp.int32, square, 0)
    lane = lax.broadcasted_iota(jnp.int32, square, 1)
    half_factor = 0.5 * DH ** (-0.5)

    def make_mask():
        ids = [ids_row(c + d) for d in (-2, -1, 0, 1)]
        wide = [jnp.broadcast_to(r, square) for r in ids]
        tall = [w.T for w in wide]
        offs = []
        for b in (1, 2, 3):
            whole = jnp.where(tall[b - 1] == wide[b], 1.0, 0.0)
            part = jnp.where((tall[b] == wide[b]) & (sub < lane), 1.0, 0.0)
            offs.append(jnp.sum(whole + part, axis=0, keepdims=True))
        allowed = jnp.where(pat_ref[...] == 1, 1.0, 0.0).astype(BF16)

        def of_rows(b):
            off = jnp.broadcast_to(offs[b], square).T
            return dot(jnp.where(off == lane.astype(F32), 1.0, 0.0).astype(BF16), allowed).astype(BF16)

        by_row = [of_rows(b) for b in range(3)]
        hot_keys = [
            jnp.where(sub.astype(F32) == jnp.broadcast_to(offs[b], square), 1.0, 0.0).astype(BF16)
            for b in range(3)
        ]
        for i, (r, b) in enumerate([(1, 0), (1, 1), (1, 2), (0, 1), (2, 1)]):
            seen = dot(by_row[r], hot_keys[b]) > 0.5
            if r == b:
                seen = seen | (sub == lane)
            seen = seen & (tall[r + 1] == wide[b + 1])
            maskh[i] = jnp.where(seen, half_factor, 0.0)

    tile_core.wait()
    mine, theirs = w_ref[...].astype(F32), wtmp[...].astype(F32)
    tile = jnp.where(
        core == 0, jnp.concatenate([mine, theirs], axis=1), jnp.concatenate([theirs, mine], axis=1)
    ).astype(BF16)

    @pl.when(core == zh)
    def _():
        wb[core, x, y, z] = tile
        for d in range(1, NZH * NZL):
            tile_z(d).start()

    for copy in incoming[3:5]:
        copy.wait()
    for a in range(2):
        for d in range(1, NY):
            at_head(a, d)

        @pl.when(z < NZL - 1)
        def _():
            own_z(a, 0).start()

        @pl.when(z > 0)
        def _():
            own_z(a, 1).start()

    near_copies([0], wraps)
    near_copies([2], outer)
    make_mask()

    def own_chunk():
        for copy in incoming[6:9]:
            copy.wait()
        for h in range(H):
            cols = slice(h * DH, (h + 1) * DH)
            weights = silu_of_half(dot_t(q_ref[:, cols], k_ref[:, cols]) * maskh[1])
            att[:, cols] = dot(weights, v_ref[:, cols])

    def halo_chunk(side):
        back = 1 - side

        @pl.when(outer[back])
        def _():
            halo_copy(side, 3).wait_recv()
            att[...] = att[...] + far_in[side].astype(F32)

        @pl.when(~outer[back])
        def _():
            for a in range(2):
                halo_copy(side, a).wait_recv()
            for h in range(H):
                cols = slice(h * DH, (h + 1) * DH)
                weights = silu_of_half(dot_t(q_ref[:, cols], halo[side, 0, :, cols]) * maskh[2 * side])
                att[:, cols] = att[:, cols] + dot(weights, halo[side, 1, :, cols])

    def far_chunk(side):
        back = 1 - side

        @pl.when(inner[back])
        def _():
            halo_copy(side, 2).wait_recv()
            for h in range(H):
                cols = slice(h * DH, (h + 1) * DH)
                weights = silu_of_half(dot_t(halo[side, 2, :, cols], k_ref[:, cols]) * maskh[3 + side])
                far_out[back, :, cols] = dot(weights, v_ref[:, cols]).astype(BF16)
            halo_copy(back, 3).start()

    def hist_chunk(t):
        z_ = z_of(t)
        if t == 0:
            incoming[5].wait()
            for d in range(1, NY):
                at_head(2, d)
        for h in range(HEADS):
            cols = slice(h * DH, (h + 1) * DH)
            keys = kvh[z_, 0, :, :, cols].reshape(-1, DH)
            values = kvh[z_, 1, :, :, cols].reshape(-1, DH)
            weights = silu_of_half(dot_t(qh[:, :, cols].reshape(-1, DH), keys) * half_factor)
            more = dot(weights, values)
            oh[h] = more if t == 0 else oh[h] + more

    for t in range(1, NZL):
        z_ = z_of(t)
        for a in range(2):
            arrived(a, z_)

            @pl.when(goes_on(z_))
            def _():
                hop_z(a, z_).start()

        if t == 1:
            near_copies([0], plain)
            own_chunk()
        if t == 2:
            near_copies([1], wraps)
        if t == 3:
            near_copies([1], plain)
        if t == 4:
            for side in range(2):
                far_chunk(side)
        if t == 2:
            for z_ in range(NZL):
                @pl.when((core != zh) | (z != z_))
                def _():
                    there = wb.at[core, x, y, z_]
                    remote(there, there, wz_send.at[0], wz_recv.at[z_], other_core).wait_recv()
            for d in range(1, NY):
                tile_y(d).start()
        if t == 3:
            for d in range(1, NY):
                there = wb.at[core, x, lax.rem(y + NY - d, NY)]
                remote(there, there, wy_send.at[0], wy_recv.at[d - 1], other_core).wait_recv()
            for d in range(1, NX):
                tile_x(d).start()
            tile_out(0).start()
        hist_chunk(t - 1)
    hist_chunk(NZL - 1)
    for y_ in range(NY):
        for h in range(HEADS):
            part_out[y_, :, h * DH:(h + 1) * DH] = oh[h, y_ * rows:(y_ + 1) * rows].astype(BF16)
    for d in range(1, NY):
        from_head(d).start()
    part_in[y] = part_out[y]
    for d in range(1, NX):
        there = wb.at[core, lax.rem(x + NX - d, NX)]
        remote(there, there, wx_send.at[0], wx_recv.at[d - 1], other_core).wait_recv()
        tile_out(NX - d).start()
    halo_chunk(0)
    halo_chunk(1)

    for copy in incoming[9:]:
        copy.wait()
    for d in range(1, NY):
        back_home(d)
    for y_ in range(NY):
        cols = slice(y_ * SHARE, (y_ + 1) * SHARE)
        att[:, cols] = att[:, cols] + part_in[y_].astype(F32)
    attended = att[...]
    center = jnp.mean(attended, axis=1, keepdims=True)
    moved = attended - center
    spread = jnp.mean(moved * moved, axis=1, keepdims=True)
    gated = (moved * lax.rsqrt(spread + 1e-05) * gate_ref[...].astype(F32)).astype(BF16)

    for d in range(NX):
        there = wb.at[1 - core, lax.rem(x + d, NX)]
        remote(there, there, wo_send.at[0], wo_recv.at[d], other_core).wait_recv()
    for x_ in range(NX):
        cols = slice(x_ * 2 * DH, (x_ + 1) * 2 * DH)
        weight = jnp.concatenate(
            [wb[0, x_].reshape(-1, DH), wb[1, x_].reshape(-1, DH)], axis=1
        )
        out_ref[:, cols] = (res_ref[:, cols].astype(F32) + dot(gated, weight)).astype(BF16)

    @pl.when(z < NZL - 1)
    def _():
        for a in range(2):
            own_z(a, 0).wait_send()

    @pl.when(z > 0)
    def _():
        for a in range(2):
            own_z(a, 1).wait_send()

    for t in range(1, NZL):
        z_ = z_of(t)

        @pl.when(goes_on(z_))
        def _():
            for a in range(2):
                hop_z(a, z_).wait_send()

    for d in range(1, NY):
        for i in range(3):
            to_head(i, d).wait_send()
        from_head(d).wait_send()
    for way in range(2):
        for a, sent in enumerate([~inner[way], ~inner[way], outer[way], inner[way]]):
            @pl.when(sent)
            def _():
                halo_copy(way, a).wait_send()

    @pl.when(core == zh)
    def _():
        for d in range(1, NZH * NZL):
            tile_z(d).wait_send()

    for d in range(1, NY):
        tile_y(d).wait_send()
    for d in range(1, NX):
        tile_x(d).wait_send()
    for d in range(NX):
        tile_out(d).wait_send()


def shards(q, k, v, gate, resid, hk, hv, ids, pattern, weight):
    rows, width = q.shape[1:]
    hist = hk.shape[1]
    hbm = pl.BlockSpec(memory_space=pl.ANY)
    vmem = pl.BlockSpec(memory_space=pltpu.VMEM)
    dma = pltpu.SemaphoreType.DMA
    out = pl.pallas_call(
        kernel,
        out_shape=jax.ShapeDtypeStruct((rows, width), BF16),
        in_specs=[hbm] * 10,
        out_specs=vmem,
        scratch_shapes=[
            pltpu.VMEM((5, rows, width), BF16),
            pltpu.VMEM(ids.shape, ids.dtype),
            pltpu.VMEM(pattern.shape, pattern.dtype),
            pltpu.VMEM(weight.shape, BF16),
            pltpu.VMEM((NZL, 2, NY, hist, SHARE), BF16),
            pltpu.VMEM((NY, rows, SHARE), BF16),
            pltpu.VMEM((HEADS, NY * rows, DH), F32),
            pltpu.VMEM((NY, rows, SHARE), BF16),
            pltpu.VMEM((NY, rows, SHARE), BF16),
            pltpu.VMEM((2, 3, rows, width), BF16),
            pltpu.VMEM((2, rows, width), BF16),
            pltpu.VMEM((2, rows, width), BF16),
            pltpu.VMEM(weight.shape, BF16),
            pltpu.VMEM((NZH, NX, NY, NZL, weight.shape[0], 2 * weight.shape[1]), BF16),
            pltpu.VMEM((5, rows, rows), F32),
            pltpu.VMEM((rows, width), F32),
            dma((11,)), dma((2, NZL)), dma((2, 2)), dma((2, NZL)), dma((3, NY - 1)), dma((3, NY - 1)),
            dma((NY - 1,)), dma((NY - 1,)), dma((2, 4)), dma((2, 4)),
            dma, dma, dma((NZH * NZL - 1,)), dma((NZL,)), dma((NY - 1,)), dma((NY - 1,)),
            dma((NX - 1,)), dma((NX - 1,)), dma((NX,)), dma((NX,)),
        ],
        compiler_params=pltpu.CompilerParams(
            collective_id=0, has_side_effects=True, vmem_limit_bytes=60 * 1024 * 1024
        ),
    )(q[0], k[0], v[0], gate[0], resid[0], hk[0], hv[0], ids, pattern, weight)
    return out[None]


def solution(mesh):
    part = P("users", "cand", None)
    return jax.shard_map(
        shards,
        mesh=mesh,
        in_specs=(part,) * 7 + (P("users", None), P(), P("cand", "users")),
        out_specs=part,
        check_vma=False,
    )
```

```python
import jax
import jax.numpy as jnp
from jax import lax
from jax.experimental import pallas as pl
from jax.experimental.pallas import tpu as pltpu
from jax.sharding import PartitionSpec as P

H = 8
DH = 128
NX, NZH, NCORE = 4, 2, 2
NY, NZL = 4, 8
NCAND = NY * NZL
HEADS = H // NY
SHARE = HEADS * DH
MESH = pl.DeviceIdType.MESH
BF16, F32 = jnp.bfloat16, jnp.float32


def dot(a, b):
    return lax.dot_general(a, b, (((1,), (0,)), ((), ())), preferred_element_type=F32)


def dot_t(a, b):
    return lax.dot_general(a, b, (((1,), (1,)), ((), ())), preferred_element_type=F32)


def silu_of_half(h):
    return (h + h * jnp.tanh(h)).astype(BF16)


def kernel(
    q_hbm, k_hbm, v_hbm, gate_hbm, res_hbm, hk_hbm, hv_hbm, ids_hbm, pat_hbm, w_hbm,
    out_ref,
    rows5, ids_ref, pat_ref, w_ref,
    kvh, qh, oh, part_out, part_in, halo, wtmp, wb, maskh, att,
    in_sem, kv_recv, own_send, z_send, ys_send, ys_recv, o_send, o_recv, halo_send, halo_recv,
    wc_send, wc_recv, wz_send, wz_recv, wy_send, wy_recv, wx_send, wx_recv, wo_send, wo_recv,
):
    u, c = lax.axis_index("users"), lax.axis_index("cand")
    core = lax.rem(u, NCORE)
    zh = lax.rem(u // NCORE, NZH)
    x = u // (NCORE * NZH)
    z = lax.rem(c, NZL)
    y = c // NZL
    rows = q_hbm.shape[0]
    q_ref, k_ref, v_ref, gate_ref, res_ref = [rows5.at[i] for i in range(5)]

    def share(y_):
        return pl.ds(pl.multiple_of(y_ * SHARE, SHARE), SHARE)

    incoming = [
        pltpu.make_async_copy(src, dst, in_sem.at[i])
        for i, (src, dst) in enumerate([
            (w_hbm, w_ref), (ids_hbm, ids_ref), (pat_hbm, pat_ref),
            (hk_hbm.at[:, share(y)], kvh.at[z, 0, y]), (hv_hbm.at[:, share(y)], kvh.at[z, 1, y]),
            (q_hbm.at[:, share(y)], qh.at[y]),
            (q_hbm, q_ref), (k_hbm, k_ref), (v_hbm, v_ref), (gate_hbm, gate_ref), (res_hbm, res_ref),
        ])
    ]
    for copy in incoming:
        copy.start()

    def dev(x_, zh_, core_, y_, z_):
        return {"users": (x_ * NZH + zh_) * NCORE + core_, "cand": y_ * NZL + z_}

    def on_cand(c_):
        return {"users": u, "cand": c_}

    def along_z(d):
        far = lax.rem(zh * NZL + z + d, NZH * NZL)
        return far // NZL, lax.rem(far, NZL)

    other_core = dev(x, zh, 1 - core, y, z)
    nxt, prv = lax.rem(c + 1, NCAND), lax.rem(c + NCAND - 1, NCAND)

    barrier = pltpu.get_barrier_semaphore()

    def greet(device):
        pl.semaphore_signal(barrier, inc=1, device_id=device, device_id_type=MESH)

    for d in range(1, NZH * NZL):
        zh_, z_ = along_z(d)
        greet(dev(x, zh_, core, y, z_))
    for d in range(1, NY):
        greet(dev(x, zh, core, lax.rem(y + d, NY), z))
    for d in range(1, NX):
        greet(dev(lax.rem(x + d, NX), zh, core, y, z))
    greet(other_core)

    @pl.when(z == NZL - 1)
    def _():
        greet(on_cand(nxt))

    @pl.when(z == 0)
    def _():
        greet(on_cand(prv))

    partners = NZH * NZL - 1 + NY - 1 + NX - 1 + 1
    edge = jnp.where(z == 0, 1, 0) + jnp.where(z == NZL - 1, 1, 0)
    pl.semaphore_wait(barrier, partners + edge)

    def remote(src, dst, send, recv, device):
        return pltpu.make_async_remote_copy(
            src_ref=src, dst_ref=dst, send_sem=send, recv_sem=recv,
            device_id=device, device_id_type=MESH,
        )

    def z_of(t):
        both = 2 * jnp.minimum(z, NZL - 1 - z)
        turn = z - (t + 1) // 2 if t % 2 else z + t // 2
        return jnp.where(t <= both, turn, jnp.where(2 * z < NZL, t, NZL - 1 - t))

    def to_head(i, d):
        y_ = lax.rem(y + d, NY)
        src = (hk_hbm, hv_hbm, q_hbm)[i].at[:, share(y_)]
        dst = qh.at[y] if i == 2 else kvh.at[z, i, y]
        return remote(src, dst, ys_send.at[i, d - 1], ys_recv.at[i, d - 1], on_cand(y_ * NZL + z))

    def at_head(i, d):
        y_ = lax.rem(y + NY - d, NY)
        here = qh.at[y_] if i == 2 else kvh.at[z, i, y_]
        remote(here, here, ys_send.at[0, 0], ys_recv.at[i, d - 1], other_core).wait_recv()

    def from_head(d):
        y_ = lax.rem(y + d, NY)
        return remote(part_out.at[y_], part_in.at[y], o_send.at[d - 1], o_recv.at[d - 1], on_cand(y_ * NZL + z))

    def back_home(d):
        here = part_in.at[lax.rem(y + NY - d, NY)]
        remote(here, here, o_send.at[0], o_recv.at[d - 1], other_core).wait_recv()

    def own_z(a, way):
        to = on_cand(y * NZL + (z + 1 if way == 0 else z - 1))
        return remote(kvh.at[z, a], kvh.at[z, a], own_send.at[way, a], kv_recv.at[a, z], to)

    def hop_z(a, z_):
        to = on_cand(y * NZL + z + jnp.where(z_ < z, 1, -1))
        return remote(kvh.at[z_, a], kvh.at[z_, a], z_send.at[a, z_], kv_recv.at[a, z_], to)

    def goes_on(z_):
        return ((z_ < z) & (z < NZL - 1)) | ((z_ > z) & (z > 0))

    def arrived(a, z_):
        here = kvh.at[z_, a]
        remote(here, here, own_send.at[0, 0], kv_recv.at[a, z_], other_core).wait_recv()

    def halo_copy(way, a):
        return remote(
            (k_hbm, v_hbm)[a], halo.at[way, a], halo_send.at[way, a], halo_recv.at[way, a],
            on_cand(nxt if way == 0 else prv),
        )

    tile_core = remote(w_hbm, wtmp, wc_send, wc_recv, other_core)

    def tile_z(d):
        zh_, z_ = along_z(d)
        here = wb.at[core, x, y, z]
        return remote(here, here, wz_send.at[d - 1], wz_recv.at[z], dev(x, zh_, core, y, z_))

    def tile_y(d):
        here = wb.at[core, x, y]
        return remote(here, here, wy_send.at[d - 1], wy_recv.at[d - 1], dev(x, zh, core, lax.rem(y + d, NY), z))

    def tile_x(d):
        here = wb.at[core, x]
        return remote(here, here, wx_send.at[d - 1], wx_recv.at[d - 1], dev(lax.rem(x + d, NX), zh, core, y, z))

    def tile_out(d):
        here = wb.at[core, lax.rem(x + d, NX)]
        return remote(here, here, wo_send.at[d], wo_recv.at[d], other_core)

    for i in range(3):
        for d in range(1, NY):
            to_head(i, d).start()
    halo_copy(0, 0).start()
    tile_core.start()

    for copy in incoming[:3]:
        copy.wait()

    def ids_row(b):
        at = jnp.clip(b, 0, NCAND - 1) * DH
        got = ids_ref[:, pl.ds(pl.multiple_of(at, DH), DH)].astype(F32)
        return jnp.where((b >= 0) & (b < NCAND), got, -1.0)

    square = (rows, rows)
    sub = lax.broadcasted_iota(jnp.int32, square, 0)
    lane = lax.broadcasted_iota(jnp.int32, square, 1)
    half_factor = 0.5 * DH ** (-0.5)

    def make_mask():
        ids = [ids_row(c + d) for d in (-2, -1, 0, 1)]
        wide = [jnp.broadcast_to(r, square) for r in ids]
        tall = [w.T for w in wide]
        offs = []
        for b in (1, 2, 3):
            whole = jnp.where(tall[b - 1] == wide[b], 1.0, 0.0)
            part = jnp.where((tall[b] == wide[b]) & (sub < lane), 1.0, 0.0)
            offs.append(jnp.sum(whole + part, axis=0, keepdims=True))
        own_off = jnp.broadcast_to(offs[1], square).T
        hot_rows = jnp.where(own_off == lane.astype(F32), 1.0, 0.0).astype(BF16)
        allowed = jnp.where(pat_ref[...] == 1, 1.0, 0.0).astype(BF16)
        by_row = dot(hot_rows, allowed).astype(BF16)
        for b in range(3):
            hot_keys = jnp.where(sub.astype(F32) == jnp.broadcast_to(offs[b], square), 1.0, 0.0).astype(BF16)
            seen = dot(by_row, hot_keys) > 0.5
            if b == 1:
                seen = seen | (sub == lane)
            seen = seen & (tall[2] == wide[b + 1])
            maskh[b] = jnp.where(seen, half_factor, 0.0)

    for copy in incoming[3:5]:
        copy.wait()
    for a in range(2):
        for d in range(1, NY):
            at_head(a, d)

        @pl.when(z < NZL - 1)
        def _():
            own_z(a, 0).start()

        @pl.when(z > 0)
        def _():
            own_z(a, 1).start()

    tile_core.wait()
    mine, theirs = w_ref[...].astype(F32), wtmp[...].astype(F32)
    tile = jnp.where(
        core == 0, jnp.concatenate([mine, theirs], axis=1), jnp.concatenate([theirs, mine], axis=1)
    ).astype(BF16)

    @pl.when(core == zh)
    def _():
        wb[core, x, y, z] = tile
        for d in range(1, NZH * NZL):
            tile_z(d).start()

    make_mask()

    def own_head(h):
        if h == 0:
            for copy in incoming[6:9]:
                copy.wait()
        cols = slice(h * DH, (h + 1) * DH)
        weights = silu_of_half(dot_t(q_ref[:, cols], k_ref[:, cols]) * maskh[1])
        att[:, cols] = dot(weights, v_ref[:, cols])

    def halo_chunk(way):
        for a in range(2):
            halo_copy(way, a).wait_recv()
        for h in range(H):
            cols = slice(h * DH, (h + 1) * DH)
            weights = silu_of_half(dot_t(q_ref[:, cols], halo[way, 0, :, cols]) * maskh[2 * way])
            att[:, cols] = att[:, cols] + dot(weights, halo[way, 1, :, cols])

    def hist_head(t, h):
        z_ = z_of(t)
        if t == 0 and h == 0:
            incoming[5].wait()
            for d in range(1, NY):
                at_head(2, d)
        cols = slice(h * DH, (h + 1) * DH)
        keys = kvh[z_, 0, :, :, cols].reshape(-1, DH)
        values = kvh[z_, 1, :, :, cols].reshape(-1, DH)
        weights = silu_of_half(dot_t(qh[:, :, cols].reshape(-1, DH), keys) * half_factor)
        more = dot(weights, values)
        oh[h] = more if t == 0 else oh[h] + more

    halo_at = {1: [(1, 0)], 3: [(0, 1)], 5: [(1, 1)]}
    for t in range(1, NZL):
        z_ = z_of(t)
        for a in range(2):
            arrived(a, z_)

            @pl.when(goes_on(z_))
            def _():
                hop_z(a, z_).start()

            if a == 0:
                hist_head(t - 1, 0)
                if t < 5:
                    own_head(2 * t - 2)
        for way, a in halo_at.get(t, []):
            halo_copy(way, a).start()
        if t == 2:
            for z_ in range(NZL):
                @pl.when((core != zh) | (z != z_))
                def _():
                    there = wb.at[core, x, y, z_]
                    remote(there, there, wz_send.at[0], wz_recv.at[z_], other_core).wait_recv()
            for d in range(1, NY):
                tile_y(d).start()
        if t == 4:
            for d in range(1, NY):
                there = wb.at[core, x, lax.rem(y + NY - d, NY)]
                remote(there, there, wy_send.at[0], wy_recv.at[d - 1], other_core).wait_recv()
            for d in range(1, NX):
                tile_x(d).start()
            tile_out(0).start()
        hist_head(t - 1, 1)
        if t < 5:
            own_head(2 * t - 1)
    for h in range(HEADS):
        hist_head(NZL - 1, h)
    for y_ in range(NY):
        for h in range(HEADS):
            part_out[y_, :, h * DH:(h + 1) * DH] = oh[h, y_ * rows:(y_ + 1) * rows].astype(BF16)
    for d in range(1, NY):
        from_head(d).start()
    part_in[y] = part_out[y]
    for d in range(1, NX):
        there = wb.at[core, lax.rem(x + NX - d, NX)]
        remote(there, there, wx_send.at[0], wx_recv.at[d - 1], other_core).wait_recv()
        tile_out(NX - d).start()
    halo_chunk(0)
    halo_chunk(1)

    for copy in incoming[9:]:
        copy.wait()
    for d in range(1, NY):
        back_home(d)
    for y_ in range(NY):
        cols = slice(y_ * SHARE, (y_ + 1) * SHARE)
        att[:, cols] = att[:, cols] + part_in[y_].astype(F32)
    attended = att[...]
    center = jnp.mean(attended, axis=1, keepdims=True)
    moved = attended - center
    spread = jnp.mean(moved * moved, axis=1, keepdims=True)
    gated = (moved * lax.rsqrt(spread + 1e-05) * gate_ref[...].astype(F32)).astype(BF16)

    for d in range(NX):
        there = wb.at[1 - core, lax.rem(x + d, NX)]
        remote(there, there, wo_send.at[0], wo_recv.at[d], other_core).wait_recv()
    for x_ in range(NX):
        cols = slice(x_ * 2 * DH, (x_ + 1) * 2 * DH)
        weight = jnp.concatenate(
            [wb[0, x_].reshape(-1, DH), wb[1, x_].reshape(-1, DH)], axis=1
        )
        out_ref[:, cols] = (res_ref[:, cols].astype(F32) + dot(gated, weight)).astype(BF16)

    @pl.when(z < NZL - 1)
    def _():
        for a in range(2):
            own_z(a, 0).wait_send()

    @pl.when(z > 0)
    def _():
        for a in range(2):
            own_z(a, 1).wait_send()

    for t in range(1, NZL):
        z_ = z_of(t)

        @pl.when(goes_on(z_))
        def _():
            for a in range(2):
                hop_z(a, z_).wait_send()

    for d in range(1, NY):
        for i in range(3):
            to_head(i, d).wait_send()
        from_head(d).wait_send()
    for way in range(2):
        for a in range(2):
            halo_copy(way, a).wait_send()

    @pl.when(core == zh)
    def _():
        for d in range(1, NZH * NZL):
            tile_z(d).wait_send()

    for d in range(1, NY):
        tile_y(d).wait_send()
    for d in range(1, NX):
        tile_x(d).wait_send()
    for d in range(NX):
        tile_out(d).wait_send()


def shards(q, k, v, gate, resid, hk, hv, ids, pattern, weight):
    rows, width = q.shape[1:]
    hist = hk.shape[1]
    hbm = pl.BlockSpec(memory_space=pl.ANY)
    vmem = pl.BlockSpec(memory_space=pltpu.VMEM)
    dma = pltpu.SemaphoreType.DMA
    out = pl.pallas_call(
        kernel,
        out_shape=jax.ShapeDtypeStruct((rows, width), BF16),
        in_specs=[hbm] * 10,
        out_specs=vmem,
        scratch_shapes=[
            pltpu.VMEM((5, rows, width), BF16),
            pltpu.VMEM(ids.shape, ids.dtype),
            pltpu.VMEM(pattern.shape, pattern.dtype),
            pltpu.VMEM(weight.shape, BF16),
            pltpu.VMEM((NZL, 2, NY, hist, SHARE), BF16),
            pltpu.VMEM((NY, rows, SHARE), BF16),
            pltpu.VMEM((HEADS, NY * rows, DH), F32),
            pltpu.VMEM((NY, rows, SHARE), BF16),
            pltpu.VMEM((NY, rows, SHARE), BF16),
            pltpu.VMEM((2, 2, rows, width), BF16),
            pltpu.VMEM(weight.shape, BF16),
            pltpu.VMEM((NZH, NX, NY, NZL, weight.shape[0], 2 * weight.shape[1]), BF16),
            pltpu.VMEM((3, rows, rows), F32),
            pltpu.VMEM((rows, width), F32),
            dma((11,)), dma((2, NZL)), dma((2, 2)), dma((2, NZL)), dma((3, NY - 1)), dma((3, NY - 1)),
            dma((NY - 1,)), dma((NY - 1,)), dma((2, 2)), dma((2, 2)),
            dma, dma, dma((NZH * NZL - 1,)), dma((NZL,)), dma((NY - 1,)), dma((NY - 1,)),
            dma((NX - 1,)), dma((NX - 1,)), dma((NX,)), dma((NX,)),
        ],
        compiler_params=pltpu.CompilerParams(
            collective_id=0, has_side_effects=True, vmem_limit_bytes=60 * 1024 * 1024
        ),
    )(q[0], k[0], v[0], gate[0], resid[0], hk[0], hv[0], ids, pattern, weight)
    return out[None]


def solution(mesh):
    part = P("users", "cand", None)
    return jax.shard_map(
        shards,
        mesh=mesh,
        in_specs=(part,) * 7 + (P("users", None), P(), P("cand", "users")),
        out_specs=part,
        check_vma=False,
    )
```

```python
import jax
import jax.numpy as jnp
from jax import lax
from jax.experimental import pallas as pl
from jax.experimental.pallas import tpu as pltpu
from jax.sharding import PartitionSpec as P

H = 8
DH = 128
NX, NZH, NCORE = 4, 2, 2
NY, NZL = 4, 8
NCAND = NY * NZL
HEADS = H // NY
SHARE = HEADS * DH
MESH = pl.DeviceIdType.MESH
BF16, F32 = jnp.bfloat16, jnp.float32


def dot(a, b):
    return lax.dot_general(a, b, (((1,), (0,)), ((), ())), preferred_element_type=F32)


def dot_t(a, b):
    return lax.dot_general(a, b, (((1,), (1,)), ((), ())), preferred_element_type=F32)


def silu_of_half(h):
    return (h + h * jnp.tanh(h)).astype(BF16)


def kernel(
    q_hbm, k_hbm, v_hbm, gate_hbm, res_hbm, hk_hbm, hv_hbm, ids_hbm, pat_hbm, w_hbm,
    out_ref,
    rows5, ids_ref, pat_ref, w_ref,
    kvh, qh, oh, part_out, part_in, halo, wtmp, wb, maskh, att,
    in_sem, kv_recv, own_send, z_send, ys_send, ys_recv, o_send, o_recv, halo_send, halo_recv,
    wc_send, wc_recv, wz_send, wz_recv, wy_send, wy_recv, wx_send, wx_recv, wo_send, wo_recv,
):
    u, c = lax.axis_index("users"), lax.axis_index("cand")
    core = lax.rem(u, NCORE)
    zh = lax.rem(u // NCORE, NZH)
    x = u // (NCORE * NZH)
    z = lax.rem(c, NZL)
    y = c // NZL
    rows = q_hbm.shape[0]
    q_ref, k_ref, v_ref, gate_ref, res_ref = [rows5.at[i] for i in range(5)]

    def share(y_):
        return pl.ds(pl.multiple_of(y_ * SHARE, SHARE), SHARE)

    incoming = [
        pltpu.make_async_copy(src, dst, in_sem.at[i])
        for i, (src, dst) in enumerate([
            (w_hbm, w_ref), (ids_hbm, ids_ref), (pat_hbm, pat_ref),
            (hk_hbm.at[:, share(y)], kvh.at[z, 0, y]), (hv_hbm.at[:, share(y)], kvh.at[z, 1, y]),
            (q_hbm.at[:, share(y)], qh.at[y]),
            (q_hbm, q_ref), (k_hbm, k_ref), (v_hbm, v_ref), (gate_hbm, gate_ref), (res_hbm, res_ref),
        ])
    ]
    for copy in incoming:
        copy.start()

    def dev(x_, zh_, core_, y_, z_):
        return {"users": (x_ * NZH + zh_) * NCORE + core_, "cand": y_ * NZL + z_}

    def on_cand(c_):
        return {"users": u, "cand": c_}

    def along_z(d):
        far = lax.rem(zh * NZL + z + d, NZH * NZL)
        return far // NZL, lax.rem(far, NZL)

    other_core = dev(x, zh, 1 - core, y, z)
    nxt, prv = lax.rem(c + 1, NCAND), lax.rem(c + NCAND - 1, NCAND)

    barrier = pltpu.get_barrier_semaphore()

    def greet(device):
        pl.semaphore_signal(barrier, inc=1, device_id=device, device_id_type=MESH)

    for d in range(1, NZH * NZL):
        zh_, z_ = along_z(d)
        greet(dev(x, zh_, core, y, z_))
    for d in range(1, NY):
        greet(dev(x, zh, core, lax.rem(y + d, NY), z))
    for d in range(1, NX):
        greet(dev(lax.rem(x + d, NX), zh, core, y, z))
    greet(other_core)

    @pl.when(z == NZL - 1)
    def _():
        greet(on_cand(nxt))

    @pl.when(z == 0)
    def _():
        greet(on_cand(prv))

    partners = NZH * NZL - 1 + NY - 1 + NX - 1 + 1
    edge = jnp.where(z == 0, 1, 0) + jnp.where(z == NZL - 1, 1, 0)
    pl.semaphore_wait(barrier, partners + edge)

    def remote(src, dst, send, recv, device):
        return pltpu.make_async_remote_copy(
            src_ref=src, dst_ref=dst, send_sem=send, recv_sem=recv,
            device_id=device, device_id_type=MESH,
        )

    def z_of(t):
        both = 2 * jnp.minimum(z, NZL - 1 - z)
        side = jnp.where(2 * z < NZL, -1, 1)
        turn = z + side * ((t + 1) // 2 if t % 2 else -(t // 2))
        return jnp.where(t <= both, turn, jnp.where(2 * z < NZL, t, NZL - 1 - t))

    def to_head(i, d):
        y_ = lax.rem(y + d, NY)
        src = (hk_hbm, hv_hbm, q_hbm)[i].at[:, share(y_)]
        dst = qh.at[y] if i == 2 else kvh.at[z, i, y]
        return remote(src, dst, ys_send.at[i, d - 1], ys_recv.at[i, d - 1], on_cand(y_ * NZL + z))

    def at_head(i, d):
        y_ = lax.rem(y + NY - d, NY)
        here = qh.at[y_] if i == 2 else kvh.at[z, i, y_]
        remote(here, here, ys_send.at[0, 0], ys_recv.at[i, d - 1], other_core).wait_recv()

    def from_head(d):
        y_ = lax.rem(y + d, NY)
        return remote(part_out.at[y_], part_in.at[y], o_send.at[d - 1], o_recv.at[d - 1], on_cand(y_ * NZL + z))

    def back_home(d):
        here = part_in.at[lax.rem(y + NY - d, NY)]
        remote(here, here, o_send.at[0], o_recv.at[d - 1], other_core).wait_recv()

    def own_z(a, way):
        to = on_cand(y * NZL + (z + 1 if way == 0 else z - 1))
        return remote(kvh.at[z, a], kvh.at[z, a], own_send.at[way, a], kv_recv.at[a, z], to)

    def hop_z(a, z_):
        to = on_cand(y * NZL + z + jnp.where(z_ < z, 1, -1))
        return remote(kvh.at[z_, a], kvh.at[z_, a], z_send.at[a, z_], kv_recv.at[a, z_], to)

    def goes_on(z_):
        return ((z_ < z) & (z < NZL - 1)) | ((z_ > z) & (z > 0))

    def arrived(a, z_):
        here = kvh.at[z_, a]
        remote(here, here, own_send.at[0, 0], kv_recv.at[a, z_], other_core).wait_recv()

    def halo_copy(way, a):
        return remote(
            (k_hbm, v_hbm)[a], halo.at[way, a], halo_send.at[way, a], halo_recv.at[way, a],
            on_cand(nxt if way == 0 else prv),
        )

    wraps = (z == NZL - 1, z == 0)
    beside = (~wraps[0], ~wraps[1])

    def near_copies(a, when):
        for way in range(2):
            @pl.when(when[way])
            def _():
                halo_copy(way, a).start()

    tile_core = remote(w_hbm, wtmp, wc_send, wc_recv, other_core)

    def tile_z(d):
        zh_, z_ = along_z(d)
        here = wb.at[core, x, y, z]
        return remote(here, here, wz_send.at[d - 1], wz_recv.at[z], dev(x, zh_, core, y, z_))

    def tile_y(d):
        here = wb.at[core, x, y]
        return remote(here, here, wy_send.at[d - 1], wy_recv.at[d - 1], dev(x, zh, core, lax.rem(y + d, NY), z))

    def tile_x(d):
        here = wb.at[core, x]
        return remote(here, here, wx_send.at[d - 1], wx_recv.at[d - 1], dev(lax.rem(x + d, NX), zh, core, y, z))

    def tile_out(d):
        here = wb.at[core, lax.rem(x + d, NX)]
        return remote(here, here, wo_send.at[d], wo_recv.at[d], other_core)

    for i in range(3):
        for d in range(1, NY):
            to_head(i, d).start()
    near_copies(0, beside)
    tile_core.start()

    for copy in incoming[:3]:
        copy.wait()

    def ids_row(b):
        at = jnp.clip(b, 0, NCAND - 1) * DH
        got = ids_ref[:, pl.ds(pl.multiple_of(at, DH), DH)].astype(F32)
        return jnp.where((b >= 0) & (b < NCAND), got, -1.0)

    square = (rows, rows)
    sub = lax.broadcasted_iota(jnp.int32, square, 0)
    lane = lax.broadcasted_iota(jnp.int32, square, 1)
    half_factor = 0.5 * DH ** (-0.5)

    def make_mask():
        ids = [ids_row(c + d) for d in (-2, -1, 0, 1)]
        wide = [jnp.broadcast_to(r, square) for r in ids]
        tall = [w.T for w in wide]
        offs = []
        for b in (1, 2, 3):
            whole = jnp.where(tall[b - 1] == wide[b], 1.0, 0.0)
            part = jnp.where((tall[b] == wide[b]) & (sub < lane), 1.0, 0.0)
            offs.append(jnp.sum(whole + part, axis=0, keepdims=True))
        own_off = jnp.broadcast_to(offs[1], square).T
        hot_rows = jnp.where(own_off == lane.astype(F32), 1.0, 0.0).astype(BF16)
        allowed = jnp.where(pat_ref[...] == 1, 1.0, 0.0).astype(BF16)
        by_row = dot(hot_rows, allowed).astype(BF16)
        for b in range(3):
            hot_keys = jnp.where(sub.astype(F32) == jnp.broadcast_to(offs[b], square), 1.0, 0.0).astype(BF16)
            seen = dot(by_row, hot_keys) > 0.5
            if b == 1:
                seen = seen | (sub == lane)
            seen = seen & (tall[2] == wide[b + 1])
            maskh[b] = jnp.where(seen, half_factor, 0.0)

    for copy in incoming[3:5]:
        copy.wait()
    for a in range(2):
        for d in range(1, NY):
            at_head(a, d)

        @pl.when(z < NZL - 1)
        def _():
            own_z(a, 0).start()

        @pl.when(z > 0)
        def _():
            own_z(a, 1).start()

    tile_core.wait()
    mine, theirs = w_ref[...].astype(F32), wtmp[...].astype(F32)
    tile = jnp.where(
        core == 0, jnp.concatenate([mine, theirs], axis=1), jnp.concatenate([theirs, mine], axis=1)
    ).astype(BF16)

    @pl.when(core == zh)
    def _():
        wb[core, x, y, z] = tile
        for d in range(1, NZH * NZL):
            tile_z(d).start()

    make_mask()

    def own_head(h):
        if h == 0:
            for copy in incoming[6:9]:
                copy.wait()
        cols = slice(h * DH, (h + 1) * DH)
        weights = silu_of_half(dot_t(q_ref[:, cols], k_ref[:, cols]) * maskh[1])
        att[:, cols] = dot(weights, v_ref[:, cols])

    def halo_chunk(way):
        for a in range(2):
            halo_copy(way, a).wait_recv()
        for h in range(H):
            cols = slice(h * DH, (h + 1) * DH)
            weights = silu_of_half(dot_t(q_ref[:, cols], halo[way, 0, :, cols]) * maskh[2 * way])
            att[:, cols] = att[:, cols] + dot(weights, halo[way, 1, :, cols])

    def hist_head(t, h):
        z_ = z_of(t)
        if t == 0 and h == 0:
            incoming[5].wait()
            for d in range(1, NY):
                at_head(2, d)
        cols = slice(h * DH, (h + 1) * DH)
        keys = kvh[z_, 0, :, :, cols].reshape(-1, DH)
        values = kvh[z_, 1, :, :, cols].reshape(-1, DH)
        weights = silu_of_half(dot_t(qh[:, :, cols].reshape(-1, DH), keys) * half_factor)
        more = dot(weights, values)
        oh[h] = more if t == 0 else oh[h] + more

    near_at = {1: (0, wraps), 3: (1, beside), 5: (1, wraps)}
    for t in range(1, NZL):
        z_ = z_of(t)
        for a in range(2):
            arrived(a, z_)

            @pl.when(goes_on(z_))
            def _():
                hop_z(a, z_).start()

            if a == 0:
                hist_head(t - 1, 0)
                if t < 5:
                    own_head(2 * t - 2)
        if t in near_at:
            near_copies(*near_at[t])
        if t == 2:
            for z_ in range(NZL):
                @pl.when((core != zh) | (z != z_))
                def _():
                    there = wb.at[core, x, y, z_]
                    remote(there, there, wz_send.at[0], wz_recv.at[z_], other_core).wait_recv()
            for d in range(1, NY):
                tile_y(d).start()
        if t == 4:
            for d in range(1, NY):
                there = wb.at[core, x, lax.rem(y + NY - d, NY)]
                remote(there, there, wy_send.at[0], wy_recv.at[d - 1], other_core).wait_recv()
            for d in range(1, NX):
                tile_x(d).start()
            tile_out(0).start()
        hist_head(t - 1, 1)
        if t < 5:
            own_head(2 * t - 1)
    for h in range(HEADS):
        hist_head(NZL - 1, h)
    for y_ in range(NY):
        for h in range(HEADS):
            part_out[y_, :, h * DH:(h + 1) * DH] = oh[h, y_ * rows:(y_ + 1) * rows].astype(BF16)
    for d in range(1, NY):
        from_head(d).start()
    part_in[y] = part_out[y]
    for d in range(1, NX):
        there = wb.at[core, lax.rem(x + NX - d, NX)]
        remote(there, there, wx_send.at[0], wx_recv.at[d - 1], other_core).wait_recv()
        tile_out(NX - d).start()
    halo_chunk(0)
    halo_chunk(1)

    for copy in incoming[9:]:
        copy.wait()
    for d in range(1, NY):
        back_home(d)
    for y_ in range(NY):
        cols = slice(y_ * SHARE, (y_ + 1) * SHARE)
        att[:, cols] = att[:, cols] + part_in[y_].astype(F32)
    attended = att[...]
    center = jnp.mean(attended, axis=1, keepdims=True)
    moved = attended - center
    spread = jnp.mean(moved * moved, axis=1, keepdims=True)
    gated = (moved * lax.rsqrt(spread + 1e-05) * gate_ref[...].astype(F32)).astype(BF16)

    for d in range(NX):
        there = wb.at[1 - core, lax.rem(x + d, NX)]
        remote(there, there, wo_send.at[0], wo_recv.at[d], other_core).wait_recv()
    for x_ in range(NX):
        cols = slice(x_ * 2 * DH, (x_ + 1) * 2 * DH)
        weight = jnp.concatenate(
            [wb[0, x_].reshape(-1, DH), wb[1, x_].reshape(-1, DH)], axis=1
        )
        out_ref[:, cols] = (res_ref[:, cols].astype(F32) + dot(gated, weight)).astype(BF16)

    @pl.when(z < NZL - 1)
    def _():
        for a in range(2):
            own_z(a, 0).wait_send()

    @pl.when(z > 0)
    def _():
        for a in range(2):
            own_z(a, 1).wait_send()

    for t in range(1, NZL):
        z_ = z_of(t)

        @pl.when(goes_on(z_))
        def _():
            for a in range(2):
                hop_z(a, z_).wait_send()

    for d in range(1, NY):
        for i in range(3):
            to_head(i, d).wait_send()
        from_head(d).wait_send()
    for way in range(2):
        for a in range(2):
            halo_copy(way, a).wait_send()

    @pl.when(core == zh)
    def _():
        for d in range(1, NZH * NZL):
            tile_z(d).wait_send()

    for d in range(1, NY):
        tile_y(d).wait_send()
    for d in range(1, NX):
        tile_x(d).wait_send()
    for d in range(NX):
        tile_out(d).wait_send()


def shards(q, k, v, gate, resid, hk, hv, ids, pattern, weight):
    rows, width = q.shape[1:]
    hist = hk.shape[1]
    hbm = pl.BlockSpec(memory_space=pl.ANY)
    vmem = pl.BlockSpec(memory_space=pltpu.VMEM)
    dma = pltpu.SemaphoreType.DMA
    out = pl.pallas_call(
        kernel,
        out_shape=jax.ShapeDtypeStruct((rows, width), BF16),
        in_specs=[hbm] * 10,
        out_specs=vmem,
        scratch_shapes=[
            pltpu.VMEM((5, rows, width), BF16),
            pltpu.VMEM(ids.shape, ids.dtype),
            pltpu.VMEM(pattern.shape, pattern.dtype),
            pltpu.VMEM(weight.shape, BF16),
            pltpu.VMEM((NZL, 2, NY, hist, SHARE), BF16),
            pltpu.VMEM((NY, rows, SHARE), BF16),
            pltpu.VMEM((HEADS, NY * rows, DH), F32),
            pltpu.VMEM((NY, rows, SHARE), BF16),
            pltpu.VMEM((NY, rows, SHARE), BF16),
            pltpu.VMEM((2, 2, rows, width), BF16),
            pltpu.VMEM(weight.shape, BF16),
            pltpu.VMEM((NZH, NX, NY, NZL, weight.shape[0], 2 * weight.shape[1]), BF16),
            pltpu.VMEM((3, rows, rows), F32),
            pltpu.VMEM((rows, width), F32),
            dma((11,)), dma((2, NZL)), dma((2, 2)), dma((2, NZL)), dma((3, NY - 1)), dma((3, NY - 1)),
            dma((NY - 1,)), dma((NY - 1,)), dma((2, 2)), dma((2, 2)),
            dma, dma, dma((NZH * NZL - 1,)), dma((NZL,)), dma((NY - 1,)), dma((NY - 1,)),
            dma((NX - 1,)), dma((NX - 1,)), dma((NX,)), dma((NX,)),
        ],
        compiler_params=pltpu.CompilerParams(
            collective_id=0, has_side_effects=True, vmem_limit_bytes=60 * 1024 * 1024
        ),
    )(q[0], k[0], v[0], gate[0], resid[0], hk[0], hv[0], ids, pattern, weight)
    return out[None]


def solution(mesh):
    part = P("users", "cand", None)
    return jax.shard_map(
        shards,
        mesh=mesh,
        in_specs=(part,) * 7 + (P("users", None), P(), P("cand", "users")),
        out_specs=part,
        check_vma=False,
    )
```

```python
import jax
import jax.numpy as jnp
from jax import lax
from jax.experimental import pallas as pl
from jax.experimental.pallas import tpu as pltpu
from jax.sharding import PartitionSpec as P

H = 8
DH = 128
NX, NZH, NCORE = 4, 2, 2
NY, NZL = 4, 8
NCAND = NY * NZL
HEADS = H // NY
SHARE = HEADS * DH
MESH = pl.DeviceIdType.MESH
BF16, F32 = jnp.bfloat16, jnp.float32


def dot(a, b):
    return lax.dot_general(a, b, (((1,), (0,)), ((), ())), preferred_element_type=F32)


def dot_t(a, b):
    return lax.dot_general(a, b, (((1,), (1,)), ((), ())), preferred_element_type=F32)


def silu_of_half(h):
    return (h + h * jnp.tanh(h)).astype(BF16)


def kernel(
    q_hbm, k_hbm, v_hbm, gate_hbm, res_hbm, hk_hbm, hv_hbm, ids_hbm, pat_hbm, w_hbm,
    out_ref,
    rows5, ids_ref, pat_ref, w_ref,
    kvh, qh, oh, part_out, part_in, halo, wtmp, wb, maskh, att,
    in_sem, kv_recv, own_send, z_send, ys_send, ys_recv, o_send, o_recv, halo_send, halo_recv,
    wc_send, wc_recv, wz_send, wz_recv, wy_send, wy_recv, wx_send, wx_recv, wo_send, wo_recv,
):
    u, c = lax.axis_index("users"), lax.axis_index("cand")
    core = lax.rem(u, NCORE)
    zh = lax.rem(u // NCORE, NZH)
    x = u // (NCORE * NZH)
    z = lax.rem(c, NZL)
    y = c // NZL
    rows = q_hbm.shape[0]
    q_ref, k_ref, v_ref, gate_ref, res_ref = [rows5.at[i] for i in range(5)]

    def share(y_):
        return pl.ds(pl.multiple_of(y_ * SHARE, SHARE), SHARE)

    incoming = [
        pltpu.make_async_copy(src, dst, in_sem.at[i])
        for i, (src, dst) in enumerate([
            (w_hbm, w_ref), (ids_hbm, ids_ref), (pat_hbm, pat_ref),
            (hk_hbm.at[:, share(y)], kvh.at[z, 0, y]), (hv_hbm.at[:, share(y)], kvh.at[z, 1, y]),
            (q_hbm.at[:, share(y)], qh.at[y]),
            (q_hbm, q_ref), (k_hbm, k_ref), (v_hbm, v_ref), (gate_hbm, gate_ref), (res_hbm, res_ref),
        ])
    ]
    for copy in incoming:
        copy.start()

    def dev(x_, zh_, core_, y_, z_):
        return {"users": (x_ * NZH + zh_) * NCORE + core_, "cand": y_ * NZL + z_}

    def on_cand(c_):
        return {"users": u, "cand": c_}

    def along_z(d):
        far = lax.rem(zh * NZL + z + d, NZH * NZL)
        return far // NZL, lax.rem(far, NZL)

    other_core = dev(x, zh, 1 - core, y, z)
    nxt, prv = lax.rem(c + 1, NCAND), lax.rem(c + NCAND - 1, NCAND)

    barrier = pltpu.get_barrier_semaphore()

    def greet(device):
        pl.semaphore_signal(barrier, inc=1, device_id=device, device_id_type=MESH)

    for d in range(1, NZH * NZL):
        zh_, z_ = along_z(d)
        greet(dev(x, zh_, core, y, z_))
    for d in range(1, NY):
        greet(dev(x, zh, core, lax.rem(y + d, NY), z))
    for d in range(1, NX):
        greet(dev(lax.rem(x + d, NX), zh, core, y, z))
    greet(other_core)

    @pl.when(z == NZL - 1)
    def _():
        greet(on_cand(nxt))

    @pl.when(z == 0)
    def _():
        greet(on_cand(prv))

    partners = NZH * NZL - 1 + NY - 1 + NX - 1 + 1
    edge = jnp.where(z == 0, 1, 0) + jnp.where(z == NZL - 1, 1, 0)
    pl.semaphore_wait(barrier, partners + edge)

    def remote(src, dst, send, recv, device):
        return pltpu.make_async_remote_copy(
            src_ref=src, dst_ref=dst, send_sem=send, recv_sem=recv,
            device_id=device, device_id_type=MESH,
        )

    def z_of(t):
        both = 2 * jnp.minimum(z, NZL - 1 - z)
        side = jnp.where(2 * z < NZL, -1, 1)
        turn = z + side * ((t + 1) // 2 if t % 2 else -(t // 2))
        return jnp.where(t <= both, turn, jnp.where(2 * z < NZL, t, NZL - 1 - t))

    def to_head(i, d):
        y_ = lax.rem(y + d, NY)
        src = (hk_hbm, hv_hbm, q_hbm)[i].at[:, share(y_)]
        dst = qh.at[y] if i == 2 else kvh.at[z, i, y]
        return remote(src, dst, ys_send.at[i, d - 1], ys_recv.at[i, d - 1], on_cand(y_ * NZL + z))

    def at_head(i, d):
        y_ = lax.rem(y + NY - d, NY)
        here = qh.at[y_] if i == 2 else kvh.at[z, i, y_]
        remote(here, here, ys_send.at[0, 0], ys_recv.at[i, d - 1], other_core).wait_recv()

    def from_head(d):
        y_ = lax.rem(y + d, NY)
        return remote(part_out.at[y_], part_in.at[y], o_send.at[d - 1], o_recv.at[d - 1], on_cand(y_ * NZL + z))

    def back_home(d):
        here = part_in.at[lax.rem(y + NY - d, NY)]
        remote(here, here, o_send.at[0], o_recv.at[d - 1], other_core).wait_recv()

    def own_z(a, way):
        to = on_cand(y * NZL + (z + 1 if way == 0 else z - 1))
        return remote(kvh.at[z, a], kvh.at[z, a], own_send.at[way, a], kv_recv.at[a, z], to)

    def hop_z(a, z_):
        to = on_cand(y * NZL + z + jnp.where(z_ < z, 1, -1))
        return remote(kvh.at[z_, a], kvh.at[z_, a], z_send.at[a, z_], kv_recv.at[a, z_], to)

    def goes_on(z_):
        return ((z_ < z) & (z < NZL - 1)) | ((z_ > z) & (z > 0))

    def arrived(a, z_):
        here = kvh.at[z_, a]
        remote(here, here, own_send.at[0, 0], kv_recv.at[a, z_], other_core).wait_recv()

    def halo_copy(way, a):
        return remote(
            (k_hbm, v_hbm)[a], halo.at[way, a], halo_send.at[way, a], halo_recv.at[way, a],
            on_cand(nxt if way == 0 else prv),
        )

    wraps = (z == NZL - 1, z == 0)
    beside = (~wraps[0], ~wraps[1])

    def near_copies(a, when):
        for way in range(2):
            @pl.when(when[way])
            def _():
                halo_copy(way, a).start()

    tile_core = remote(w_hbm, wtmp, wc_send, wc_recv, other_core)

    def tile_z(d):
        zh_, z_ = along_z(d)
        here = wb.at[core, x, y, z]
        return remote(here, here, wz_send.at[d - 1], wz_recv.at[z], dev(x, zh_, core, y, z_))

    def tile_y(d):
        here = wb.at[core, x, y]
        return remote(here, here, wy_send.at[d - 1], wy_recv.at[d - 1], dev(x, zh, core, lax.rem(y + d, NY), z))

    def tile_x(d):
        here = wb.at[core, x]
        return remote(here, here, wx_send.at[d - 1], wx_recv.at[d - 1], dev(lax.rem(x + d, NX), zh, core, y, z))

    def tile_out(d):
        here = wb.at[core, lax.rem(x + d, NX)]
        return remote(here, here, wo_send.at[d], wo_recv.at[d], other_core)

    for i in range(3):
        for d in range(1, NY):
            to_head(i, d).start()
    near_copies(0, beside)
    tile_core.start()

    for copy in incoming[:3]:
        copy.wait()

    def ids_row(b):
        at = jnp.clip(b, 0, NCAND - 1) * DH
        got = ids_ref[:, pl.ds(pl.multiple_of(at, DH), DH)].astype(F32)
        return jnp.where((b >= 0) & (b < NCAND), got, -1.0)

    square = (rows, rows)
    sub = lax.broadcasted_iota(jnp.int32, square, 0)
    lane = lax.broadcasted_iota(jnp.int32, square, 1)
    half_factor = 0.5 * DH ** (-0.5)

    def make_mask():
        ids = [ids_row(c + d) for d in (-2, -1, 0, 1)]
        wide = [jnp.broadcast_to(r, square) for r in ids]
        tall = [w.T for w in wide]
        offs = []
        for b in (1, 2, 3):
            whole = jnp.where(tall[b - 1] == wide[b], 1.0, 0.0)
            part = jnp.where((tall[b] == wide[b]) & (sub < lane), 1.0, 0.0)
            offs.append(jnp.sum(whole + part, axis=0, keepdims=True))
        own_off = jnp.broadcast_to(offs[1], square).T
        hot_rows = jnp.where(own_off == lane.astype(F32), 1.0, 0.0).astype(BF16)
        allowed = jnp.where(pat_ref[...] == 1, 1.0, 0.0).astype(BF16)
        by_row = dot(hot_rows, allowed).astype(BF16)
        for b in range(3):
            hot_keys = jnp.where(sub.astype(F32) == jnp.broadcast_to(offs[b], square), 1.0, 0.0).astype(BF16)
            seen = dot(by_row, hot_keys) > 0.5
            if b == 1:
                seen = seen | (sub == lane)
            seen = seen & (tall[2] == wide[b + 1])
            maskh[b] = jnp.where(seen, half_factor, 0.0)

    for copy in incoming[3:5]:
        copy.wait()
    for a in range(2):
        for d in range(1, NY):
            at_head(a, d)

        @pl.when(z < NZL - 1)
        def _():
            own_z(a, 0).start()

        @pl.when(z > 0)
        def _():
            own_z(a, 1).start()

    tile_core.wait()
    mine, theirs = w_ref[...].astype(F32), wtmp[...].astype(F32)
    tile = jnp.where(
        core == 0, jnp.concatenate([mine, theirs], axis=1), jnp.concatenate([theirs, mine], axis=1)
    ).astype(BF16)

    @pl.when(core == zh)
    def _():
        wb[core, x, y, z] = tile
        for d in range(1, NZH * NZL):
            tile_z(d).start()

    make_mask()

    def own_head(h):
        if h == 0:
            for copy in incoming[6:9]:
                copy.wait()
        cols = slice(h * DH, (h + 1) * DH)
        weights = silu_of_half(dot_t(q_ref[:, cols], k_ref[:, cols]) * maskh[1])
        att[:, cols] = dot(weights, v_ref[:, cols])

    def halo_chunk(side):
        for a in range(2):
            here = halo.at[side, a]
            remote(here, here, halo_send.at[0, 0], halo_recv.at[side, a], other_core).wait_recv()
        for h in range(H):
            cols = slice(h * DH, (h + 1) * DH)
            weights = silu_of_half(dot_t(q_ref[:, cols], halo[side, 0, :, cols]) * maskh[2 * side])
            att[:, cols] = att[:, cols] + dot(weights, halo[side, 1, :, cols])

    def hist_head(t, h):
        z_ = z_of(t)
        if t == 0 and h == 0:
            incoming[5].wait()
            for d in range(1, NY):
                at_head(2, d)
        cols = slice(h * DH, (h + 1) * DH)
        keys = kvh[z_, 0, :, :, cols].reshape(-1, DH)
        values = kvh[z_, 1, :, :, cols].reshape(-1, DH)
        weights = silu_of_half(dot_t(qh[:, :, cols].reshape(-1, DH), keys) * half_factor)
        more = dot(weights, values)
        oh[h] = more if t == 0 else oh[h] + more

    near_at = {1: (0, wraps), 3: (1, beside), 4: (1, wraps)}
    for t in range(1, NZL):
        z_ = z_of(t)
        for a in range(2):
            arrived(a, z_)

            @pl.when(goes_on(z_))
            def _():
                hop_z(a, z_).start()

            if a == 0:
                hist_head(t - 1, 0)
                if t < 5:
                    own_head(2 * t - 2)
        if t in near_at:
            near_copies(*near_at[t])
        if t == 2:
            for z_ in range(NZL):
                @pl.when((core != zh) | (z != z_))
                def _():
                    there = wb.at[core, x, y, z_]
                    remote(there, there, wz_send.at[0], wz_recv.at[z_], other_core).wait_recv()
            for d in range(1, NY):
                tile_y(d).start()
        if t == 4:
            for d in range(1, NY):
                there = wb.at[core, x, lax.rem(y + NY - d, NY)]
                remote(there, there, wy_send.at[0], wy_recv.at[d - 1], other_core).wait_recv()
            for d in range(1, NX):
                tile_x(d).start()
            tile_out(0).start()
        hist_head(t - 1, 1)
        if t < 5:
            own_head(2 * t - 1)
    for h in range(HEADS):
        hist_head(NZL - 1, h)
    for y_ in range(NY):
        for h in range(HEADS):
            part_out[y_, :, h * DH:(h + 1) * DH] = oh[h, y_ * rows:(y_ + 1) * rows].astype(BF16)
    for d in range(1, NY):
        from_head(d).start()
    part_in[y] = part_out[y]
    for d in range(1, NX):
        there = wb.at[core, lax.rem(x + NX - d, NX)]
        remote(there, there, wx_send.at[0], wx_recv.at[d - 1], other_core).wait_recv()
        tile_out(NX - d).start()
    near = jnp.where(z == 0, 1, 0)
    halo_chunk(near)
    halo_chunk(1 - near)

    for copy in incoming[9:]:
        copy.wait()
    for d in range(1, NY):
        back_home(d)
    for y_ in range(NY):
        cols = slice(y_ * SHARE, (y_ + 1) * SHARE)
        att[:, cols] = att[:, cols] + part_in[y_].astype(F32)
    attended = att[...]
    center = jnp.mean(attended, axis=1, keepdims=True)
    moved = attended - center
    spread = jnp.mean(moved * moved, axis=1, keepdims=True)
    gated = (moved * lax.rsqrt(spread + 1e-05) * gate_ref[...].astype(F32)).astype(BF16)

    for d in range(NX):
        there = wb.at[1 - core, lax.rem(x + d, NX)]
        remote(there, there, wo_send.at[0], wo_recv.at[d], other_core).wait_recv()
    for x_ in range(NX):
        cols = slice(x_ * 2 * DH, (x_ + 1) * 2 * DH)
        weight = jnp.concatenate(
            [wb[0, x_].reshape(-1, DH), wb[1, x_].reshape(-1, DH)], axis=1
        )
        out_ref[:, cols] = (res_ref[:, cols].astype(F32) + dot(gated, weight)).astype(BF16)

    @pl.when(z < NZL - 1)
    def _():
        for a in range(2):
            own_z(a, 0).wait_send()

    @pl.when(z > 0)
    def _():
        for a in range(2):
            own_z(a, 1).wait_send()

    for t in range(1, NZL):
        z_ = z_of(t)

        @pl.when(goes_on(z_))
        def _():
            for a in range(2):
                hop_z(a, z_).wait_send()

    for d in range(1, NY):
        for i in range(3):
            to_head(i, d).wait_send()
        from_head(d).wait_send()
    for way in range(2):
        for a in range(2):
            halo_copy(way, a).wait_send()

    @pl.when(core == zh)
    def _():
        for d in range(1, NZH * NZL):
            tile_z(d).wait_send()

    for d in range(1, NY):
        tile_y(d).wait_send()
    for d in range(1, NX):
        tile_x(d).wait_send()
    for d in range(NX):
        tile_out(d).wait_send()


def shards(q, k, v, gate, resid, hk, hv, ids, pattern, weight):
    rows, width = q.shape[1:]
    hist = hk.shape[1]
    hbm = pl.BlockSpec(memory_space=pl.ANY)
    vmem = pl.BlockSpec(memory_space=pltpu.VMEM)
    dma = pltpu.SemaphoreType.DMA
    out = pl.pallas_call(
        kernel,
        out_shape=jax.ShapeDtypeStruct((rows, width), BF16),
        in_specs=[hbm] * 10,
        out_specs=vmem,
        scratch_shapes=[
            pltpu.VMEM((5, rows, width), BF16),
            pltpu.VMEM(ids.shape, ids.dtype),
            pltpu.VMEM(pattern.shape, pattern.dtype),
            pltpu.VMEM(weight.shape, BF16),
            pltpu.VMEM((NZL, 2, NY, hist, SHARE), BF16),
            pltpu.VMEM((NY, rows, SHARE), BF16),
            pltpu.VMEM((HEADS, NY * rows, DH), F32),
            pltpu.VMEM((NY, rows, SHARE), BF16),
            pltpu.VMEM((NY, rows, SHARE), BF16),
            pltpu.VMEM((2, 2, rows, width), BF16),
            pltpu.VMEM(weight.shape, BF16),
            pltpu.VMEM((NZH, NX, NY, NZL, weight.shape[0], 2 * weight.shape[1]), BF16),
            pltpu.VMEM((3, rows, rows), F32),
            pltpu.VMEM((rows, width), F32),
            dma((11,)), dma((2, NZL)), dma((2, 2)), dma((2, NZL)), dma((3, NY - 1)), dma((3, NY - 1)),
            dma((NY - 1,)), dma((NY - 1,)), dma((2, 2)), dma((2, 2)),
            dma, dma, dma((NZH * NZL - 1,)), dma((NZL,)), dma((NY - 1,)), dma((NY - 1,)),
            dma((NX - 1,)), dma((NX - 1,)), dma((NX,)), dma((NX,)),
        ],
        compiler_params=pltpu.CompilerParams(
            collective_id=0, has_side_effects=True, vmem_limit_bytes=60 * 1024 * 1024
        ),
    )(q[0], k[0], v[0], gate[0], resid[0], hk[0], hv[0], ids, pattern, weight)
    return out[None]


def solution(mesh):
    part = P("users", "cand", None)
    return jax.shard_map(
        shards,
        mesh=mesh,
        in_specs=(part,) * 7 + (P("users", None), P(), P("cand", "users")),
        out_specs=part,
        check_vma=False,
    )
```

```python
import jax
import jax.numpy as jnp
from jax import lax
from jax.experimental import pallas as pl
from jax.experimental.pallas import tpu as pltpu
from jax.sharding import PartitionSpec as P

H = 8
DH = 128
NX, NZH, NCORE = 4, 2, 2
NY, NZL = 4, 8
NCAND = NY * NZL
HEADS = H // NY
SHARE = HEADS * DH
MESH = pl.DeviceIdType.MESH
BF16, F32 = jnp.bfloat16, jnp.float32


def dot(a, b):
    return lax.dot_general(a, b, (((1,), (0,)), ((), ())), preferred_element_type=F32)


def dot_t(a, b):
    return lax.dot_general(a, b, (((1,), (1,)), ((), ())), preferred_element_type=F32)


def silu_of_half(h):
    return (h + h * jnp.tanh(h)).astype(BF16)


def kernel(
    q_hbm, k_hbm, v_hbm, gate_hbm, res_hbm, hk_hbm, hv_hbm, ids_hbm, pat_hbm, w_hbm,
    out_ref,
    rows5, ids_ref, pat_ref, w_ref,
    kvh, qh, oh, part_out, part_in, halo, wtmp, wb, maskh, att,
    in_sem, kv_recv, own_send, z_send, ys_send, ys_recv, o_send, o_recv, halo_send, halo_recv,
    wc_send, wc_recv, wz_send, wz_recv, wy_send, wy_recv, wx_send, wx_recv, wo_send, wo_recv,
):
    u, c = lax.axis_index("users"), lax.axis_index("cand")
    core = lax.rem(u, NCORE)
    zh = lax.rem(u // NCORE, NZH)
    x = u // (NCORE * NZH)
    z = lax.rem(c, NZL)
    y = c // NZL
    rows = q_hbm.shape[0]
    q_ref, k_ref, v_ref, gate_ref, res_ref = [rows5.at[i] for i in range(5)]

    def share(y_):
        return pl.ds(pl.multiple_of(y_ * SHARE, SHARE), SHARE)

    incoming = [
        pltpu.make_async_copy(src, dst, in_sem.at[i])
        for i, (src, dst) in enumerate([
            (w_hbm, w_ref), (ids_hbm, ids_ref), (pat_hbm, pat_ref),
            (hk_hbm.at[:, share(y)], kvh.at[z, 0, y]), (hv_hbm.at[:, share(y)], kvh.at[z, 1, y]),
            (q_hbm.at[:, share(y)], qh.at[y]),
            (q_hbm, q_ref), (k_hbm, k_ref), (v_hbm, v_ref), (gate_hbm, gate_ref), (res_hbm, res_ref),
        ])
    ]
    for copy in incoming:
        copy.start()

    def dev(x_, zh_, core_, y_, z_):
        return {"users": (x_ * NZH + zh_) * NCORE + core_, "cand": y_ * NZL + z_}

    def on_cand(c_):
        return {"users": u, "cand": c_}

    def along_z(d):
        far = lax.rem(zh * NZL + z + d, NZH * NZL)
        return far // NZL, lax.rem(far, NZL)

    other_core = dev(x, zh, 1 - core, y, z)
    nxt, prv = lax.rem(c + 1, NCAND), lax.rem(c + NCAND - 1, NCAND)

    barrier = pltpu.get_barrier_semaphore()

    def greet(device):
        pl.semaphore_signal(barrier, inc=1, device_id=device, device_id_type=MESH)

    for d in range(1, NZH * NZL):
        zh_, z_ = along_z(d)
        greet(dev(x, zh_, core, y, z_))
    for d in range(1, NY):
        greet(dev(x, zh, core, lax.rem(y + d, NY), z))
    for d in range(1, NX):
        greet(dev(lax.rem(x + d, NX), zh, core, y, z))
    greet(other_core)

    @pl.when(z == NZL - 1)
    def _():
        greet(on_cand(nxt))

    @pl.when(z == 0)
    def _():
        greet(on_cand(prv))

    partners = NZH * NZL - 1 + NY - 1 + NX - 1 + 1
    edge = jnp.where(z == 0, 1, 0) + jnp.where(z == NZL - 1, 1, 0)
    pl.semaphore_wait(barrier, partners + edge)

    def remote(src, dst, send, recv, device):
        return pltpu.make_async_remote_copy(
            src_ref=src, dst_ref=dst, send_sem=send, recv_sem=recv,
            device_id=device, device_id_type=MESH,
        )

    def z_of(t):
        both = 2 * jnp.minimum(z, NZL - 1 - z)
        side = jnp.where(2 * z < NZL, -1, 1)
        turn = z + side * ((t + 1) // 2 if t % 2 else -(t // 2))
        return jnp.where(t <= both, turn, jnp.where(2 * z < NZL, t, NZL - 1 - t))

    def to_head(i, d):
        y_ = lax.rem(y + d, NY)
        src = (hk_hbm, hv_hbm, q_hbm)[i].at[:, share(y_)]
        dst = qh.at[y] if i == 2 else kvh.at[z, i, y]
        return remote(src, dst, ys_send.at[i, d - 1], ys_recv.at[i, d - 1], on_cand(y_ * NZL + z))

    def at_head(i, d):
        y_ = lax.rem(y + NY - d, NY)
        here = qh.at[y_] if i == 2 else kvh.at[z, i, y_]
        remote(here, here, ys_send.at[0, 0], ys_recv.at[i, d - 1], other_core).wait_recv()

    def from_head(d):
        y_ = lax.rem(y + d, NY)
        return remote(part_out.at[y_], part_in.at[y], o_send.at[d - 1], o_recv.at[d - 1], on_cand(y_ * NZL + z))

    def back_home(d):
        here = part_in.at[lax.rem(y + NY - d, NY)]
        remote(here, here, o_send.at[0], o_recv.at[d - 1], other_core).wait_recv()

    def own_z(a, way):
        to = on_cand(y * NZL + (z + 1 if way == 0 else z - 1))
        return remote(kvh.at[z, a], kvh.at[z, a], own_send.at[way, a], kv_recv.at[a, z], to)

    def hop_z(a, z_):
        to = on_cand(y * NZL + z + jnp.where(z_ < z, 1, -1))
        return remote(kvh.at[z_, a], kvh.at[z_, a], z_send.at[a, z_], kv_recv.at[a, z_], to)

    def goes_on(z_):
        return ((z_ < z) & (z < NZL - 1)) | ((z_ > z) & (z > 0))

    def arrived(a, z_):
        here = kvh.at[z_, a]
        remote(here, here, own_send.at[0, 0], kv_recv.at[a, z_], other_core).wait_recv()

    def halo_copy(way, a):
        return remote(
            (k_hbm, v_hbm)[a], halo.at[way, a], halo_send.at[way, a], halo_recv.at[way, a],
            on_cand(nxt if way == 0 else prv),
        )

    wraps = (z == NZL - 1, z == 0)
    beside = (~wraps[0], ~wraps[1])

    def near_copies(a, when):
        for way in range(2):
            @pl.when(when[way])
            def _():
                halo_copy(way, a).start()

    tile_core = remote(w_hbm, wtmp, wc_send, wc_recv, other_core)

    def tile_z(d):
        zh_, z_ = along_z(d)
        here = wb.at[core, x, y, z]
        return remote(here, here, wz_send.at[d - 1], wz_recv.at[z], dev(x, zh_, core, y, z_))

    def tile_y(d):
        here = wb.at[core, x, y]
        return remote(here, here, wy_send.at[d - 1], wy_recv.at[d - 1], dev(x, zh, core, lax.rem(y + d, NY), z))

    def tile_x(d):
        here = wb.at[core, x]
        return remote(here, here, wx_send.at[d - 1], wx_recv.at[d - 1], dev(lax.rem(x + d, NX), zh, core, y, z))

    def tile_out(d):
        here = wb.at[core, lax.rem(x + d, NX)]
        return remote(here, here, wo_send.at[d], wo_recv.at[d], other_core)

    for i in range(3):
        for d in range(1, NY):
            to_head(i, d).start()
    near_copies(0, beside)
    tile_core.start()

    for copy in incoming[:3]:
        copy.wait()

    def ids_row(b):
        at = jnp.clip(b, 0, NCAND - 1) * DH
        got = ids_ref[:, pl.ds(pl.multiple_of(at, DH), DH)].astype(F32)
        return jnp.where((b >= 0) & (b < NCAND), got, -1.0)

    square = (rows, rows)
    sub = lax.broadcasted_iota(jnp.int32, square, 0)
    lane = lax.broadcasted_iota(jnp.int32, square, 1)
    half_factor = 0.5 * DH ** (-0.5)

    def make_mask():
        ids = [ids_row(c + d) for d in (-2, -1, 0, 1)]
        wide = [jnp.broadcast_to(r, square) for r in ids]
        tall = [w.T for w in wide]
        offs = []
        for b in (1, 2, 3):
            whole = jnp.where(tall[b - 1] == wide[b], 1.0, 0.0)
            part = jnp.where((tall[b] == wide[b]) & (sub < lane), 1.0, 0.0)
            offs.append(jnp.sum(whole + part, axis=0, keepdims=True))
        own_off = jnp.broadcast_to(offs[1], square).T
        hot_rows = jnp.where(own_off == lane.astype(F32), 1.0, 0.0).astype(BF16)
        allowed = jnp.where(pat_ref[...] == 1, 1.0, 0.0).astype(BF16)
        by_row = dot(hot_rows, allowed).astype(BF16)
        for b in range(3):
            hot_keys = jnp.where(sub.astype(F32) == jnp.broadcast_to(offs[b], square), 1.0, 0.0).astype(BF16)
            seen = dot(by_row, hot_keys) > 0.5
            if b == 1:
                seen = seen | (sub == lane)
            seen = seen & (tall[2] == wide[b + 1])
            maskh[b] = jnp.where(seen, half_factor, 0.0)

    for copy in incoming[3:5]:
        copy.wait()
    for a in range(2):
        for d in range(1, NY):
            at_head(a, d)

        @pl.when(z < NZL - 1)
        def _():
            own_z(a, 0).start()

        @pl.when(z > 0)
        def _():
            own_z(a, 1).start()

    tile_core.wait()
    mine, theirs = w_ref[...].astype(F32), wtmp[...].astype(F32)
    tile = jnp.where(
        core == 0, jnp.concatenate([mine, theirs], axis=1), jnp.concatenate([theirs, mine], axis=1)
    ).astype(BF16)

    @pl.when(core == zh)
    def _():
        wb[core, x, y, z] = tile
        for d in range(1, NZH * NZL):
            tile_z(d).start()

    make_mask()

    def own_head(h):
        if h == 0:
            for copy in incoming[6:9]:
                copy.wait()
        cols = slice(h * DH, (h + 1) * DH)
        weights = silu_of_half(dot_t(q_ref[:, cols], k_ref[:, cols]) * maskh[1])
        att[:, cols] = dot(weights, v_ref[:, cols])

    def halo_chunk(side):
        for a in range(2):
            here = halo.at[side, a]
            remote(here, here, halo_send.at[0, 0], halo_recv.at[side, a], other_core).wait_recv()
        for h in range(H):
            cols = slice(h * DH, (h + 1) * DH)
            weights = silu_of_half(dot_t(q_ref[:, cols], halo[side, 0, :, cols]) * maskh[2 * side])
            att[:, cols] = att[:, cols] + dot(weights, halo[side, 1, :, cols])

    def hist_head(t, h):
        z_ = z_of(t)
        if t == 0 and h == 0:
            incoming[5].wait()
            for d in range(1, NY):
                at_head(2, d)
        cols = slice(h * DH, (h + 1) * DH)
        keys = kvh[z_, 0, :, :, cols].reshape(-1, DH)
        values = kvh[z_, 1, :, :, cols].reshape(-1, DH)
        weights = silu_of_half(dot_t(qh[:, :, cols].reshape(-1, DH), keys) * half_factor)
        more = dot(weights, values)
        oh[h] = more if t == 0 else oh[h] + more

    near_at = {1: (0, wraps), 3: (1, beside), 4: (1, wraps)}
    for t in range(1, NZL):
        z_ = z_of(t)
        for a in range(2):
            arrived(a, z_)

            @pl.when(goes_on(z_))
            def _():
                hop_z(a, z_).start()

            if a == 0:
                hist_head(t - 1, 0)
                if t < 5:
                    own_head(2 * t - 2)
        if t in near_at:
            near_copies(*near_at[t])
        if t == 2:
            for z_ in range(NZL):
                @pl.when((core != zh) | (z != z_))
                def _():
                    there = wb.at[core, x, y, z_]
                    remote(there, there, wz_send.at[0], wz_recv.at[z_], other_core).wait_recv()
            for d in range(1, NY):
                tile_y(d).start()
        if t == 3:
            for d in range(1, NY):
                there = wb.at[core, x, lax.rem(y + NY - d, NY)]
                remote(there, there, wy_send.at[0], wy_recv.at[d - 1], other_core).wait_recv()
            for d in range(1, NX):
                tile_x(d).start()
            tile_out(0).start()
        hist_head(t - 1, 1)
        if t < 5:
            own_head(2 * t - 1)
    for h in range(HEADS):
        hist_head(NZL - 1, h)
    for y_ in range(NY):
        for h in range(HEADS):
            part_out[y_, :, h * DH:(h + 1) * DH] = oh[h, y_ * rows:(y_ + 1) * rows].astype(BF16)
    for d in range(1, NY):
        from_head(d).start()
    part_in[y] = part_out[y]
    for d in range(1, NX):
        there = wb.at[core, lax.rem(x + NX - d, NX)]
        remote(there, there, wx_send.at[0], wx_recv.at[d - 1], other_core).wait_recv()
        tile_out(NX - d).start()
    near = jnp.where(z == 0, 1, 0)
    halo_chunk(near)
    halo_chunk(1 - near)

    for copy in incoming[9:]:
        copy.wait()
    for d in range(1, NY):
        back_home(d)
    for y_ in range(NY):
        cols = slice(y_ * SHARE, (y_ + 1) * SHARE)
        att[:, cols] = att[:, cols] + part_in[y_].astype(F32)
    attended = att[...]
    center = jnp.mean(attended, axis=1, keepdims=True)
    moved = attended - center
    spread = jnp.mean(moved * moved, axis=1, keepdims=True)
    gated = (moved * lax.rsqrt(spread + 1e-05) * gate_ref[...].astype(F32)).astype(BF16)

    for d in range(NX):
        there = wb.at[1 - core, lax.rem(x + d, NX)]
        remote(there, there, wo_send.at[0], wo_recv.at[d], other_core).wait_recv()
    for x_ in range(NX):
        cols = slice(x_ * 2 * DH, (x_ + 1) * 2 * DH)
        weight = jnp.concatenate(
            [wb[0, x_].reshape(-1, DH), wb[1, x_].reshape(-1, DH)], axis=1
        )
        out_ref[:, cols] = (res_ref[:, cols].astype(F32) + dot(gated, weight)).astype(BF16)

    @pl.when(z < NZL - 1)
    def _():
        for a in range(2):
            own_z(a, 0).wait_send()

    @pl.when(z > 0)
    def _():
        for a in range(2):
            own_z(a, 1).wait_send()

    for t in range(1, NZL):
        z_ = z_of(t)

        @pl.when(goes_on(z_))
        def _():
            for a in range(2):
                hop_z(a, z_).wait_send()

    for d in range(1, NY):
        for i in range(3):
            to_head(i, d).wait_send()
        from_head(d).wait_send()
    for way in range(2):
        for a in range(2):
            halo_copy(way, a).wait_send()

    @pl.when(core == zh)
    def _():
        for d in range(1, NZH * NZL):
            tile_z(d).wait_send()

    for d in range(1, NY):
        tile_y(d).wait_send()
    for d in range(1, NX):
        tile_x(d).wait_send()
    for d in range(NX):
        tile_out(d).wait_send()


def shards(q, k, v, gate, resid, hk, hv, ids, pattern, weight):
    rows, width = q.shape[1:]
    hist = hk.shape[1]
    hbm = pl.BlockSpec(memory_space=pl.ANY)
    vmem = pl.BlockSpec(memory_space=pltpu.VMEM)
    dma = pltpu.SemaphoreType.DMA
    out = pl.pallas_call(
        kernel,
        out_shape=jax.ShapeDtypeStruct((rows, width), BF16),
        in_specs=[hbm] * 10,
        out_specs=vmem,
        scratch_shapes=[
            pltpu.VMEM((5, rows, width), BF16),
            pltpu.VMEM(ids.shape, ids.dtype),
            pltpu.VMEM(pattern.shape, pattern.dtype),
            pltpu.VMEM(weight.shape, BF16),
            pltpu.VMEM((NZL, 2, NY, hist, SHARE), BF16),
            pltpu.VMEM((NY, rows, SHARE), BF16),
            pltpu.VMEM((HEADS, NY * rows, DH), F32),
            pltpu.VMEM((NY, rows, SHARE), BF16),
            pltpu.VMEM((NY, rows, SHARE), BF16),
            pltpu.VMEM((2, 2, rows, width), BF16),
            pltpu.VMEM(weight.shape, BF16),
            pltpu.VMEM((NZH, NX, NY, NZL, weight.shape[0], 2 * weight.shape[1]), BF16),
            pltpu.VMEM((3, rows, rows), F32),
            pltpu.VMEM((rows, width), F32),
            dma((11,)), dma((2, NZL)), dma((2, 2)), dma((2, NZL)), dma((3, NY - 1)), dma((3, NY - 1)),
            dma((NY - 1,)), dma((NY - 1,)), dma((2, 2)), dma((2, 2)),
            dma, dma, dma((NZH * NZL - 1,)), dma((NZL,)), dma((NY - 1,)), dma((NY - 1,)),
            dma((NX - 1,)), dma((NX - 1,)), dma((NX,)), dma((NX,)),
        ],
        compiler_params=pltpu.CompilerParams(
            collective_id=0, has_side_effects=True, vmem_limit_bytes=60 * 1024 * 1024
        ),
    )(q[0], k[0], v[0], gate[0], resid[0], hk[0], hv[0], ids, pattern, weight)
    return out[None]


def solution(mesh):
    part = P("users", "cand", None)
    return jax.shard_map(
        shards,
        mesh=mesh,
        in_specs=(part,) * 7 + (P("users", None), P(), P("cand", "users")),
        out_specs=part,
        check_vma=False,
    )
```

```python
import jax
import jax.numpy as jnp
from jax import lax
from jax.experimental import pallas as pl
from jax.experimental.pallas import tpu as pltpu
from jax.sharding import PartitionSpec as P

H = 8
DH = 128
NX, NZH, NCORE = 4, 2, 2
NY, NZL = 4, 8
NCAND = NY * NZL
HEADS = H // NY
SHARE = HEADS * DH
MESH = pl.DeviceIdType.MESH
BF16, F32 = jnp.bfloat16, jnp.float32


def dot(a, b):
    return lax.dot_general(a, b, (((1,), (0,)), ((), ())), preferred_element_type=F32)


def dot_t(a, b):
    return lax.dot_general(a, b, (((1,), (1,)), ((), ())), preferred_element_type=F32)


def silu_of_half(h):
    return (h + h * jnp.tanh(h)).astype(BF16)


def kernel(
    q_hbm, k_hbm, v_hbm, gate_hbm, res_hbm, hk_hbm, hv_hbm, ids_hbm, pat_hbm, w_hbm,
    out_ref,
    rows5, ids_ref, pat_ref, w_ref,
    kvh, qh, oh, part_out, part_in, halo, wtmp, wb, maskh, att,
    in_sem, kv_recv, own_send, z_send, ys_send, ys_recv, o_send, o_recv, halo_send, halo_recv,
    wc_send, wc_recv, wz_send, wz_recv, wy_send, wy_recv, wx_send, wx_recv, wo_send, wo_recv,
):
    u, c = lax.axis_index("users"), lax.axis_index("cand")
    core = lax.rem(u, NCORE)
    zh = lax.rem(u // NCORE, NZH)
    x = u // (NCORE * NZH)
    z = lax.rem(c, NZL)
    y = c // NZL
    rows = q_hbm.shape[0]
    q_ref, k_ref, v_ref, gate_ref, res_ref = [rows5.at[i] for i in range(5)]

    def share(y_):
        return pl.ds(pl.multiple_of(y_ * SHARE, SHARE), SHARE)

    incoming = [
        pltpu.make_async_copy(src, dst, in_sem.at[i])
        for i, (src, dst) in enumerate([
            (w_hbm, w_ref), (ids_hbm, ids_ref), (pat_hbm, pat_ref),
            (hk_hbm.at[:, share(y)], kvh.at[z, 0, y]), (hv_hbm.at[:, share(y)], kvh.at[z, 1, y]),
            (q_hbm.at[:, share(y)], qh.at[y]),
            (q_hbm, q_ref), (k_hbm, k_ref), (v_hbm, v_ref), (gate_hbm, gate_ref), (res_hbm, res_ref),
        ])
    ]
    for copy in incoming:
        copy.start()

    def dev(x_, zh_, core_, y_, z_):
        return {"users": (x_ * NZH + zh_) * NCORE + core_, "cand": y_ * NZL + z_}

    def on_cand(c_):
        return {"users": u, "cand": c_}

    def along_z(d):
        far = lax.rem(zh * NZL + z + d, NZH * NZL)
        return far // NZL, lax.rem(far, NZL)

    other_core = dev(x, zh, 1 - core, y, z)
    nxt, prv = lax.rem(c + 1, NCAND), lax.rem(c + NCAND - 1, NCAND)

    barrier = pltpu.get_barrier_semaphore()

    def greet(device):
        pl.semaphore_signal(barrier, inc=1, device_id=device, device_id_type=MESH)

    for d in range(1, NZH * NZL):
        zh_, z_ = along_z(d)
        greet(dev(x, zh_, core, y, z_))
    for d in range(1, NY):
        greet(dev(x, zh, core, lax.rem(y + d, NY), z))
    for d in range(1, NX):
        greet(dev(lax.rem(x + d, NX), zh, core, y, z))
    greet(other_core)

    @pl.when(z == NZL - 1)
    def _():
        greet(on_cand(nxt))

    @pl.when(z == 0)
    def _():
        greet(on_cand(prv))

    partners = NZH * NZL - 1 + NY - 1 + NX - 1 + 1
    edge = jnp.where(z == 0, 1, 0) + jnp.where(z == NZL - 1, 1, 0)
    pl.semaphore_wait(barrier, partners + edge)

    def remote(src, dst, send, recv, device):
        return pltpu.make_async_remote_copy(
            src_ref=src, dst_ref=dst, send_sem=send, recv_sem=recv,
            device_id=device, device_id_type=MESH,
        )

    def z_of(t):
        both = 2 * jnp.minimum(z, NZL - 1 - z)
        side = jnp.where(2 * z < NZL, -1, 1)
        turn = z + side * ((t + 1) // 2 if t % 2 else -(t // 2))
        return jnp.where(t <= both, turn, jnp.where(2 * z < NZL, t, NZL - 1 - t))

    def to_head(i, d):
        y_ = lax.rem(y + d, NY)
        src = (hk_hbm, hv_hbm, q_hbm)[i].at[:, share(y_)]
        dst = qh.at[y] if i == 2 else kvh.at[z, i, y]
        return remote(src, dst, ys_send.at[i, d - 1], ys_recv.at[i, d - 1], on_cand(y_ * NZL + z))

    def at_head(i, d):
        y_ = lax.rem(y + NY - d, NY)
        here = qh.at[y_] if i == 2 else kvh.at[z, i, y_]
        remote(here, here, ys_send.at[0, 0], ys_recv.at[i, d - 1], other_core).wait_recv()

    def from_head(d):
        y_ = lax.rem(y + d, NY)
        return remote(part_out.at[y_], part_in.at[y], o_send.at[d - 1], o_recv.at[d - 1], on_cand(y_ * NZL + z))

    def back_home(d):
        here = part_in.at[lax.rem(y + NY - d, NY)]
        remote(here, here, o_send.at[0], o_recv.at[d - 1], other_core).wait_recv()

    def own_z(a, way):
        to = on_cand(y * NZL + (z + 1 if way == 0 else z - 1))
        return remote(kvh.at[z, a], kvh.at[z, a], own_send.at[way, a], kv_recv.at[a, z], to)

    def hop_z(a, z_):
        to = on_cand(y * NZL + z + jnp.where(z_ < z, 1, -1))
        return remote(kvh.at[z_, a], kvh.at[z_, a], z_send.at[a, z_], kv_recv.at[a, z_], to)

    def goes_on(z_):
        return ((z_ < z) & (z < NZL - 1)) | ((z_ > z) & (z > 0))

    def arrived(a, z_):
        here = kvh.at[z_, a]
        remote(here, here, own_send.at[0, 0], kv_recv.at[a, z_], other_core).wait_recv()

    def halo_copy(way, a):
        return remote(
            (k_hbm, v_hbm)[a], halo.at[way, a], halo_send.at[way, a], halo_recv.at[way, a],
            on_cand(nxt if way == 0 else prv),
        )

    wraps = (z == NZL - 1, z == 0)
    beside = (~wraps[0], ~wraps[1])

    def near_copies(a, when):
        for way in range(2):
            @pl.when(when[way])
            def _():
                halo_copy(way, a).start()

    tile_core = remote(w_hbm, wtmp, wc_send, wc_recv, other_core)

    def tile_z(d):
        zh_, z_ = along_z(d)
        here = wb.at[core, x, y, z]
        return remote(here, here, wz_send.at[d - 1], wz_recv.at[z], dev(x, zh_, core, y, z_))

    def tile_y(d):
        here = wb.at[core, x, y]
        return remote(here, here, wy_send.at[d - 1], wy_recv.at[d - 1], dev(x, zh, core, lax.rem(y + d, NY), z))

    def tile_x(d):
        here = wb.at[core, x]
        return remote(here, here, wx_send.at[d - 1], wx_recv.at[d - 1], dev(lax.rem(x + d, NX), zh, core, y, z))

    def tile_out(d):
        here = wb.at[core, lax.rem(x + d, NX)]
        return remote(here, here, wo_send.at[d], wo_recv.at[d], other_core)

    for i in range(3):
        for d in range(1, NY):
            to_head(i, d).start()
    near_copies(0, beside)
    tile_core.start()

    for copy in incoming[:3]:
        copy.wait()

    def ids_row(b):
        at = jnp.clip(b, 0, NCAND - 1) * DH
        got = ids_ref[:, pl.ds(pl.multiple_of(at, DH), DH)].astype(F32)
        return jnp.where((b >= 0) & (b < NCAND), got, -1.0)

    square = (rows, rows)
    sub = lax.broadcasted_iota(jnp.int32, square, 0)
    lane = lax.broadcasted_iota(jnp.int32, square, 1)
    half_factor = 0.5 * DH ** (-0.5)

    def make_mask():
        ids = [ids_row(c + d) for d in (-2, -1, 0, 1)]
        wide = [jnp.broadcast_to(r, square) for r in ids]
        tall = [w.T for w in wide]
        offs = []
        for b in (1, 2, 3):
            whole = jnp.where(tall[b - 1] == wide[b], 1.0, 0.0)
            part = jnp.where((tall[b] == wide[b]) & (sub < lane), 1.0, 0.0)
            offs.append(jnp.sum(whole + part, axis=0, keepdims=True))
        own_off = jnp.broadcast_to(offs[1], square).T
        hot_rows = jnp.where(own_off == lane.astype(F32), 1.0, 0.0).astype(BF16)
        allowed = jnp.where(pat_ref[...] == 1, 1.0, 0.0).astype(BF16)
        by_row = dot(hot_rows, allowed).astype(BF16)
        for b in range(3):
            hot_keys = jnp.where(sub.astype(F32) == jnp.broadcast_to(offs[b], square), 1.0, 0.0).astype(BF16)
            seen = dot(by_row, hot_keys) > 0.5
            if b == 1:
                seen = seen | (sub == lane)
            seen = seen & (tall[2] == wide[b + 1])
            maskh[b] = jnp.where(seen, half_factor, 0.0)

    for copy in incoming[3:5]:
        copy.wait()
    for a in range(2):
        for d in range(1, NY):
            at_head(a, d)

        @pl.when(z < NZL - 1)
        def _():
            own_z(a, 0).start()

        @pl.when(z > 0)
        def _():
            own_z(a, 1).start()

    tile_core.wait()
    mine, theirs = w_ref[...].astype(F32), wtmp[...].astype(F32)
    tile = jnp.where(
        core == 0, jnp.concatenate([mine, theirs], axis=1), jnp.concatenate([theirs, mine], axis=1)
    ).astype(BF16)

    @pl.when(core == zh)
    def _():
        wb[core, x, y, z] = tile
        for d in range(1, NZH * NZL):
            tile_z(d).start()

    make_mask()

    def own_head(h):
        if h == 0:
            for copy in incoming[6:9]:
                copy.wait()
        cols = slice(h * DH, (h + 1) * DH)
        weights = silu_of_half(dot_t(q_ref[:, cols], k_ref[:, cols]) * maskh[1])
        att[:, cols] = dot(weights, v_ref[:, cols])

    def halo_chunk(side):
        for a in range(2):
            here = halo.at[side, a]
            remote(here, here, halo_send.at[0, 0], halo_recv.at[side, a], other_core).wait_recv()
        for h in range(H):
            cols = slice(h * DH, (h + 1) * DH)
            weights = silu_of_half(dot_t(q_ref[:, cols], halo[side, 0, :, cols]) * maskh[2 * side])
            att[:, cols] = att[:, cols] + dot(weights, halo[side, 1, :, cols])

    def hist_head(t, h):
        z_ = z_of(t)
        if t == 0 and h == 0:
            incoming[5].wait()
            for d in range(1, NY):
                at_head(2, d)
        cols = slice(h * DH, (h + 1) * DH)
        keys = kvh[z_, 0, :, :, cols].reshape(-1, DH)
        values = kvh[z_, 1, :, :, cols].reshape(-1, DH)
        weights = silu_of_half(dot_t(qh[:, :, cols].reshape(-1, DH), keys) * half_factor)
        more = dot(weights, values)
        oh[h] = more if t == 0 else oh[h] + more

    near_at = {1: (0, wraps), 3: (1, wraps), 4: (1, beside)}
    for t in range(1, NZL):
        z_ = z_of(t)
        for a in range(2):
            arrived(a, z_)

            @pl.when(goes_on(z_))
            def _():
                hop_z(a, z_).start()

            if a == 0:
                hist_head(t - 1, 0)
                if t < 5:
                    own_head(2 * t - 2)
        if t in near_at:
            near_copies(*near_at[t])
        if t == 2:
            for z_ in range(NZL):
                @pl.when((core != zh) | (z != z_))
                def _():
                    there = wb.at[core, x, y, z_]
                    remote(there, there, wz_send.at[0], wz_recv.at[z_], other_core).wait_recv()
            for d in range(1, NY):
                tile_y(d).start()
        if t == 3:
            for d in range(1, NY):
                there = wb.at[core, x, lax.rem(y + NY - d, NY)]
                remote(there, there, wy_send.at[0], wy_recv.at[d - 1], other_core).wait_recv()
            for d in range(1, NX):
                tile_x(d).start()
            tile_out(0).start()
        hist_head(t - 1, 1)
        if t < 5:
            own_head(2 * t - 1)
    for h in range(HEADS):
        hist_head(NZL - 1, h)
    for y_ in range(NY):
        for h in range(HEADS):
            part_out[y_, :, h * DH:(h + 1) * DH] = oh[h, y_ * rows:(y_ + 1) * rows].astype(BF16)
    for d in range(1, NY):
        from_head(d).start()
    part_in[y] = part_out[y]
    for d in range(1, NX):
        there = wb.at[core, lax.rem(x + NX - d, NX)]
        remote(there, there, wx_send.at[0], wx_recv.at[d - 1], other_core).wait_recv()
        tile_out(NX - d).start()
    near = jnp.where(z == 0, 1, 0)
    halo_chunk(near)
    halo_chunk(1 - near)

    for copy in incoming[9:]:
        copy.wait()
    for d in range(1, NY):
        back_home(d)
    for y_ in range(NY):
        cols = slice(y_ * SHARE, (y_ + 1) * SHARE)
        att[:, cols] = att[:, cols] + part_in[y_].astype(F32)
    attended = att[...]
    center = jnp.mean(attended, axis=1, keepdims=True)
    moved = attended - center
    spread = jnp.mean(moved * moved, axis=1, keepdims=True)
    gated = (moved * lax.rsqrt(spread + 1e-05) * gate_ref[...].astype(F32)).astype(BF16)

    for d in range(NX):
        there = wb.at[1 - core, lax.rem(x + d, NX)]
        remote(there, there, wo_send.at[0], wo_recv.at[d], other_core).wait_recv()
    for x_ in range(NX):
        cols = slice(x_ * 2 * DH, (x_ + 1) * 2 * DH)
        weight = jnp.concatenate(
            [wb[0, x_].reshape(-1, DH), wb[1, x_].reshape(-1, DH)], axis=1
        )
        out_ref[:, cols] = (res_ref[:, cols].astype(F32) + dot(gated, weight)).astype(BF16)

    @pl.when(z < NZL - 1)
    def _():
        for a in range(2):
            own_z(a, 0).wait_send()

    @pl.when(z > 0)
    def _():
        for a in range(2):
            own_z(a, 1).wait_send()

    for t in range(1, NZL):
        z_ = z_of(t)

        @pl.when(goes_on(z_))
        def _():
            for a in range(2):
                hop_z(a, z_).wait_send()

    for d in range(1, NY):
        for i in range(3):
            to_head(i, d).wait_send()
        from_head(d).wait_send()
    for way in range(2):
        for a in range(2):
            halo_copy(way, a).wait_send()

    @pl.when(core == zh)
    def _():
        for d in range(1, NZH * NZL):
            tile_z(d).wait_send()

    for d in range(1, NY):
        tile_y(d).wait_send()
    for d in range(1, NX):
        tile_x(d).wait_send()
    for d in range(NX):
        tile_out(d).wait_send()


def shards(q, k, v, gate, resid, hk, hv, ids, pattern, weight):
    rows, width = q.shape[1:]
    hist = hk.shape[1]
    hbm = pl.BlockSpec(memory_space=pl.ANY)
    vmem = pl.BlockSpec(memory_space=pltpu.VMEM)
    dma = pltpu.SemaphoreType.DMA
    out = pl.pallas_call(
        kernel,
        out_shape=jax.ShapeDtypeStruct((rows, width), BF16),
        in_specs=[hbm] * 10,
        out_specs=vmem,
        scratch_shapes=[
            pltpu.VMEM((5, rows, width), BF16),
            pltpu.VMEM(ids.shape, ids.dtype),
            pltpu.VMEM(pattern.shape, pattern.dtype),
            pltpu.VMEM(weight.shape, BF16),
            pltpu.VMEM((NZL, 2, NY, hist, SHARE), BF16),
            pltpu.VMEM((NY, rows, SHARE), BF16),
            pltpu.VMEM((HEADS, NY * rows, DH), F32),
            pltpu.VMEM((NY, rows, SHARE), BF16),
            pltpu.VMEM((NY, rows, SHARE), BF16),
            pltpu.VMEM((2, 2, rows, width), BF16),
            pltpu.VMEM(weight.shape, BF16),
            pltpu.VMEM((NZH, NX, NY, NZL, weight.shape[0], 2 * weight.shape[1]), BF16),
            pltpu.VMEM((3, rows, rows), F32),
            pltpu.VMEM((rows, width), F32),
            dma((11,)), dma((2, NZL)), dma((2, 2)), dma((2, NZL)), dma((3, NY - 1)), dma((3, NY - 1)),
            dma((NY - 1,)), dma((NY - 1,)), dma((2, 2)), dma((2, 2)),
            dma, dma, dma((NZH * NZL - 1,)), dma((NZL,)), dma((NY - 1,)), dma((NY - 1,)),
            dma((NX - 1,)), dma((NX - 1,)), dma((NX,)), dma((NX,)),
        ],
        compiler_params=pltpu.CompilerParams(
            collective_id=0, has_side_effects=True, vmem_limit_bytes=60 * 1024 * 1024
        ),
    )(q[0], k[0], v[0], gate[0], resid[0], hk[0], hv[0], ids, pattern, weight)
    return out[None]


def solution(mesh):
    part = P("users", "cand", None)
    return jax.shard_map(
        shards,
        mesh=mesh,
        in_specs=(part,) * 7 + (P("users", None), P(), P("cand", "users")),
        out_specs=part,
        check_vma=False,
    )
```

```python
import jax
import jax.numpy as jnp
from jax import lax
from jax.experimental import pallas as pl
from jax.experimental.pallas import tpu as pltpu
from jax.sharding import PartitionSpec as P

H = 8
DH = 128
NX, NZH, NCORE = 4, 2, 2
NY, NZL = 4, 8
NCAND = NY * NZL
HEADS = H // NY
SHARE = HEADS * DH
MESH = pl.DeviceIdType.MESH
BF16, F32 = jnp.bfloat16, jnp.float32


def dot(a, b):
    return lax.dot_general(a, b, (((1,), (0,)), ((), ())), preferred_element_type=F32)


def dot_t(a, b):
    return lax.dot_general(a, b, (((1,), (1,)), ((), ())), preferred_element_type=F32)


def silu_of_half(h):
    return (h + h * jnp.tanh(h)).astype(BF16)


def kernel(
    q_hbm, k_hbm, v_hbm, gate_hbm, res_hbm, hk_hbm, hv_hbm, ids_hbm, pat_hbm, w_hbm,
    out_hbm,
    out_buf, rows5, ids_ref, pat_ref, w_ref,
    kvh, qh, oh, part_out, part_in, halo, wtmp, wb, maskh, att,
    in_sem, kv_recv, own_send, z_send, ys_send, ys_recv, o_send, o_recv, halo_send, halo_recv,
    wc_send, wc_recv, wz_send, wz_recv, wy_send, wy_recv, wx_send, wx_recv, wo_send, wo_recv, out_sem,
):
    u, c = lax.axis_index("users"), lax.axis_index("cand")
    core = lax.rem(u, NCORE)
    zh = lax.rem(u // NCORE, NZH)
    x = u // (NCORE * NZH)
    z = lax.rem(c, NZL)
    y = c // NZL
    rows = q_hbm.shape[0]
    q_ref, k_ref, v_ref, gate_ref, res_ref = [rows5.at[i] for i in range(5)]

    def leaving(x_):
        cols = slice(x_ * 2 * DH, (x_ + 1) * 2 * DH)
        return pltpu.make_async_copy(out_buf.at[:, cols], out_hbm.at[:, cols], out_sem.at[x_])

    def share(y_):
        return pl.ds(pl.multiple_of(y_ * SHARE, SHARE), SHARE)

    incoming = [
        pltpu.make_async_copy(src, dst, in_sem.at[i])
        for i, (src, dst) in enumerate([
            (w_hbm, w_ref), (ids_hbm, ids_ref), (pat_hbm, pat_ref),
            (hk_hbm.at[:, share(y)], kvh.at[z, 0, y]), (hv_hbm.at[:, share(y)], kvh.at[z, 1, y]),
            (q_hbm.at[:, share(y)], qh.at[y]),
            (q_hbm, q_ref), (k_hbm, k_ref), (v_hbm, v_ref), (gate_hbm, gate_ref), (res_hbm, res_ref),
        ])
    ]
    for copy in incoming:
        copy.start()

    def dev(x_, zh_, core_, y_, z_):
        return {"users": (x_ * NZH + zh_) * NCORE + core_, "cand": y_ * NZL + z_}

    def on_cand(c_):
        return {"users": u, "cand": c_}

    def along_z(d):
        far = lax.rem(zh * NZL + z + d, NZH * NZL)
        return far // NZL, lax.rem(far, NZL)

    other_core = dev(x, zh, 1 - core, y, z)
    nxt, prv = lax.rem(c + 1, NCAND), lax.rem(c + NCAND - 1, NCAND)

    barrier = pltpu.get_barrier_semaphore()

    def greet(device):
        pl.semaphore_signal(barrier, inc=1, device_id=device, device_id_type=MESH)

    for d in range(1, NZH * NZL):
        zh_, z_ = along_z(d)
        greet(dev(x, zh_, core, y, z_))
    for d in range(1, NY):
        greet(dev(x, zh, core, lax.rem(y + d, NY), z))
    for d in range(1, NX):
        greet(dev(lax.rem(x + d, NX), zh, core, y, z))
    greet(other_core)

    @pl.when(z == NZL - 1)
    def _():
        greet(on_cand(nxt))

    @pl.when(z == 0)
    def _():
        greet(on_cand(prv))

    partners = NZH * NZL - 1 + NY - 1 + NX - 1 + 1
    edge = jnp.where(z == 0, 1, 0) + jnp.where(z == NZL - 1, 1, 0)
    pl.semaphore_wait(barrier, partners + edge)

    def remote(src, dst, send, recv, device):
        return pltpu.make_async_remote_copy(
            src_ref=src, dst_ref=dst, send_sem=send, recv_sem=recv,
            device_id=device, device_id_type=MESH,
        )

    def z_of(t):
        both = 2 * jnp.minimum(z, NZL - 1 - z)
        side = jnp.where(2 * z < NZL, -1, 1)
        turn = z + side * ((t + 1) // 2 if t % 2 else -(t // 2))
        return jnp.where(t <= both, turn, jnp.where(2 * z < NZL, t, NZL - 1 - t))

    def to_head(i, d):
        y_ = lax.rem(y + d, NY)
        src = (hk_hbm, hv_hbm, q_hbm)[i].at[:, share(y_)]
        dst = qh.at[y] if i == 2 else kvh.at[z, i, y]
        return remote(src, dst, ys_send.at[i, d - 1], ys_recv.at[i, d - 1], on_cand(y_ * NZL + z))

    def at_head(i, d):
        y_ = lax.rem(y + NY - d, NY)
        here = qh.at[y_] if i == 2 else kvh.at[z, i, y_]
        remote(here, here, ys_send.at[0, 0], ys_recv.at[i, d - 1], other_core).wait_recv()

    def from_head(d):
        y_ = lax.rem(y + d, NY)
        return remote(part_out.at[y_], part_in.at[y], o_send.at[d - 1], o_recv.at[d - 1], on_cand(y_ * NZL + z))

    def back_home(d):
        here = part_in.at[lax.rem(y + NY - d, NY)]
        remote(here, here, o_send.at[0], o_recv.at[d - 1], other_core).wait_recv()

    def own_z(a, way):
        to = on_cand(y * NZL + (z + 1 if way == 0 else z - 1))
        return remote(kvh.at[z, a], kvh.at[z, a], own_send.at[way, a], kv_recv.at[a, z], to)

    def hop_z(a, z_):
        to = on_cand(y * NZL + z + jnp.where(z_ < z, 1, -1))
        return remote(kvh.at[z_, a], kvh.at[z_, a], z_send.at[a, z_], kv_recv.at[a, z_], to)

    def goes_on(z_):
        return ((z_ < z) & (z < NZL - 1)) | ((z_ > z) & (z > 0))

    def arrived(a, z_):
        here = kvh.at[z_, a]
        remote(here, here, own_send.at[0, 0], kv_recv.at[a, z_], other_core).wait_recv()

    def halo_copy(way, a):
        return remote(
            (k_hbm, v_hbm)[a], halo.at[way, a], halo_send.at[way, a], halo_recv.at[way, a],
            on_cand(nxt if way == 0 else prv),
        )

    wraps = (z == NZL - 1, z == 0)
    beside = (~wraps[0], ~wraps[1])

    def near_copies(a, when):
        for way in range(2):
            @pl.when(when[way])
            def _():
                halo_copy(way, a).start()

    tile_core = remote(w_hbm, wtmp, wc_send, wc_recv, other_core)

    def tile_z(d):
        zh_, z_ = along_z(d)
        here = wb.at[core, x, y, z]
        return remote(here, here, wz_send.at[d - 1], wz_recv.at[z], dev(x, zh_, core, y, z_))

    def tile_y(d):
        here = wb.at[core, x, y]
        return remote(here, here, wy_send.at[d - 1], wy_recv.at[d - 1], dev(x, zh, core, lax.rem(y + d, NY), z))

    def tile_x(d):
        here = wb.at[core, x]
        return remote(here, here, wx_send.at[d - 1], wx_recv.at[d - 1], dev(lax.rem(x + d, NX), zh, core, y, z))

    def tile_out(d):
        here = wb.at[core, lax.rem(x + d, NX)]
        return remote(here, here, wo_send.at[d], wo_recv.at[d], other_core)

    for i in range(3):
        for d in range(1, NY):
            to_head(i, d).start()
    near_copies(0, beside)
    tile_core.start()

    for copy in incoming[:3]:
        copy.wait()

    def ids_row(b):
        at = jnp.clip(b, 0, NCAND - 1) * DH
        got = ids_ref[:, pl.ds(pl.multiple_of(at, DH), DH)].astype(F32)
        return jnp.where((b >= 0) & (b < NCAND), got, -1.0)

    square = (rows, rows)
    sub = lax.broadcasted_iota(jnp.int32, square, 0)
    lane = lax.broadcasted_iota(jnp.int32, square, 1)
    half_factor = 0.5 * DH ** (-0.5)

    def make_mask():
        ids = [ids_row(c + d) for d in (-2, -1, 0, 1)]
        wide = [jnp.broadcast_to(r, square) for r in ids]
        tall = [w.T for w in wide]
        offs = []
        for b in (1, 2, 3):
            whole = jnp.where(tall[b - 1] == wide[b], 1.0, 0.0)
            part = jnp.where((tall[b] == wide[b]) & (sub < lane), 1.0, 0.0)
            offs.append(jnp.sum(whole + part, axis=0, keepdims=True))
        own_off = jnp.broadcast_to(offs[1], square).T
        hot_rows = jnp.where(own_off == lane.astype(F32), 1.0, 0.0).astype(BF16)
        allowed = jnp.where(pat_ref[...] == 1, 1.0, 0.0).astype(BF16)
        by_row = dot(hot_rows, allowed).astype(BF16)
        for b in range(3):
            hot_keys = jnp.where(sub.astype(F32) == jnp.broadcast_to(offs[b], square), 1.0, 0.0).astype(BF16)
            seen = dot(by_row, hot_keys) > 0.5
            if b == 1:
                seen = seen | (sub == lane)
            seen = seen & (tall[2] == wide[b + 1])
            maskh[b] = jnp.where(seen, half_factor, 0.0)

    for copy in incoming[3:5]:
        copy.wait()
    for a in range(2):
        for d in range(1, NY):
            at_head(a, d)

        @pl.when(z < NZL - 1)
        def _():
            own_z(a, 0).start()

        @pl.when(z > 0)
        def _():
            own_z(a, 1).start()

    tile_core.wait()
    mine, theirs = w_ref[...].astype(F32), wtmp[...].astype(F32)
    tile = jnp.where(
        core == 0, jnp.concatenate([mine, theirs], axis=1), jnp.concatenate([theirs, mine], axis=1)
    ).astype(BF16)

    @pl.when(core == zh)
    def _():
        wb[core, x, y, z] = tile
        for d in range(1, NZH * NZL):
            tile_z(d).start()

    make_mask()

    def own_head(h):
        if h == 0:
            for copy in incoming[6:9]:
                copy.wait()
        cols = slice(h * DH, (h + 1) * DH)
        weights = silu_of_half(dot_t(q_ref[:, cols], k_ref[:, cols]) * maskh[1])
        att[:, cols] = dot(weights, v_ref[:, cols])

    def halo_chunk(side):
        for a in range(2):
            here = halo.at[side, a]
            remote(here, here, halo_send.at[0, 0], halo_recv.at[side, a], other_core).wait_recv()
        for h in range(H):
            cols = slice(h * DH, (h + 1) * DH)
            weights = silu_of_half(dot_t(q_ref[:, cols], halo[side, 0, :, cols]) * maskh[2 * side])
            att[:, cols] = att[:, cols] + dot(weights, halo[side, 1, :, cols])

    def hist_head(t, h):
        z_ = z_of(t)
        if t == 0 and h == 0:
            incoming[5].wait()
            for d in range(1, NY):
                at_head(2, d)
        cols = slice(h * DH, (h + 1) * DH)
        keys = kvh[z_, 0, :, :, cols].reshape(-1, DH)
        values = kvh[z_, 1, :, :, cols].reshape(-1, DH)
        weights = silu_of_half(dot_t(qh[:, :, cols].reshape(-1, DH), keys) * half_factor)
        more = dot(weights, values)
        oh[h] = more if t == 0 else oh[h] + more

    near_at = {1: (0, wraps), 3: (1, beside), 4: (1, wraps)}
    for t in range(1, NZL):
        z_ = z_of(t)
        for a in range(2):
            arrived(a, z_)

            @pl.when(goes_on(z_))
            def _():
                hop_z(a, z_).start()

            if a == 0:
                hist_head(t - 1, 0)
                if t < 5:
                    own_head(2 * t - 2)
        if t in near_at:
            near_copies(*near_at[t])
        if t == 2:
            for z_ in range(NZL):
                @pl.when((core != zh) | (z != z_))
                def _():
                    there = wb.at[core, x, y, z_]
                    remote(there, there, wz_send.at[0], wz_recv.at[z_], other_core).wait_recv()
            for d in range(1, NY):
                tile_y(d).start()
        if t == 3:
            for d in range(1, NY):
                there = wb.at[core, x, lax.rem(y + NY - d, NY)]
                remote(there, there, wy_send.at[0], wy_recv.at[d - 1], other_core).wait_recv()
            for d in range(1, NX):
                tile_x(d).start()
            tile_out(0).start()
        hist_head(t - 1, 1)
        if t < 5:
            own_head(2 * t - 1)
    for d in range(1, NX):
        there = wb.at[core, lax.rem(x + NX - d, NX)]
        remote(there, there, wx_send.at[0], wx_recv.at[d - 1], other_core).wait_recv()
        tile_out(NX - d).start()
    for h in range(HEADS):
        hist_head(NZL - 1, h)
    for y_ in range(NY):
        for h in range(HEADS):
            part_out[y_, :, h * DH:(h + 1) * DH] = oh[h, y_ * rows:(y_ + 1) * rows].astype(BF16)
    for d in range(1, NY):
        from_head(d).start()
    part_in[y] = part_out[y]
    near = jnp.where(z == 0, 1, 0)
    halo_chunk(near)
    halo_chunk(1 - near)

    for copy in incoming[9:]:
        copy.wait()
    for d in range(1, NY):
        back_home(d)
    for y_ in range(NY):
        cols = slice(y_ * SHARE, (y_ + 1) * SHARE)
        att[:, cols] = att[:, cols] + part_in[y_].astype(F32)
    attended = att[...]
    center = jnp.mean(attended, axis=1, keepdims=True)
    moved = attended - center
    spread = jnp.mean(moved * moved, axis=1, keepdims=True)
    gated = (moved * lax.rsqrt(spread + 1e-05) * gate_ref[...].astype(F32)).astype(BF16)

    for d in range(NX):
        there = wb.at[1 - core, lax.rem(x + d, NX)]
        remote(there, there, wo_send.at[0], wo_recv.at[d], other_core).wait_recv()
    for x_ in range(NX):
        cols = slice(x_ * 2 * DH, (x_ + 1) * 2 * DH)
        weight = jnp.concatenate(
            [wb[0, x_].reshape(-1, DH), wb[1, x_].reshape(-1, DH)], axis=1
        )
        out_buf[:, cols] = (res_ref[:, cols].astype(F32) + dot(gated, weight)).astype(BF16)
        leaving(x_).start()

    @pl.when(z < NZL - 1)
    def _():
        for a in range(2):
            own_z(a, 0).wait_send()

    @pl.when(z > 0)
    def _():
        for a in range(2):
            own_z(a, 1).wait_send()

    for t in range(1, NZL):
        z_ = z_of(t)

        @pl.when(goes_on(z_))
        def _():
            for a in range(2):
                hop_z(a, z_).wait_send()

    for d in range(1, NY):
        for i in range(3):
            to_head(i, d).wait_send()
        from_head(d).wait_send()
    for way in range(2):
        for a in range(2):
            halo_copy(way, a).wait_send()

    @pl.when(core == zh)
    def _():
        for d in range(1, NZH * NZL):
            tile_z(d).wait_send()

    for d in range(1, NY):
        tile_y(d).wait_send()
    for d in range(1, NX):
        tile_x(d).wait_send()
    for d in range(NX):
        tile_out(d).wait_send()
        leaving(d).wait()


def shards(q, k, v, gate, resid, hk, hv, ids, pattern, weight):
    rows, width = q.shape[1:]
    hist = hk.shape[1]
    hbm = pl.BlockSpec(memory_space=pl.ANY)
    dma = pltpu.SemaphoreType.DMA
    out = pl.pallas_call(
        kernel,
        out_shape=jax.ShapeDtypeStruct((rows, width), BF16),
        in_specs=[hbm] * 10,
        out_specs=hbm,
        scratch_shapes=[
            pltpu.VMEM((rows, width), BF16),
            pltpu.VMEM((5, rows, width), BF16),
            pltpu.VMEM(ids.shape, ids.dtype),
            pltpu.VMEM(pattern.shape, pattern.dtype),
            pltpu.VMEM(weight.shape, BF16),
            pltpu.VMEM((NZL, 2, NY, hist, SHARE), BF16),
            pltpu.VMEM((NY, rows, SHARE), BF16),
            pltpu.VMEM((HEADS, NY * rows, DH), F32),
            pltpu.VMEM((NY, rows, SHARE), BF16),
            pltpu.VMEM((NY, rows, SHARE), BF16),
            pltpu.VMEM((2, 2, rows, width), BF16),
            pltpu.VMEM(weight.shape, BF16),
            pltpu.VMEM((NZH, NX, NY, NZL, weight.shape[0], 2 * weight.shape[1]), BF16),
            pltpu.VMEM((3, rows, rows), F32),
            pltpu.VMEM((rows, width), F32),
            dma((11,)), dma((2, NZL)), dma((2, 2)), dma((2, NZL)), dma((3, NY - 1)), dma((3, NY - 1)),
            dma((NY - 1,)), dma((NY - 1,)), dma((2, 2)), dma((2, 2)),
            dma, dma, dma((NZH * NZL - 1,)), dma((NZL,)), dma((NY - 1,)), dma((NY - 1,)),
            dma((NX - 1,)), dma((NX - 1,)), dma((NX,)), dma((NX,)), dma((NX,)),
        ],
        compiler_params=pltpu.CompilerParams(
            collective_id=0, has_side_effects=True, vmem_limit_bytes=60 * 1024 * 1024
        ),
    )(q[0], k[0], v[0], gate[0], resid[0], hk[0], hv[0], ids, pattern, weight)
    return out[None]


def solution(mesh):
    part = P("users", "cand", None)
    return jax.shard_map(
        shards,
        mesh=mesh,
        in_specs=(part,) * 7 + (P("users", None), P(), P("cand", "users")),
        out_specs=part,
        check_vma=False,
    )
```
